128 devices in a mesh: elem: 128 (over x, y, z, core).
Axes of the slice: x: 4, y: 4, z: 4, core: 2. Of those that a mesh axis runs over, the one named last changes fastest.
Arguments:
- prognostic: float32 [524288, 128], P('elem'), may hold values from -6 to 6
- metric: float32 [2, 524288], P(None, 'elem'), may hold values from 0.5 to 1
- inv_mass: float32 [524288], P('elem'), may hold values from 1 to 12.6
- viscosity: float32 [128], replicated, may hold values from 8e-05 to 0.00024
- partner: int32 [3, 524288], P(None, 'elem'), may hold values from 0 to 4096, as said below
- send_rows: int32 [256, 768], P('elem'), may hold values from 0 to 4095, as said below
- recv_rows: int32 [512, 768], P('elem'), may hold values from 0 to 4096, as said below
Outputs:
- smoothed: float32 [524288, 128], P('elem')
The draws below stay inside these ranges and needn't reach their ends.
Inputs may be any that keep to these rules, and one draw needn't show every extreme that they name: `partner`: for each local row, the other rows of the same block that hold the same grid point (up to three), the rest 4096. `send_rows`: directions in order: 1 ahead, 1 behind along the curve, cyclically. In direction k, entry m is a local row holding the m-th grid point along the element edge shared through that direction, already holding that point's local sum. `recv_rows`: rows 2 k and 2 k + 1 of a block: the one or two local rows holding grid point m of the edge shared through direction k, else 4096.
All inputs are finite; a program needn't handle non-finite values.
Results may differ from the reference program's by a relative error of at most 0.0001.
Values sent between devices are 32-bit elements; how exact they have to be, the bound alone decides.
No kernel may reach another device: no remote copies, remote signals or barrier semaphores. Data moves between devices by JAX's collectives and lax.ppermute only.
A program may use at most 64 MiB of HBM per device.

```python
import math
import jax
import jax.numpy as jnp
import numpy as np
from jax import lax

H = 256
W = 1
SUBCYCLES = 2
LF = 128
ROWS = 524288
N_ELEM = 128


def strip_layout(key):
    devices = N_ELEM
    elem_count = H * W
    row_count = 16 * elem_count
    slot_count = 3 * H
    device_keys = jax.random.split(key, devices)
    cell_order = jax.vmap(lambda one_key: jax.random.permutation(one_key, elem_count))(device_keys).astype(jnp.int32)
    ranks = jnp.arange(elem_count, dtype=jnp.int32)
    slot_lookup = jax.vmap(lambda order_row: jnp.zeros((elem_count,), jnp.int32).at[order_row].set(ranks))(cell_order)

    def device_maps(order_row, lookup):

        def row_at(cell_x, cell_y, point_x, point_y):
            safe_x = jnp.clip(cell_x, 0, W - 1)
            return lookup[safe_x * H + cell_y] * 16 + point_x * 4 + point_y
        row_ids = jnp.arange(row_count, dtype=jnp.int32)
        slot_ids = row_ids // 16
        point_x = row_ids % 16 // 4
        point_y = row_ids % 4
        cell_index = order_row[slot_ids]
        cell_x = cell_index // H
        cell_y = cell_index % H
        step_x = jnp.where(point_x == 0, -1, jnp.where(point_x == 3, 1, 0))
        step_y = jnp.where(point_y == 0, -1, jnp.where(point_y == 3, 1, 0))
        next_x = cell_x + step_x
        next_y = (cell_y + step_y) % H
        x_valid = (step_x != 0) & (next_x >= 0) & (next_x < W)
        y_valid = step_y != 0
        padding = jnp.int32(row_count)
        along_x = jnp.where(x_valid, row_at(next_x, cell_y, 3 - point_x, point_y), padding)
        along_y = jnp.where(y_valid, row_at(cell_x, next_y, point_x, 3 - point_y), padding)
        diagonal = jnp.where(x_valid & y_valid, row_at(next_x, next_y, 3 - point_x, 3 - point_y), padding)
        partners = jnp.stack([along_x, along_y, diagonal])
        edge_ids = jnp.arange(slot_count, dtype=jnp.int32)
        edge_y = edge_ids // 3
        edge_point = edge_ids % 3
        prev_y = (edge_y - 1) % H
        zero_col = jnp.zeros_like(edge_ids)
        left_first = row_at(zero_col, edge_y, 0, edge_point)
        right_first = row_at(zero_col + (W - 1), edge_y, 3, edge_point)
        left_second = jnp.where(edge_point == 0, row_at(zero_col, prev_y, 0, 3), padding)
        right_second = jnp.where(edge_point == 0, row_at(zero_col + (W - 1), prev_y, 3, 3), padding)
        sends = jnp.stack([right_first, left_first])
        receives = jnp.stack([left_first, left_second, right_first, right_second])
        return (partners.astype(jnp.int32), sends.astype(jnp.int32), receives.astype(jnp.int32))
    partners, sends, receives = jax.vmap(device_maps)(cell_order, slot_lookup)
    partner_all = jnp.transpose(partners, (1, 0, 2)).reshape(3, devices * row_count)
    return (partner_all, sends.reshape(devices * 2, slot_count), receives.reshape(devices * 4, slot_count))


def draw_partner(key, part):
    return strip_layout(key)[0]


def draw_send_rows(key, part):
    return strip_layout(key)[1]


def draw_recv_rows(key, part):
    return strip_layout(key)[2]


def draw_inv_mass(key, part):
    key = jax.random.fold_in(key, 7)
    row_count = 16 * H * W * N_ELEM
    row_ids = jnp.arange(row_count, dtype=jnp.int32)
    point_x = row_ids % 16 // 4
    point_y = row_ids % 4
    weight_vec = jnp.array([1.0, 5.0, 5.0, 1.0], jnp.float32) / 6.0
    copies_x = jnp.where((point_x == 0) | (point_x == 3), 2.0, 1.0)
    copies_y = jnp.where((point_y == 0) | (point_y == 3), 2.0, 1.0)
    gain_values = jax.random.uniform(key, (row_count,), jnp.float32, 0.7, 1.4)
    return (gain_values / (weight_vec[point_x] * weight_vec[point_y] * copies_x * copies_y)).astype(jnp.float32)


def level_of(rng, extent, cuts, low, high):
    factor_of, own = 1.0, jax.random.fold_in(rng, 6)
    for position, parts in cuts:
        heights = jnp.exp(jax.random.uniform(jax.random.fold_in(own, position), (parts,), jnp.float32, low / len(cuts), high / len(cuts)))
        factor_of = factor_of * jnp.repeat(heights, extent[position] // parts).reshape([-1 if axis == position else 1 for axis in range(len(extent))])
    return factor_of


def noise(own_key, extent, width, reach, shards=(), kind=jnp.bfloat16):
    drawn = width * jax.random.normal(own_key, extent, jnp.float32)
    if shards:
        drawn = drawn * level_of(own_key, extent, shards, -0.22, 0.18)
    return jnp.clip(drawn, -reach, reach).astype(kind)


def setup_inputs(seed: int = 0) -> dict:
    key_of = jax.random.split(jax.random.key(seed), 8)
    return {
        "prognostic": noise(key_of[0], (ROWS, LF), 1.0, 6.0, ((0, 128),), jnp.float32),
        "metric": jnp.clip(0.5 + 0.5 * jax.random.uniform(key_of[1], (2, ROWS), jnp.float32) ** level_of(key_of[1], (2, ROWS), ((1, 128),), -0.2, 0.2), 0.5, 1.0),
        "inv_mass": draw_inv_mass(jax.random.fold_in(key_of[7], 71), 0),
        "viscosity": jnp.clip(jnp.exp(jax.random.uniform(key_of[3], (LF,), jnp.float32, math.log(7.999999797903001e-05), math.log(0.00024))), 7.999999797903001e-05, 0.00024),
        "partner": draw_partner(jax.random.fold_in(key_of[7], 71), 0),
        "send_rows": draw_send_rows(jax.random.fold_in(key_of[7], 71), 0),
        "recv_rows": draw_recv_rows(jax.random.fold_in(key_of[7], 71), 0),
    }


curve_offsets = (1, -1)

def node_tables():
    root = 1.0 / math.sqrt(5.0)
    points = [-1.0, -root, root, 1.0]
    weights = np.array([1.0, 5.0, 5.0, 1.0]) / 6.0
    products = []
    for first in range(4):
        value = 1.0
        for other in range(4):
            if other != first:
                value = value * (points[first] - points[other])
        products.append(value)
    table = []
    for first in range(4):
        line = []
        for other in range(4):
            if other == first:
                total = 0.0
                for third in range(4):
                    if third != first:
                        total = total + 1.0 / (points[first] - points[third])
                line.append(total)
            else:
                line.append(products[first] / (products[other] * (points[first] - points[other])))
        table.append(line)
    return (np.array(table), weights)

def weak_laplacian(values, metric_x, metric_y):
    derivative, weights = node_tables()
    derivative = jnp.asarray(derivative, jnp.float32)
    weight_vec = jnp.asarray(weights, jnp.float32)
    along_i = weight_vec.reshape(1, 4, 1, 1)
    along_j = weight_vec.reshape(1, 1, 4, 1)
    element_grid = values.reshape(-1, 4, 4, values.shape[-1])
    highest = lax.Precision.HIGHEST
    grad_x = jnp.einsum('ik,ekjc->eijc', derivative, element_grid, precision=highest)
    grad_y = jnp.einsum('jk,eikc->eijc', derivative, element_grid, precision=highest)
    flux_x = metric_x * grad_x * along_i
    flux_y = metric_y * grad_y * along_j
    part_x = jnp.einsum('ki,ekjc->eijc', derivative, flux_x, precision=highest) * along_j
    part_y = jnp.einsum('kj,eikc->eijc', derivative, flux_y, precision=highest) * along_i
    return -(part_x + part_y).reshape(values.shape)

def take_rows(table, index):
    return jax.vmap(lambda block, picks: block[picks])(table, index)

def add_rows(table, picks, extra):
    return table.at[picks].add(extra)

def assemble(values, partner, send_rows, recv_rows, inv_mass):
    devices = N_ELEM
    columns = values.shape[-1]
    per_device = values.reshape(devices, -1, columns)
    row_count = per_device.shape[1]
    zero_rows = jnp.zeros((devices, 1, columns), values.dtype)
    padded = jnp.concatenate([per_device, zero_rows], axis=1)
    links = partner.reshape(3, devices, row_count)
    local_sum = per_device + take_rows(padded, links[0]) + take_rows(padded, links[1]) + take_rows(padded, links[2])
    sendable = jnp.concatenate([local_sum, zero_rows], axis=1)
    outgoing = send_rows.reshape(devices, 2, -1)
    incoming = recv_rows.reshape(devices, 4, -1)
    arrived = jnp.zeros((devices, row_count + 1, columns), values.dtype)
    for direction, offset in enumerate(curve_offsets):
        payload = take_rows(sendable, outgoing[:, direction])
        landed = jnp.roll(payload, offset, axis=0)
        for copy_index in range(2):
            arrived = jax.vmap(add_rows)(arrived, incoming[:, 2 * direction + copy_index], landed)
    total = (local_sum + arrived[:, :row_count]) * inv_mass.reshape(devices, row_count, 1)
    return total.reshape(values.shape)

def reference(prognostic, metric, inv_mass, viscosity, partner, send_rows, recv_rows):
    metric_x = metric[0].reshape(-1, 4, 4, 1)
    metric_y = metric[1].reshape(-1, 4, 4, 1)
    fields = prognostic
    for subcycle in range(SUBCYCLES):
        first_pass = assemble(weak_laplacian(fields, metric_x, metric_y), partner, send_rows, recv_rows, inv_mass)
        second_pass = assemble(weak_laplacian(first_pass, metric_x, metric_y), partner, send_rows, recv_rows, inv_mass)
        fields = fields - viscosity[None, :] * second_pass
    return fields
```

```python
import math

import jax
import jax.numpy as jnp
import numpy as np
from jax import lax
from jax.experimental import pallas as pl
from jax.experimental.pallas import tpu as pltpu
from jax.sharding import PartitionSpec as P

SUBCYCLES = 2
ELEMS = 256
ROWS = 16 * ELEMS
COLS = 128
EDGE = 3 * ELEMS
SEGS = 8
STEPS = ELEMS // SEGS
NONE = ROWS
VMEM_LIMIT = 24 * 2**20
HIGH = lax.Precision.HIGHEST


def node_tables():
    root = 1.0 / math.sqrt(5.0)
    points = [-1.0, -root, root, 1.0]
    weights = np.array([1.0, 5.0, 5.0, 1.0]) / 6.0
    products = []
    for first in range(4):
        value = 1.0
        for other in range(4):
            if other != first:
                value = value * (points[first] - points[other])
        products.append(value)
    table = []
    for first in range(4):
        line = []
        for other in range(4):
            if other == first:
                total = 0.0
                for third in range(4):
                    if third != first:
                        total = total + 1.0 / (points[first] - points[third])
                line.append(total)
            else:
                line.append(products[first] / (products[other] * (points[first] - points[other])))
        table.append(line)
    return (np.array(table), weights)


D, WEIGHTS = node_tables()


def gradient(v):
    o0, o1 = v[0] - v[3], v[1] - v[2]
    h = (v[0] + v[3]) - (v[1] + v[2])
    q0 = float(0.5 * (D[0, 0] + D[0, 3])) * h
    q1 = float(0.5 * (D[1, 0] + D[1, 3])) * h
    s0 = float(0.5 * (D[0, 0] - D[0, 3])) * o0 + float(0.5 * (D[0, 1] - D[0, 2])) * o1
    s1 = float(0.5 * (D[1, 0] - D[1, 3])) * o0 + float(0.5 * (D[1, 1] - D[1, 2])) * o1
    return [s0 + q0, s1 + q1, s1 - q1, s0 - q0]


def divergence(f):
    g0, g1 = f[0] - f[3], f[1] - f[2]
    t0, t1 = f[0] + f[3], f[1] + f[2]
    z = float(0.5 * (D[0, 0] + D[0, 3])) * g0 + float(0.5 * (D[1, 0] + D[1, 3])) * g1
    r0 = float(0.5 * (D[0, 0] - D[0, 3])) * t0 + float(0.5 * (D[1, 0] - D[1, 3])) * t1
    r1 = float(0.5 * (D[0, 1] - D[0, 2])) * t0 + float(0.5 * (D[1, 1] - D[1, 2])) * t1
    return [z + r0, r1 - z, -z - r1, z - r0]


def weak(x, mx, my):
    out = [None] * 16
    for j in range(4):
        g = gradient([x[4 * i + j] for i in range(4)])
        f = divergence([mx(4 * i + j) * g[i] for i in range(4)])
        for i in range(4):
            out[4 * i + j] = f[i]
    for i in range(4):
        g = gradient([x[4 * i + j] for j in range(4)])
        f = divergence([my(4 * i + j) * g[j] for j in range(4)])
        for j in range(4):
            out[4 * i + j] = out[4 * i + j] + f[j]
    return out


def plane(ref, q, t):
    return ref[pl.ds(pl.multiple_of(q * ELEMS + t * SEGS, SEGS), SEGS), :]


def set_plane(ref, q, t, value):
    ref[pl.ds(pl.multiple_of(q * ELEMS + t * SEGS, SEGS), SEGS), :] = value


def following(ref, q, t):
    last = t == STEPS - 1
    value = plane(ref, q, jnp.where(last, 0, t + 1))
    return jnp.where(last, pltpu.roll(value, SEGS - 1, 0), value)


def place_of(y):
    return lax.rem(y, STEPS) * SEGS + lax.div(y, STEPS)


def state_row(r):
    return lax.rem(r, 16) * ELEMS + place_of(lax.div(r, 16))


def wire_row(m):
    return lax.rem(m, 3) * ELEMS + place_of(lax.div(m, 3))


def one(ref, row):
    return ref[pl.ds(row, 1), :]


def ring_sums(s_ref):
    for i in range(4):
        for t in range(STEPS):
            upper = plane(s_ref, 4 * i, (t + 1) % STEPS)
            if t == STEPS - 1:
                upper = first
                lower = plane(s_ref, 4 * i + 3, t)
                total = lower + pltpu.roll(upper, SEGS - 1, 0)
                set_plane(s_ref, 4 * i + 3, t, total)
                set_plane(s_ref, 4 * i, 0, pltpu.roll(total, 1, 0))
            else:
                if t == 0:
                    first = plane(s_ref, 4 * i, 0)
                total = plane(s_ref, 4 * i + 3, t) + upper
                set_plane(s_ref, 4 * i + 3, t, total)
                set_plane(s_ref, 4 * i, t + 1, total)


def edge_messages(s_ref, behind_ref, ahead_ref):
    behind_ref[...] = s_ref[0:EDGE, :]
    ahead_ref[...] = s_ref[12 * ELEMS:15 * ELEMS, :]


def general_sums(v_ref, s_ref, partner_any, partner_s):
    pltpu.sync_copy(partner_any, partner_s)

    def body(r, carry):
        total = one(v_ref, state_row(r))
        for k in range(3):
            other = partner_s[k, r]
            found = one(v_ref, state_row(jnp.minimum(other, ROWS - 1)))
            total = total + jnp.where(other < NONE, found, 0.0)
        s_ref[pl.ds(state_row(r), 1), :] = total
        return carry

    lax.fori_loop(0, ROWS, body, 0)


def general_messages(s_ref, behind_ref, ahead_ref, send_any, send_s):
    pltpu.sync_copy(send_any, send_s)

    def body(m, carry):
        ahead_ref[pl.ds(wire_row(m), 1), :] = one(s_ref, state_row(send_s[0, m]))
        behind_ref[pl.ds(wire_row(m), 1), :] = one(s_ref, state_row(send_s[1, m]))
        return carry

    lax.fori_loop(0, EDGE, body, 0)


def general_receive(total_ref, left_ref, right_ref, recv_any, recv_s):
    pltpu.sync_copy(recv_any, recv_s)

    def body(m, carry):
        for k, arrived in ((0, left_ref), (1, right_ref)):
            for c in range(2):
                target = recv_s[2 * k + c, m]

                @pl.when(target < NONE)
                def _():
                    row = pl.ds(state_row(target), 1)
                    total_ref[row, :] = total_ref[row, :] + one(arrived, wire_row(m))
        return carry

    lax.fori_loop(0, EDGE, body, 0)


def finish(ok, v_ref, s_ref, behind_ref, ahead_ref, partner_any, send_any, partner_s, send_s):
    @pl.when(ok)
    def _():
        ring_sums(s_ref)
        edge_messages(s_ref, behind_ref, ahead_ref)

    @pl.when(jnp.logical_not(ok))
    def _():
        general_sums(v_ref, s_ref, partner_any, partner_s)
        general_messages(s_ref, behind_ref, ahead_ref, send_any, send_s)


def iota(shape, axis):
    return lax.broadcasted_iota(jnp.int32, shape, axis)


def count(bad):
    return jnp.sum(jnp.where(bad, 1.0, 0.0))


def by_element(chunks):
    own = (iota((16, 256), 1) >> 4) == iota((16, 256), 0)
    return jnp.concatenate([jnp.where(own, jnp.broadcast_to(c, (16, 256)), 0.0) for c in chunks], axis=0)


def first_kernel(prog, metric, inv_mass, send_s, send_v, recv_v, partner_v, partner_any, send_any,
                 u_ref, s_ref, mx_ref, my_ref, im_ref, behind_ref, ahead_ref, flag_ref,
                 raw, v_ref, table, partner_s, send_g, sem):
    load = pltpu.make_async_copy(prog, raw, sem)
    load.start()

    send = send_v[...]
    order_row = send[0:1, :] >> 4
    place = iota((ELEMS, 1), 0)
    ring = (place & 7) * STEPS + (place >> 3)
    picked = iota((ELEMS, EDGE), 1) == 3 * ring + 1
    order = jnp.sum(jnp.where(picked, order_row.astype(jnp.float32), 0.0), axis=1, keepdims=True)
    lane_e = iota((ELEMS, ELEMS), 1)
    hot = (lane_e.astype(jnp.float32) == order).astype(jnp.float32)
    bad = count(jnp.sum(hot, axis=0, keepdims=True) != 1.0)

    partner = partner_v[...]
    least = jnp.minimum(jnp.minimum(partner[0:1], partner[1:2]), partner[2:3]).astype(jnp.float32)
    added = (partner[0:1] + partner[1:2] + partner[2:3]).astype(jnp.float32)
    mass = inv_mass[...]
    groups = []
    for k in range(2):
        row = metric[k:k + 1, :]
        groups.append([row[:, 256 * c:256 * c + 256] for c in range(16)])
    groups.append([jnp.concatenate([mass[2 * c:2 * c + 1, :], mass[2 * c + 1:2 * c + 2, :]], axis=1) for c in range(16)])
    for row in (least, added):
        groups.append([row[:, 256 * c:256 * c + 256] for c in range(16)])
    point = iota((256, 128), 0) & 15
    lane = iota((256, 128), 1)
    raw_table = jnp.zeros((ELEMS, 128), jnp.float32)
    for g, chunks in enumerate(groups):
        chosen = (lane == point + 16 * g).astype(jnp.float32)
        raw_table = raw_table + jnp.dot(by_element(chunks), chosen, precision=HIGH, preferred_element_type=jnp.float32)
    ordered = jnp.dot(hot, raw_table, precision=HIGH, preferred_element_type=jnp.float32)

    last = order[(STEPS - 1) * SEGS:, :]
    before = jnp.concatenate([pltpu.roll(jnp.broadcast_to(last, (SEGS, 128)), 1, 0)[:, 0:1], order[:-SEGS, :]], axis=0)
    after = jnp.concatenate([order[SEGS:, :], pltpu.roll(jnp.broadcast_to(order[:SEGS, :], (SEGS, 128)), SEGS - 1, 0)[:, 0:1]], axis=0)
    point_i = (lane >> 2) & 3
    point_j = lane & 3
    group = lane >> 4
    offset = (4 * point_i).astype(jnp.float32)
    expect = jnp.where(point_j == 0, 16.0 * before + offset + 3.0,
                       jnp.where(point_j == 3, 16.0 * after + offset, float(NONE)))
    expect = expect + jnp.where(group == 4, float(2 * NONE), 0.0)
    bad = bad + count(((group == 3) | (group == 4)) & (ordered != expect))

    m = iota((1, EDGE), 1)
    p = m - 3 * ((m * 43691) >> 17)
    wide = jnp.broadcast_to(order_row, (8, EDGE))
    up1 = pltpu.roll(wide, EDGE - 1, 1)[0:1]
    down1 = pltpu.roll(wide, 1, 1)[0:1]
    down2 = pltpu.roll(wide, 2, 1)[0:1]
    own = 16 * jnp.where(p == 0, up1, jnp.where(p == 1, order_row, down1)) + p
    other = jnp.where(p == 0, 16 * down2 + 3, NONE)
    recv = recv_v[...]
    for k, shift in ((0, 12), (1, 0)):
        named = send[k:k + 1, :] - shift
        bad = bad + count((named != own) & ((p != 0) | (named != other)))
        a, b = recv[2 * (1 - k):2 * (1 - k) + 1, :], recv[2 * (1 - k) + 1:2 * (1 - k) + 2, :]
        want = jnp.where(p == 0, other + shift, NONE)
        bad = bad + count((jnp.minimum(a, b) != jnp.minimum(own + shift, want))
                          | (jnp.maximum(a, b) != jnp.maximum(own + shift, want)))
    ok = bad == 0.0
    flag_ref[0] = jnp.where(ok, 1, 0)

    table[...] = ordered

    @pl.when(jnp.logical_not(ok))
    def _():
        same = (lane_e == ring).astype(jnp.float32)
        table[...] = jnp.dot(same, raw_table, precision=HIGH, preferred_element_type=jnp.float32)

    placed = table[...]
    for q in range(16):
        scale = -float(WEIGHTS[q // 4] * WEIGHTS[q % 4])
        rows = slice(q * ELEMS, (q + 1) * ELEMS)
        mx_ref[rows, :] = jnp.broadcast_to(scale * placed[:, q:q + 1], (ELEMS, 128))
        my_ref[rows, :] = jnp.broadcast_to(scale * placed[:, 16 + q:17 + q], (ELEMS, 128))
        im_ref[rows, :] = jnp.broadcast_to(placed[:, 32 + q:33 + q], (ELEMS, 128))

    load.wait()

    def gather(t, carry):
        for s in range(SEGS):
            y = STEPS * s + t
            e = jnp.where(ok, send_s[0, 3 * y + 1] >> 4, y)
            for half in range(2):
                value = raw[pl.ds(pl.multiple_of(16 * e + 8 * half, 8), 8), :]
                u_ref[pl.ds(8 * half * ELEMS + t * SEGS + s, 8, stride=ELEMS), :] = value
        return carry

    lax.fori_loop(0, STEPS, gather, 0)

    def body(t, carry):
        x = [plane(u_ref, q, t) for q in range(16)]
        out = weak(x, lambda q: plane(mx_ref, q, t), lambda q: plane(my_ref, q, t))
        for q in range(16):
            set_plane(s_ref, q, t, out[q])
        return carry

    lax.fori_loop(0, STEPS, body, 0)

    @pl.when(jnp.logical_not(ok))
    def _():
        v_ref[...] = s_ref[...]

    finish(ok, v_ref, s_ref, behind_ref, ahead_ref, partner_any, send_any, partner_s, send_g)


def joined(s_ref, left_ref, right_ref, im_ref, t):
    x = [plane(s_ref, q, t) for q in range(16)]
    for base, arrived in ((0, left_ref), (12, right_ref)):
        for j in range(3):
            x[base + j] = x[base + j] + plane(arrived, j, t)
        x[base + 3] = x[base + 3] + following(arrived, 0, t)
    return [x[q] * plane(im_ref, q, t) for q in range(16)]


def pass_kernel(updates, flag, s_in, left, right, mx_ref, my_ref, im_ref, u_in, visc, partner_any, send_any, recv_any, *rest):
    if updates:
        u_ref, s_ref, behind_ref, ahead_ref, v_ref, partner_s, send_s, recv_s = rest
    else:
        s_ref, behind_ref, ahead_ref, v_ref, partner_s, send_s, recv_s = rest
    ok = flag[0] == 1

    def step(t, x, out_ref):
        if updates:
            rate = visc[...]
            for q in range(16):
                x[q] = plane(u_in, q, t) - rate * x[q]
                set_plane(u_ref, q, t, x[q])
        out = weak(x, lambda q: plane(mx_ref, q, t), lambda q: plane(my_ref, q, t))
        for q in range(16):
            set_plane(out_ref, q, t, out[q])

    @pl.when(ok)
    def _():
        def body(t, carry):
            step(t, joined(s_in, left, right, im_ref, t), s_ref)
            return carry

        lax.fori_loop(0, STEPS, body, 0)

    @pl.when(jnp.logical_not(ok))
    def _():
        v_ref[...] = s_in[...]
        general_receive(v_ref, left, right, recv_any, recv_s)

        def body(t, carry):
            step(t, [plane(v_ref, q, t) * plane(im_ref, q, t) for q in range(16)], v_ref)
            return carry

        lax.fori_loop(0, STEPS, body, 0)

    finish(ok, v_ref, s_ref, behind_ref, ahead_ref, partner_any, send_any, partner_s, send_s)


def last_kernel(flag, order_s, s_in, left, right, im_ref, u_in, visc, recv_any, out, u_ref, raw, v_ref, recv_s, sem):
    ok = flag[0] == 1
    rate = visc[...]

    @pl.when(ok)
    def _():
        def body(t, carry):
            x = joined(s_in, left, right, im_ref, t)
            for q in range(16):
                set_plane(u_ref, q, t, plane(u_in, q, t) - rate * x[q])
            return carry

        lax.fori_loop(0, STEPS, body, 0)

    @pl.when(jnp.logical_not(ok))
    def _():
        v_ref[...] = s_in[...]
        general_receive(v_ref, left, right, recv_any, recv_s)
        u_ref[...] = u_in[...] - rate * (v_ref[...] * im_ref[...])

    def scatter(t, carry):
        for s in range(SEGS):
            y = STEPS * s + t
            e = jnp.where(ok, order_s[0, 3 * y + 1] >> 4, y)
            for half in range(2):
                value = u_ref[pl.ds(8 * half * ELEMS + t * SEGS + s, 8, stride=ELEMS), :]
                raw[pl.ds(pl.multiple_of(16 * e + 8 * half, 8), 8), :] = value
        return carry

    lax.fori_loop(0, STEPS, scatter, 0)
    store = pltpu.make_async_copy(raw, out, sem)
    store.start()
    store.wait()


VM = pl.BlockSpec(memory_space=pltpu.VMEM)
SM = pl.BlockSpec(memory_space=pltpu.SMEM)
HB = pl.BlockSpec(memory_space=pl.ANY)
FIELD = jax.ShapeDtypeStruct((ROWS, COLS), jnp.float32)
MESSAGE = jax.ShapeDtypeStruct((EDGE, COLS), jnp.float32)
SCRATCH = pltpu.VMEM((ROWS, COLS), jnp.float32)
PARTNER_S = pltpu.SMEM((3, ROWS), jnp.int32)
SEND_S = pltpu.SMEM((2, EDGE), jnp.int32)
RECV_S = pltpu.SMEM((4, EDGE), jnp.int32)


def call(kernel, ins, outs, specs, shapes, scratch, flops, moved, name):
    return pl.pallas_call(
        kernel,
        out_shape=shapes,
        in_specs=specs,
        out_specs=outs,
        scratch_shapes=scratch,
        compiler_params=pltpu.CompilerParams(vmem_limit_bytes=VMEM_LIMIT),
        cost_estimate=pl.CostEstimate(flops=flops, bytes_accessed=moved, transcendentals=0),
        name=name,
    )(*ins)


def swap(behind, ahead):
    size = lax.axis_size("elem")
    left = lax.ppermute(ahead, "elem", [(i, (i + 1) % size) for i in range(size)])
    right = lax.ppermute(behind, "elem", [(i, (i - 1) % size) for i in range(size)])
    return left, right


def shards(prognostic, metric, inv_mass, viscosity, partner, send_rows, recv_rows):
    visc = viscosity.reshape(1, COLS)
    work = 24 * ROWS * COLS
    u, s, mx, my, im, behind, ahead, flag = call(
        first_kernel,
        (prognostic, metric, inv_mass.reshape(ROWS // 128, 128), send_rows, send_rows, recv_rows, partner, partner, send_rows),
        [VM, VM, VM, VM, VM, VM, VM, SM],
        [HB, VM, VM, SM, VM, VM, VM, HB, HB],
        [FIELD, FIELD, FIELD, FIELD, FIELD, MESSAGE, MESSAGE, jax.ShapeDtypeStruct((1,), jnp.int32)],
        [SCRATCH, SCRATCH, pltpu.VMEM((ELEMS, 128), jnp.float32), PARTNER_S, SEND_S, pltpu.SemaphoreType.DMA],
        2 * work, 8 * 4 * ROWS * COLS, "first",
    )
    for cycle in range(SUBCYCLES):
        for updates in (False, True):
            left, right = swap(behind, ahead)
            if updates and cycle == SUBCYCLES - 1:
                break
            ins = (flag, s, left, right, mx, my, im, u, visc, partner, send_rows, recv_rows)
            shapes = [FIELD] * (2 if updates else 1) + [MESSAGE, MESSAGE]
            results = call(
                lambda *refs, updates=updates: pass_kernel(updates, *refs),
                ins, [VM] * len(shapes), [SM, VM, VM, VM, VM, VM, VM, VM, VM, HB, HB, HB], shapes,
                [SCRATCH, PARTNER_S, SEND_S, RECV_S],
                work, 6 * 4 * ROWS * COLS, "update" if updates else "second",
            )
            if updates:
                u = results[0]
            s, behind, ahead = results[-3:]
    return call(
        last_kernel,
        (flag, send_rows, s, left, right, im, u, visc, recv_rows),
        HB, [SM, SM, VM, VM, VM, VM, VM, VM, HB], FIELD,
        [SCRATCH, SCRATCH, SCRATCH, RECV_S, pltpu.SemaphoreType.DMA],
        work // 8, 4 * 4 * ROWS * COLS, "last",
    )


def solution(mesh):
    placed = (
        P("elem", None),
        P(None, "elem"),
        P("elem"),
        P(),
        P(None, "elem"),
        P("elem", None),
        P("elem", None),
    )
    return jax.shard_map(
        shards, mesh=mesh, in_specs=placed, out_specs=P("elem", None), check_vma=False
    )
```

```python
import math

import jax
import jax.numpy as jnp
import numpy as np
from jax import lax
from jax.experimental import pallas as pl
from jax.experimental.pallas import tpu as pltpu
from jax.sharding import PartitionSpec as P

SUBCYCLES = 2
ELEMS = 256
ROWS = 16 * ELEMS
COLS = 128
EDGE = 3 * ELEMS
SEGS = 8
STEPS = ELEMS // SEGS
NONE = ROWS
VMEM_LIMIT = 24 * 2**20


def node_tables():
    root = 1.0 / math.sqrt(5.0)
    points = [-1.0, -root, root, 1.0]
    weights = np.array([1.0, 5.0, 5.0, 1.0]) / 6.0
    products = []
    for first in range(4):
        value = 1.0
        for other in range(4):
            if other != first:
                value = value * (points[first] - points[other])
        products.append(value)
    table = []
    for first in range(4):
        line = []
        for other in range(4):
            if other == first:
                total = 0.0
                for third in range(4):
                    if third != first:
                        total = total + 1.0 / (points[first] - points[third])
                line.append(total)
            else:
                line.append(products[first] / (products[other] * (points[first] - points[other])))
        table.append(line)
    return (np.array(table), weights)


D, WEIGHTS = node_tables()


def gradient(v):
    o0, o1 = v[0] - v[3], v[1] - v[2]
    h = (v[0] + v[3]) - (v[1] + v[2])
    q0 = float(0.5 * (D[0, 0] + D[0, 3])) * h
    q1 = float(0.5 * (D[1, 0] + D[1, 3])) * h
    s0 = float(0.5 * (D[0, 0] - D[0, 3])) * o0 + float(0.5 * (D[0, 1] - D[0, 2])) * o1
    s1 = float(0.5 * (D[1, 0] - D[1, 3])) * o0 + float(0.5 * (D[1, 1] - D[1, 2])) * o1
    return [s0 + q0, s1 + q1, s1 - q1, s0 - q0]


def divergence(f):
    g0, g1 = f[0] - f[3], f[1] - f[2]
    t0, t1 = f[0] + f[3], f[1] + f[2]
    z = float(0.5 * (D[0, 0] + D[0, 3])) * g0 + float(0.5 * (D[1, 0] + D[1, 3])) * g1
    r0 = float(0.5 * (D[0, 0] - D[0, 3])) * t0 + float(0.5 * (D[1, 0] - D[1, 3])) * t1
    r1 = float(0.5 * (D[0, 1] - D[0, 2])) * t0 + float(0.5 * (D[1, 1] - D[1, 2])) * t1
    return [z + r0, r1 - z, -z - r1, z - r0]


def weak(x, mx, my):
    out = [None] * 16
    for j in range(4):
        g = gradient([x[4 * i + j] for i in range(4)])
        f = divergence([mx(4 * i + j) * g[i] for i in range(4)])
        for i in range(4):
            out[4 * i + j] = f[i]
    for i in range(4):
        g = gradient([x[4 * i + j] for j in range(4)])
        f = divergence([my(4 * i + j) * g[j] for j in range(4)])
        for j in range(4):
            out[4 * i + j] = out[4 * i + j] + f[j]
    return out


def plane(ref, q, t):
    return ref[pl.ds(pl.multiple_of(q * ELEMS + t * SEGS, SEGS), SEGS), :]


def set_plane(ref, q, t, value):
    ref[pl.ds(pl.multiple_of(q * ELEMS + t * SEGS, SEGS), SEGS), :] = value


def following(ref, q, t):
    last = t == STEPS - 1
    value = plane(ref, q, jnp.where(last, 0, t + 1))
    return jnp.where(last, pltpu.roll(value, SEGS - 1, 0), value)


def place_of(y):
    return lax.rem(y, STEPS) * SEGS + lax.div(y, STEPS)


def state_row(r):
    return lax.rem(r, 16) * ELEMS + place_of(lax.div(r, 16))


def wire_row(m):
    return lax.rem(m, 3) * ELEMS + place_of(lax.div(m, 3))


def one(ref, row):
    return ref[pl.ds(row, 1), :]


def ring_sums(s_ref):
    for i in range(4):
        for t in range(STEPS):
            upper = plane(s_ref, 4 * i, (t + 1) % STEPS)
            if t == STEPS - 1:
                upper = first
                lower = plane(s_ref, 4 * i + 3, t)
                total = lower + pltpu.roll(upper, SEGS - 1, 0)
                set_plane(s_ref, 4 * i + 3, t, total)
                set_plane(s_ref, 4 * i, 0, pltpu.roll(total, 1, 0))
            else:
                if t == 0:
                    first = plane(s_ref, 4 * i, 0)
                total = plane(s_ref, 4 * i + 3, t) + upper
                set_plane(s_ref, 4 * i + 3, t, total)
                set_plane(s_ref, 4 * i, t + 1, total)


def edge_messages(s_ref, behind_ref, ahead_ref):
    behind_ref[...] = s_ref[0:EDGE, :]
    ahead_ref[...] = s_ref[12 * ELEMS:15 * ELEMS, :]


def general_sums(v_ref, s_ref, partner_any, partner_s):
    pltpu.sync_copy(partner_any, partner_s)

    def body(r, carry):
        total = one(v_ref, state_row(r))
        for k in range(3):
            other = partner_s[k, r]
            found = one(v_ref, state_row(jnp.minimum(other, ROWS - 1)))
            total = total + jnp.where(other < NONE, found, 0.0)
        s_ref[pl.ds(state_row(r), 1), :] = total
        return carry

    lax.fori_loop(0, ROWS, body, 0)


def general_messages(s_ref, behind_ref, ahead_ref, send_any, send_s):
    pltpu.sync_copy(send_any, send_s)

    def body(m, carry):
        ahead_ref[pl.ds(wire_row(m), 1), :] = one(s_ref, state_row(send_s[0, m]))
        behind_ref[pl.ds(wire_row(m), 1), :] = one(s_ref, state_row(send_s[1, m]))
        return carry

    lax.fori_loop(0, EDGE, body, 0)


def general_receive(total_ref, left_ref, right_ref, recv_any, recv_s):
    pltpu.sync_copy(recv_any, recv_s)

    def body(m, carry):
        for k, arrived in ((0, left_ref), (1, right_ref)):
            for c in range(2):
                target = recv_s[2 * k + c, m]

                @pl.when(target < NONE)
                def _():
                    row = pl.ds(state_row(target), 1)
                    total_ref[row, :] = total_ref[row, :] + one(arrived, wire_row(m))
        return carry

    lax.fori_loop(0, EDGE, body, 0)


def iota(shape, axis):
    return lax.broadcasted_iota(jnp.int32, shape, axis)


def flipped(v):
    sub = iota((SEGS, COLS), 0)
    for b in (1, 2, 4):
        low = (sub & b) == 0
        out = list(v)
        for i in range(8):
            if i & b == 0:
                out[i] = jnp.where(low, v[i], pltpu.roll(v[i + b], b, 0))
                out[i + b] = jnp.where(low, pltpu.roll(v[i], 8 - b, 0), v[i + b])
        v = out
    return v


def tile(ref, row):
    return ref[pl.ds(pl.multiple_of(row, 8), 8), :]


def lanes_total(bad):
    ones = jnp.where(bad, 1.0, 0.0)
    if ones.shape[0] > 1:
        ones = jnp.sum(ones, axis=0, keepdims=True)
    total = ones[:, 0:128]
    for c in range(1, ones.shape[1] // 128):
        total = total + ones[:, 128 * c:128 * c + 128]
    return total


def pieces(row):
    high = row.astype(jnp.bfloat16).astype(jnp.float32)
    rest = row - high
    middle = rest.astype(jnp.bfloat16).astype(jnp.float32)
    return [high, middle, rest - middle]


def element_table(groups):
    own = (iota((16, 256), 1) >> 4) == iota((16, 256), 0)
    lane = iota((256, 128), 1)
    point = iota((256, 128), 0) & 15
    table = None
    for g, chunks in enumerate(groups):
        rows = [jnp.where(own, jnp.broadcast_to(c, (16, 256)), 0.0) for c in chunks]
        spread = jnp.concatenate(rows, axis=0).astype(jnp.bfloat16)
        chosen = (lane == point + 16 * g).astype(jnp.float32).astype(jnp.bfloat16)
        part = jnp.dot(spread, chosen, preferred_element_type=jnp.float32)
        table = part if table is None else table + part
    return table


def in_order(order, table):
    hot = (iota((ELEMS, ELEMS), 1).astype(jnp.float32) == order).astype(jnp.float32).astype(jnp.bfloat16)
    return jnp.dot(hot, table.astype(jnp.bfloat16), preferred_element_type=jnp.float32)


def first_kernel(prog, metric_h, send_h, recv_h, partner_h,
                 u_ref, s_ref, mx_ref, my_ref, order_ref, behind_ref, ahead_ref, flag_ref,
                 raw, v_ref, table, metric, send_v, recv_v, partner_v, send_s, partner_s, sems):
    loads = [pltpu.make_async_copy(a, b, sems.at[k]) for k, (a, b) in enumerate(
        ((send_h, send_v), (metric_h, metric), (partner_h, partner_v), (recv_h, recv_v), (send_h, send_s), (prog, raw)))]
    for load in loads:
        load.start()
    loads[0].wait()

    send = send_v[...]
    order_row = send[0:1, :] >> 4
    place = iota((ELEMS, 1), 0)
    ring = (place & 7) * STEPS + (place >> 3)
    picked = iota((ELEMS, EDGE), 1) == 3 * ring + 1
    order = jnp.sum(jnp.where(picked, order_row.astype(jnp.float32), 0.0), axis=1, keepdims=True)
    hot = (iota((ELEMS, ELEMS), 1).astype(jnp.float32) == order).astype(jnp.float32)
    seen = jnp.sum(hot, axis=0, keepdims=True)
    bad = lanes_total(seen != 1.0)

    loads[1].wait()
    loads[2].wait()
    partner = partner_v[...]
    least = jnp.minimum(jnp.minimum(partner[0:1], partner[1:2]), partner[2:3])
    bad = bad + lanes_total(partner[0:1] + partner[1:2] + partner[2:3] - least != 2 * NONE)
    both = [pieces(metric[k:k + 1, :]) for k in range(2)]
    rows = [both[k][n] for n in range(3) for k in range(2)]
    rows += [(least >> 4).astype(jnp.float32), (least & 15).astype(jnp.float32)]
    raw_table = element_table([[row[:, 256 * c:256 * c + 256] for c in range(16)] for row in rows])
    ordered = in_order(order, raw_table)

    wide_order = jnp.broadcast_to(order, (ELEMS, 128))
    before = jnp.concatenate([pltpu.roll(wide_order[ELEMS - SEGS:, :], 1, 0), wide_order[:-SEGS, :]], axis=0)
    after = jnp.concatenate([wide_order[SEGS:, :], pltpu.roll(wide_order[:SEGS, :], SEGS - 1, 0)], axis=0)
    lane = iota((1, 128), 1)
    point_i = (lane >> 2) & 3
    point_j = lane & 3
    expect_a = jnp.where(point_j == 0, before, jnp.where(point_j == 3, after, float(ELEMS)))
    expect_b = jnp.where(point_j == 0, 4 * point_i + 3, jnp.where(point_j == 3, 4 * point_i, 0)).astype(jnp.float32)
    expect = jnp.where(lane < 112, expect_a, expect_b)
    bad = bad + lanes_total((lane >= 96) & (ordered != expect))

    loads[3].wait()
    m = iota((1, EDGE), 1)
    p = m - 3 * ((m * 43691) >> 17)
    wide = jnp.broadcast_to(order_row, (8, EDGE))
    up1 = pltpu.roll(wide, EDGE - 1, 1)[0:1]
    down1 = pltpu.roll(wide, 1, 1)[0:1]
    down2 = pltpu.roll(wide, 2, 1)[0:1]
    own = 16 * jnp.where(p == 0, up1, jnp.where(p == 1, order_row, down1)) + p
    other = jnp.where(p == 0, 16 * down2 + 3, NONE)
    recv = recv_v[...]
    for k, shift in ((0, 12), (1, 0)):
        named = send[k:k + 1, :] - shift
        bad = bad + lanes_total((named != own) & ((p != 0) | (named != other)))
        a, b = recv[2 * (1 - k):2 * (1 - k) + 1, :], recv[2 * (1 - k) + 1:2 * (1 - k) + 2, :]
        want = jnp.where(p == 0, other + shift, NONE)
        bad = bad + lanes_total((jnp.minimum(a, b) != jnp.minimum(own + shift, want))
                                | (jnp.maximum(a, b) != jnp.maximum(own + shift, want)))
    ok = jnp.sum(bad) == 0.0
    flag_ref[0] = jnp.where(ok, 1, 0)

    weights = jnp.where((point_i == 0) | (point_i == 3), -1.0, -5.0) * jnp.where((point_j == 0) | (point_j == 3), 1.0, 5.0)
    weights = weights * (1.0 / 36.0)

    def set_table(ordered):
        table[...] = weights * (ordered + pltpu.roll(ordered, 96, 1) + pltpu.roll(ordered, 64, 1))

    set_table(ordered)
    order_ref[...] = wide_order

    @pl.when(jnp.logical_not(ok))
    def _():
        order_ref[...] = jnp.broadcast_to(ring.astype(jnp.float32), (ELEMS, 128))
        set_table(in_order(ring.astype(jnp.float32), raw_table))

    loads[4].wait()
    loads[5].wait()

    def body(t, carry):
        elems = []
        for s in range(SEGS):
            y = STEPS * s + t
            elems.append(16 * jnp.where(ok, send_s[0, 3 * y + 1] >> 4, y))
        x = flipped([tile(raw, e) for e in elems]) + flipped([tile(raw, e + 8) for e in elems])
        row = tile(table, t * SEGS)
        mx, my = [], []
        for q in range(16):
            set_plane(u_ref, q, t, x[q])
            mx.append(jnp.broadcast_to(row[:, q:q + 1], (SEGS, COLS)))
            my.append(jnp.broadcast_to(row[:, 16 + q:17 + q], (SEGS, COLS)))
            set_plane(mx_ref, q, t, mx[q])
            set_plane(my_ref, q, t, my[q])
        out = weak(x, lambda q: mx[q], lambda q: my[q])
        for q in range(16):
            set_plane(s_ref, q, t, out[q])
        return carry

    lax.fori_loop(0, STEPS, body, 0, unroll=2)

    @pl.when(ok)
    def _():
        ring_sums(s_ref)
        edge_messages(s_ref, behind_ref, ahead_ref)

    @pl.when(jnp.logical_not(ok))
    def _():
        v_ref[...] = s_ref[...]
        general_sums(v_ref, s_ref, partner_h, partner_s)
        general_messages(s_ref, behind_ref, ahead_ref, send_h, send_s)


def edge_values(arrived, im_ref, base, t, scale):
    values = [plane(arrived, j, t) for j in range(3)] + [following(arrived, 0, t)]
    values = [values[j] * plane(im_ref, base + j, t) for j in range(4)]
    return values if scale is None else [scale * v for v in values]


def edge_gradient(left, right):
    h, o = left + right, left - right
    q0, q1 = float(0.5 * (D[0, 0] + D[0, 3])) * h, float(0.5 * (D[1, 0] + D[1, 3])) * h
    s0, s1 = float(0.5 * (D[0, 0] - D[0, 3])) * o, float(0.5 * (D[1, 0] - D[1, 3])) * o
    return [s0 + q0, s1 + q1, s1 - q1, s0 - q0]


def along_edge(c, my_ref, base, t):
    g = gradient(c)
    return divergence([plane(my_ref, base + j, t) * g[j] for j in range(4)])


def prepare_kernel(flag, s_in, mx_ref, my_ref, order, inv_mass, im_ref, kx_ref, w_ref, table):
    mass = inv_mass[...]
    mass = [jnp.concatenate([mass[2 * c:2 * c + 1, :], mass[2 * c + 1:2 * c + 2, :]], axis=1) for c in range(16)]
    split = [pieces(c) for c in mass]
    ordered = in_order(order[:, 0:1], element_table([[c[n] for c in split] for n in range(3)]))
    table[...] = ordered + pltpu.roll(ordered, 112, 1) + pltpu.roll(ordered, 96, 1)
    ok = flag[0] == 1

    def body(t, carry):
        row = tile(table, t * SEGS)
        x = []
        for q in range(16):
            im = jnp.broadcast_to(row[:, q:q + 1], (SEGS, COLS))
            set_plane(im_ref, q, t, im)
            x.append(im * plane(s_in, q, t))
        mx = [plane(mx_ref, q, t) for q in range(16)]
        for j in range(4):
            for n, (a, b) in enumerate(((0, 0), (0, 3), (3, 3))):
                total = None
                for k in range(4):
                    term = float(D[k, a] * D[k, b]) * mx[4 * k + j]
                    total = term if total is None else total + term
                set_plane(kx_ref, 4 * n + j, t, total)
        out = weak(x, lambda q: mx[q], lambda q: plane(my_ref, q, t))
        for q in range(16):
            set_plane(w_ref, q, t, out[q])
        return carry

    lax.fori_loop(0, STEPS, body, 0, unroll=2)

    @pl.when(jnp.logical_not(ok))
    def _():
        w_ref[...] = s_in[...]


def edge_kernel(updates, flag, w_ref, left, right, mx_ref, my_ref, im_ref, kx_ref, u_in, visc, partner_any, send_any, recv_any,
                g_ref, behind_ref, ahead_ref, v_ref, partner_s, send_s, recv_s):
    ok = flag[0] == 1

    @pl.when(ok)
    def _():
        scale = -visc[...] if updates else None

        def body(t, carry):
            cl = edge_values(left, im_ref, 0, t, scale)
            cr = edge_values(right, im_ref, 12, t, scale)
            tail = []
            for base, c, out, k0, k1, before in ((0, cl, behind_ref, 0, 4, carry[0]), (12, cr, ahead_ref, 4, 8, carry[1])):
                f = along_edge(c, my_ref, base, t)
                for j in range(4):
                    f[j] = f[j] + plane(w_ref, base + j, t) + plane(kx_ref, k0 + j, t) * cl[j] + plane(kx_ref, k1 + j, t) * cr[j]
                set_plane(out, 0, t, f[0] + before)
                set_plane(out, 1, t, f[1])
                set_plane(out, 2, t, f[2])
                tail.append(f[3])
            return tuple(tail)

        zero = jnp.zeros((SEGS, COLS), jnp.float32)
        tail = lax.fori_loop(0, STEPS, body, (zero, zero), unroll=4)
        for out, last in zip((behind_ref, ahead_ref), tail):
            out[0:SEGS, :] = out[0:SEGS, :] + pltpu.roll(last, 1, 0)

    @pl.when(jnp.logical_not(ok))
    def _():
        v_ref[...] = w_ref[...]
        general_receive(v_ref, left, right, recv_any, recv_s)

        def body(t, carry):
            x = [plane(v_ref, q, t) * plane(im_ref, q, t) for q in range(16)]
            if updates:
                x = [plane(u_in, q, t) - visc[...] * x[q] for q in range(16)]
            out = weak(x, lambda q: plane(mx_ref, q, t), lambda q: plane(my_ref, q, t))
            for q in range(16):
                set_plane(v_ref, q, t, out[q])
            return carry

        lax.fori_loop(0, STEPS, body, 0)
        general_sums(v_ref, g_ref, partner_any, partner_s)
        general_messages(g_ref, behind_ref, ahead_ref, send_any, send_s)


def inner_kernel(kind, flag, w_in, g_in, left, right, mx_ref, my_ref, im_ref, u_in, visc, recv_any, u_ref, w_ref, s_ref, recv_s):
    ok = flag[0] == 1
    rate = visc[...]

    @pl.when(ok)
    def _():
        scale = -rate if kind == 1 else None

        def complete(t, carry):
            cl = edge_values(left, im_ref, 0, t, scale)
            cr = edge_values(right, im_ref, 12, t, scale)
            lines = [along_edge(cl, my_ref, 0, t), along_edge(cr, my_ref, 12, t)]
            for j in range(4):
                g = edge_gradient(cl[j], cr[j])
                f = divergence([plane(mx_ref, 4 * i + j, t) * g[i] for i in range(4)])
                f[0] = f[0] + lines[0][j]
                f[3] = f[3] + lines[1][j]
                for i in range(4):
                    set_plane(s_ref, 4 * i + j, t, plane(w_in, 4 * i + j, t) + f[i])
            if kind == 1:
                for j in range(4):
                    set_plane(u_ref, j, t, plane(u_in, j, t) + cl[j])
                    set_plane(u_ref, 12 + j, t, plane(u_in, 12 + j, t) + cr[j])
                for q in range(4, 12):
                    set_plane(u_ref, q, t, plane(u_in, q, t))
            return carry

        lax.fori_loop(0, STEPS, complete, 0, unroll=2)
        ring_sums(s_ref)

        def onward(t, carry):
            x = [plane(s_ref, q, t) * plane(im_ref, q, t) for q in range(16)]
            if kind != 1:
                x = [plane(u_in, q, t) - rate * x[q] for q in range(16)]
                for q in range(16):
                    set_plane(u_ref, q, t, x[q])
            if kind != 2:
                out = weak(x, lambda q: plane(mx_ref, q, t), lambda q: plane(my_ref, q, t))
                for q in range(16):
                    set_plane(w_ref, q, t, out[q])
            return carry

        lax.fori_loop(0, STEPS, onward, 0, unroll=2)

    @pl.when(jnp.logical_not(ok))
    def _():
        w_ref[...] = g_in[...]
        if kind == 1:
            s_ref[...] = w_in[...]
            general_receive(s_ref, left, right, recv_any, recv_s)
            u_ref[...] = u_in[...] - rate * (s_ref[...] * im_ref[...])
        else:
            u_ref[...] = u_in[...]


def last_kernel(flag, order_s, w_in, left, right, im_ref, u_in, visc, recv_any, out, raw, v_ref, recv_s, sem):
    ok = flag[0] == 1
    rate = visc[...]

    def leave(t, x):
        elems = []
        for s in range(SEGS):
            y = STEPS * s + t
            elems.append(16 * jnp.where(ok, order_s[0, 3 * y + 1] >> 4, y))
        for half in range(2):
            rows = flipped(x[8 * half:8 * half + 8])
            for s in range(SEGS):
                raw[pl.ds(pl.multiple_of(elems[s] + 8 * half, 8), 8), :] = rows[s]

    @pl.when(ok)
    def _():
        def body(t, carry):
            x = [plane(u_in, q, t) for q in range(16)]
            for base, arrived in ((0, left), (12, right)):
                c = edge_values(arrived, im_ref, base, t, rate)
                for j in range(4):
                    x[base + j] = x[base + j] - c[j]
            leave(t, x)
            return carry

        lax.fori_loop(0, STEPS, body, 0, unroll=2)

    @pl.when(jnp.logical_not(ok))
    def _():
        v_ref[...] = w_in[...]
        general_receive(v_ref, left, right, recv_any, recv_s)
        v_ref[...] = u_in[...] - rate * (v_ref[...] * im_ref[...])

        def body(t, carry):
            leave(t, [plane(v_ref, q, t) for q in range(16)])
            return carry

        lax.fori_loop(0, STEPS, body, 0)

    store = pltpu.make_async_copy(raw, out, sem)
    store.start()
    store.wait()


VM = pl.BlockSpec(memory_space=pltpu.VMEM)
SM = pl.BlockSpec(memory_space=pltpu.SMEM)
HB = pl.BlockSpec(memory_space=pltpu.HBM)
FIELD = jax.ShapeDtypeStruct((ROWS, COLS), jnp.float32)
MESSAGE = jax.ShapeDtypeStruct((EDGE, COLS), jnp.float32)
TABLE = jax.ShapeDtypeStruct((ELEMS, COLS), jnp.float32)
SCRATCH = pltpu.VMEM((ROWS, COLS), jnp.float32)
TABLE_V = pltpu.VMEM((ELEMS, COLS), jnp.float32)
PARTNER_S = pltpu.SMEM((3, ROWS), jnp.int32)
SEND_S = pltpu.SMEM((2, EDGE), jnp.int32)
RECV_S = pltpu.SMEM((4, EDGE), jnp.int32)
WORK = 24 * ROWS * COLS
SIZE = 4 * ROWS * COLS


def call(kernel, ins, specs, shapes, outs, scratch, flops, moved, name):
    ins = [pltpu.with_memory_space_constraint(a, pltpu.HBM) if spec is HB else a for a, spec in zip(ins, specs)]
    return pl.pallas_call(
        kernel,
        out_shape=shapes,
        in_specs=specs,
        out_specs=outs,
        scratch_shapes=scratch,
        compiler_params=pltpu.CompilerParams(vmem_limit_bytes=VMEM_LIMIT),
        cost_estimate=pl.CostEstimate(flops=flops, bytes_accessed=moved, transcendentals=0),
        name=name,
    )(*ins)


def swap(behind, ahead):
    size = lax.axis_size("elem")
    left = lax.ppermute(ahead, "elem", [(i, (i + 1) % size) for i in range(size)])
    right = lax.ppermute(behind, "elem", [(i, (i - 1) % size) for i in range(size)])
    return left, right


def shards(prognostic, metric, inv_mass, viscosity, partner, send_rows, recv_rows):
    visc = viscosity.reshape(1, COLS)
    u, s, mx, my, order, behind, ahead, flag = call(
        first_kernel,
        (prognostic, metric, send_rows, recv_rows, partner),
        [HB] * 5,
        [FIELD, FIELD, FIELD, FIELD, TABLE, MESSAGE, MESSAGE, jax.ShapeDtypeStruct((1,), jnp.int32)],
        [VM] * 7 + [SM],
        [SCRATCH, SCRATCH, TABLE_V, pltpu.VMEM((2, ROWS), jnp.float32), pltpu.VMEM((2, EDGE), jnp.int32),
         pltpu.VMEM((4, EDGE), jnp.int32), pltpu.VMEM((3, ROWS), jnp.int32), SEND_S, PARTNER_S, pltpu.SemaphoreType.DMA((6,))],
        2 * WORK, 8 * SIZE, "first",
    )
    left, right = swap(behind, ahead)
    im, kx, w = call(
        prepare_kernel,
        (flag, s, mx, my, order, inv_mass.reshape(ROWS // 128, 128)),
        [SM, VM, VM, VM, VM, VM],
        [FIELD, jax.ShapeDtypeStruct((12 * ELEMS, COLS), jnp.float32), FIELD],
        [VM] * 3, [TABLE_V], WORK, 6 * SIZE, "prepare",
    )
    for step in range(2 * SUBCYCLES - 1):
        updates = step % 2 == 1
        g, behind, ahead = call(
            lambda *refs, updates=updates: edge_kernel(updates, *refs),
            (flag, w, left, right, mx, my, im, kx, u, visc, partner, send_rows, recv_rows),
            [SM] + [VM] * 9 + [HB] * 3, [FIELD, MESSAGE, MESSAGE], [VM] * 3,
            [SCRATCH, PARTNER_S, SEND_S, RECV_S], WORK // 3, 2 * SIZE, "edges",
        )
        came = (left, right)
        left, right = swap(behind, ahead)
        kind = 1 if updates else 2 if step == 2 * SUBCYCLES - 2 else 0
        u, w = call(
            lambda *refs, kind=kind: inner_kernel(kind, *refs),
            (flag, w, g, *came, mx, my, im, u, visc, recv_rows),
            [SM] + [VM] * 9 + [HB], [FIELD, FIELD], [VM] * 2,
            [SCRATCH, RECV_S], WORK * 2, 8 * SIZE, "inner",
        )
    return call(
        last_kernel,
        (flag, send_rows, w, left, right, im, u, visc, recv_rows),
        [SM, SM] + [VM] * 6 + [HB], FIELD, HB,
        [SCRATCH, SCRATCH, RECV_S, pltpu.SemaphoreType.DMA], WORK // 8, 4 * SIZE, "last",
    )


def solution(mesh):
    placed = (
        P("elem", None),
        P(None, "elem"),
        P("elem"),
        P(),
        P(None, "elem"),
        P("elem", None),
        P("elem", None),
    )
    return jax.shard_map(
        shards, mesh=mesh, in_specs=placed, out_specs=P("elem", None), check_vma=False
    )
```

```python
import functools
import math

import jax
import jax.numpy as jnp
import numpy as np
from jax import lax
from jax.experimental import pallas as pl
from jax.experimental.pallas import tpu as pltpu
from jax.sharding import PartitionSpec as P

SUBCYCLES = 2
ELEMS = 256
ROWS = 16 * ELEMS
COLS = 128
EDGE = 3 * ELEMS
SEGS = 8
STEPS = ELEMS // SEGS
NONE = ROWS
VMEM_LIMIT = 12 * 2**20


def node_tables():
    root = 1.0 / math.sqrt(5.0)
    points = [-1.0, -root, root, 1.0]
    weights = np.array([1.0, 5.0, 5.0, 1.0]) / 6.0
    products = []
    for first in range(4):
        value = 1.0
        for other in range(4):
            if other != first:
                value = value * (points[first] - points[other])
        products.append(value)
    table = []
    for first in range(4):
        line = []
        for other in range(4):
            if other == first:
                total = 0.0
                for third in range(4):
                    if third != first:
                        total = total + 1.0 / (points[first] - points[third])
                line.append(total)
            else:
                line.append(products[first] / (products[other] * (points[first] - points[other])))
        table.append(line)
    return (np.array(table), weights)


D, WEIGHTS = node_tables()


def gradient(v):
    o0, o1 = v[0] - v[3], v[1] - v[2]
    h = (v[0] + v[3]) - (v[1] + v[2])
    q0 = float(0.5 * (D[0, 0] + D[0, 3])) * h
    q1 = float(0.5 * (D[1, 0] + D[1, 3])) * h
    s0 = float(0.5 * (D[0, 0] - D[0, 3])) * o0 + float(0.5 * (D[0, 1] - D[0, 2])) * o1
    s1 = float(0.5 * (D[1, 0] - D[1, 3])) * o0 + float(0.5 * (D[1, 1] - D[1, 2])) * o1
    return [s0 + q0, s1 + q1, s1 - q1, s0 - q0]


def divergence(f):
    g0, g1 = f[0] - f[3], f[1] - f[2]
    t0, t1 = f[0] + f[3], f[1] + f[2]
    z = float(0.5 * (D[0, 0] + D[0, 3])) * g0 + float(0.5 * (D[1, 0] + D[1, 3])) * g1
    r0 = float(0.5 * (D[0, 0] - D[0, 3])) * t0 + float(0.5 * (D[1, 0] - D[1, 3])) * t1
    r1 = float(0.5 * (D[0, 1] - D[0, 2])) * t0 + float(0.5 * (D[1, 1] - D[1, 2])) * t1
    return [z + r0, r1 - z, -z - r1, z - r0]


def weak(x, mx, my):
    out = [None] * 16
    for j in range(4):
        g = gradient([x[4 * i + j] for i in range(4)])
        f = divergence([mx(4 * i + j) * g[i] for i in range(4)])
        for i in range(4):
            out[4 * i + j] = f[i]
    for i in range(4):
        g = gradient([x[4 * i + j] for j in range(4)])
        f = divergence([my(4 * i + j) * g[j] for j in range(4)])
        for j in range(4):
            out[4 * i + j] = out[4 * i + j] + f[j]
    return out


def plane(ref, q, t):
    return ref[pl.ds(pl.multiple_of(q * ELEMS + t * SEGS, SEGS), SEGS), :]


def set_plane(ref, q, t, value):
    ref[pl.ds(pl.multiple_of(q * ELEMS + t * SEGS, SEGS), SEGS), :] = value


def following(ref, q, t):
    last = t == STEPS - 1
    value = plane(ref, q, jnp.where(last, 0, t + 1))
    return jnp.where(last, pltpu.roll(value, SEGS - 1, 0), value)


def place_of(y):
    return lax.rem(y, STEPS) * SEGS + lax.div(y, STEPS)


def state_row(r):
    return lax.rem(r, 16) * ELEMS + place_of(lax.div(r, 16))


def wire_row(m):
    return lax.rem(m, 3) * ELEMS + place_of(lax.div(m, 3))


def one(ref, row):
    return ref[pl.ds(row, 1), :]


def ring_sums(s_ref):
    for i in range(4):
        for t in range(STEPS):
            upper = plane(s_ref, 4 * i, (t + 1) % STEPS)
            if t == STEPS - 1:
                upper = first
                lower = plane(s_ref, 4 * i + 3, t)
                total = lower + pltpu.roll(upper, SEGS - 1, 0)
                set_plane(s_ref, 4 * i + 3, t, total)
                set_plane(s_ref, 4 * i, 0, pltpu.roll(total, 1, 0))
            else:
                if t == 0:
                    first = plane(s_ref, 4 * i, 0)
                total = plane(s_ref, 4 * i + 3, t) + upper
                set_plane(s_ref, 4 * i + 3, t, total)
                set_plane(s_ref, 4 * i, t + 1, total)


def edge_messages(s_ref, behind_ref, ahead_ref):
    behind_ref[...] = s_ref[0:EDGE, :]
    ahead_ref[...] = s_ref[12 * ELEMS:15 * ELEMS, :]


def general_sums(v_ref, s_ref, partner_any, partner_s):
    pltpu.sync_copy(partner_any, partner_s)

    def body(r, carry):
        total = one(v_ref, state_row(r))
        for k in range(3):
            other = partner_s[k, r]
            found = one(v_ref, state_row(jnp.minimum(other, ROWS - 1)))
            total = total + jnp.where(other < NONE, found, 0.0)
        s_ref[pl.ds(state_row(r), 1), :] = total
        return carry

    lax.fori_loop(0, ROWS, body, 0)


def general_messages(s_ref, behind_ref, ahead_ref, send_any, send_s):
    pltpu.sync_copy(send_any, send_s)

    def body(m, carry):
        ahead_ref[pl.ds(wire_row(m), 1), :] = one(s_ref, state_row(send_s[0, m]))
        behind_ref[pl.ds(wire_row(m), 1), :] = one(s_ref, state_row(send_s[1, m]))
        return carry

    lax.fori_loop(0, EDGE, body, 0)


def general_receive(total_ref, left_ref, right_ref, recv_any, recv_s):
    pltpu.sync_copy(recv_any, recv_s)

    def body(m, carry):
        for k, arrived in ((0, left_ref), (1, right_ref)):
            for c in range(2):
                target = recv_s[2 * k + c, m]

                @pl.when(target < NONE)
                def _():
                    row = pl.ds(state_row(target), 1)
                    total_ref[row, :] = total_ref[row, :] + one(arrived, wire_row(m))
        return carry

    lax.fori_loop(0, EDGE, body, 0)


def iota(shape, axis):
    return lax.broadcasted_iota(jnp.int32, shape, axis)


def flipped(v):
    sub = iota((SEGS, COLS), 0)
    for b in (1, 2, 4):
        low = (sub & b) == 0
        out = list(v)
        for i in range(8):
            if i & b == 0:
                out[i] = jnp.where(low, v[i], pltpu.roll(v[i + b], b, 0))
                out[i + b] = jnp.where(low, pltpu.roll(v[i], 8 - b, 0), v[i + b])
        v = out
    return v


def tile(ref, row):
    return ref[pl.ds(pl.multiple_of(row, 8), 8), :]


def lanes_total(bad):
    ones = jnp.where(bad, 1.0, 0.0)
    if ones.shape[0] > 1:
        ones = jnp.sum(ones, axis=0, keepdims=True)
    total = ones[:, 0:128]
    for c in range(1, ones.shape[1] // 128):
        total = total + ones[:, 128 * c:128 * c + 128]
    return total


def pieces(row):
    high = row.astype(jnp.bfloat16).astype(jnp.float32)
    rest = row - high
    middle = rest.astype(jnp.bfloat16).astype(jnp.float32)
    return [high, middle, rest - middle]


def element_table(groups):
    own = (iota((16, 256), 1) >> 4) == iota((16, 256), 0)
    lane = iota((256, 128), 1)
    point = iota((256, 128), 0) & 15
    table = None
    for g, chunks in enumerate(groups):
        rows = [jnp.where(own, jnp.broadcast_to(c, (16, 256)), 0.0) for c in chunks]
        spread = jnp.concatenate(rows, axis=0).astype(jnp.bfloat16)
        chosen = (lane == point + 16 * g).astype(jnp.float32).astype(jnp.bfloat16)
        part = jnp.dot(spread, chosen, preferred_element_type=jnp.float32)
        table = part if table is None else table + part
    return table


def in_order(order, table):
    hot = (iota((ELEMS, ELEMS), 1).astype(jnp.float32) == order).astype(jnp.float32).astype(jnp.bfloat16)
    return jnp.dot(hot, table.astype(jnp.bfloat16), preferred_element_type=jnp.float32)


def first_kernel(prog, metric_h, send_h, recv_h, partner_h,
                 u_ref, s_ref, mx_ref, my_ref, order_ref, behind_ref, ahead_ref, pair_ref, flag_ref,
                 raw, v_ref, table, metric, send_v, recv_v, partner_v, send_s, partner_s, sems):
    loads = [pltpu.make_async_copy(a, b, sems.at[k]) for k, (a, b) in enumerate(
        ((send_h, send_v), (metric_h, metric), (partner_h, partner_v), (recv_h, recv_v), (send_h, send_s), (prog, raw)))]
    for load in loads:
        load.start()
    loads[0].wait()

    send = send_v[...]
    order_row = send[0:1, :] >> 4
    place = iota((ELEMS, 1), 0)
    ring = (place & 7) * STEPS + (place >> 3)
    picked = iota((ELEMS, EDGE), 1) == 3 * ring + 1
    order = jnp.sum(jnp.where(picked, order_row.astype(jnp.float32), 0.0), axis=1, keepdims=True)
    hot = (iota((ELEMS, ELEMS), 1).astype(jnp.float32) == order).astype(jnp.float32)
    seen = jnp.sum(hot, axis=0, keepdims=True)
    bad = lanes_total(seen != 1.0)

    loads[1].wait()
    loads[2].wait()
    partner = partner_v[...]
    least = jnp.minimum(jnp.minimum(partner[0:1], partner[1:2]), partner[2:3])
    bad = bad + lanes_total(partner[0:1] + partner[1:2] + partner[2:3] - least != 2 * NONE)
    both = [pieces(metric[k:k + 1, :]) for k in range(2)]
    rows = [both[k][n] for n in range(3) for k in range(2)]
    rows += [(least >> 4).astype(jnp.float32), (least & 15).astype(jnp.float32)]
    raw_table = element_table([[row[:, 256 * c:256 * c + 256] for c in range(16)] for row in rows])
    ordered = in_order(order, raw_table)

    wide_order = jnp.broadcast_to(order, (ELEMS, 128))
    before = jnp.concatenate([pltpu.roll(wide_order[ELEMS - SEGS:, :], 1, 0), wide_order[:-SEGS, :]], axis=0)
    after = jnp.concatenate([wide_order[SEGS:, :], pltpu.roll(wide_order[:SEGS, :], SEGS - 1, 0)], axis=0)
    lane = iota((1, 128), 1)
    point_i = (lane >> 2) & 3
    point_j = lane & 3
    expect_a = jnp.where(point_j == 0, before, jnp.where(point_j == 3, after, float(ELEMS)))
    expect_b = jnp.where(point_j == 0, 4 * point_i + 3, jnp.where(point_j == 3, 4 * point_i, 0)).astype(jnp.float32)
    expect = jnp.where(lane < 112, expect_a, expect_b)
    bad = bad + lanes_total((lane >= 96) & (ordered != expect))

    loads[3].wait()
    m = iota((1, EDGE), 1)
    p = m - 3 * ((m * 43691) >> 17)
    wide = jnp.broadcast_to(order_row, (8, EDGE))
    up1 = pltpu.roll(wide, EDGE - 1, 1)[0:1]
    down1 = pltpu.roll(wide, 1, 1)[0:1]
    down2 = pltpu.roll(wide, 2, 1)[0:1]
    own = 16 * jnp.where(p == 0, up1, jnp.where(p == 1, order_row, down1)) + p
    other = jnp.where(p == 0, 16 * down2 + 3, NONE)
    recv = recv_v[...]
    for k, shift in ((0, 12), (1, 0)):
        named = send[k:k + 1, :] - shift
        bad = bad + lanes_total((named != own) & ((p != 0) | (named != other)))
        a, b = recv[2 * (1 - k):2 * (1 - k) + 1, :], recv[2 * (1 - k) + 1:2 * (1 - k) + 2, :]
        want = jnp.where(p == 0, other + shift, NONE)
        bad = bad + lanes_total((jnp.minimum(a, b) != jnp.minimum(own + shift, want))
                                | (jnp.maximum(a, b) != jnp.maximum(own + shift, want)))
    ok = jnp.sum(bad) == 0.0
    odd = lax.rem(lax.axis_index("elem"), 2)
    flag_ref[...] = jnp.where(iota((8, 128), 0) == 0, jnp.where(ok, 1, 0), odd)

    weights = jnp.where((point_i == 0) | (point_i == 3), -1.0, -5.0) * jnp.where((point_j == 0) | (point_j == 3), 1.0, 5.0)
    weights = weights * (1.0 / 36.0)

    def set_table(ordered):
        table[...] = weights * (ordered + pltpu.roll(ordered, 96, 1) + pltpu.roll(ordered, 64, 1))

    set_table(ordered)
    order_ref[...] = wide_order

    @pl.when(jnp.logical_not(ok))
    def _():
        order_ref[...] = jnp.broadcast_to(ring.astype(jnp.float32), (ELEMS, 128))
        set_table(in_order(ring.astype(jnp.float32), raw_table))

    loads[4].wait()
    loads[5].wait()

    def body(t, carry):
        elems = []
        for s in range(SEGS):
            y = STEPS * s + t
            elems.append(16 * jnp.where(ok, send_s[0, 3 * y + 1] >> 4, y))
        x = flipped([tile(raw, e) for e in elems]) + flipped([tile(raw, e + 8) for e in elems])
        row = tile(table, t * SEGS)
        mx, my = [], []
        for q in range(16):
            set_plane(u_ref, q, t, x[q])
            mx.append(jnp.broadcast_to(row[:, q:q + 1], (SEGS, COLS)))
            my.append(jnp.broadcast_to(row[:, 16 + q:17 + q], (SEGS, COLS)))
            set_plane(mx_ref, q, t, mx[q])
            set_plane(my_ref, q, t, my[q])
        out = weak(x, lambda q: mx[q], lambda q: my[q])
        for q in range(16):
            set_plane(s_ref, q, t, out[q])
        return carry

    lax.fori_loop(0, STEPS, body, 0, unroll=2)

    @pl.when(ok)
    def _():
        ring_sums(s_ref)
        edge_messages(s_ref, behind_ref, ahead_ref)

    @pl.when(jnp.logical_not(ok))
    def _():
        v_ref[...] = s_ref[...]
        general_sums(v_ref, s_ref, partner_h, partner_s)
        general_messages(s_ref, behind_ref, ahead_ref, send_h, send_s)

    @pl.when(odd == 1)
    def _():
        pair_ref[...] = behind_ref[...]

    @pl.when(odd == 0)
    def _():
        pair_ref[...] = ahead_ref[...]


def edge_values(arrived, im_ref, base, t, scale):
    values = [plane(arrived, j, t) for j in range(3)] + [following(arrived, 0, t)]
    values = [values[j] * plane(im_ref, base + j, t) for j in range(4)]
    return values if scale is None else [scale * v for v in values]


def edge_gradient(left, right):
    h, o = left + right, left - right
    q0, q1 = float(0.5 * (D[0, 0] + D[0, 3])) * h, float(0.5 * (D[1, 0] + D[1, 3])) * h
    s0, s1 = float(0.5 * (D[0, 0] - D[0, 3])) * o, float(0.5 * (D[1, 0] - D[1, 3])) * o
    return [s0 + q0, s1 + q1, s1 - q1, s0 - q0]


def along_edge(c, my_ref, base, t):
    g = gradient(c)
    return divergence([plane(my_ref, base + j, t) * g[j] for j in range(4)])


def prepare_kernel(flag, s_in, mx_ref, my_ref, order, inv_mass, im_ref, kx_ref, w_ref, table):
    mass = inv_mass[...]
    mass = [jnp.concatenate([mass[2 * c:2 * c + 1, :], mass[2 * c + 1:2 * c + 2, :]], axis=1) for c in range(16)]
    split = [pieces(c) for c in mass]
    ordered = in_order(order[:, 0:1], element_table([[c[n] for c in split] for n in range(3)]))
    table[...] = ordered + pltpu.roll(ordered, 112, 1) + pltpu.roll(ordered, 96, 1)
    ok = flag[0, 0] == 1

    def body(t, carry):
        row = tile(table, t * SEGS)
        x = []
        for q in range(16):
            im = jnp.broadcast_to(row[:, q:q + 1], (SEGS, COLS))
            set_plane(im_ref, q, t, im)
            x.append(im * plane(s_in, q, t))
        mx = [plane(mx_ref, q, t) for q in range(16)]
        for j in range(4):
            for n, (a, b) in enumerate(((0, 0), (0, 3), (3, 3))):
                total = None
                for k in range(4):
                    term = float(D[k, a] * D[k, b]) * mx[4 * k + j]
                    total = term if total is None else total + term
                set_plane(kx_ref, 4 * n + j, t, total)
        out = weak(x, lambda q: mx[q], lambda q: plane(my_ref, q, t))
        for q in range(16):
            set_plane(w_ref, q, t, out[q])
        return carry

    lax.fori_loop(0, STEPS, body, 0, unroll=2)

    @pl.when(jnp.logical_not(ok))
    def _():
        w_ref[...] = s_in[...]


def edge_kernel(updates, odd, flag, seen, w_ref, chain, pair, mx_ref, my_ref, im_ref, kx_ref, u_in, visc, partner_any, send_any, recv_any, *rest):
    pair_ref, g_out, chain_ref, v_ref, g_ref, partner_s, send_s, recv_s = rest[-8:]
    ok = (flag[0, 0] == 1) & (flag[1, 0] == odd)
    left, right = (pair, chain) if odd else (chain, pair)
    behind_ref, ahead_ref = (pair_ref, chain_ref) if odd else (chain_ref, pair_ref)

    @pl.when(ok)
    def _():
        scale = -visc[...] if updates else None

        def body(t, carry):
            cl = edge_values(left, im_ref, 0, t, scale)
            cr = edge_values(right, im_ref, 12, t, scale)
            tail = []
            for base, c, out, k0, k1, before in ((0, cl, behind_ref, 0, 4, carry[0]), (12, cr, ahead_ref, 4, 8, carry[1])):
                f = along_edge(c, my_ref, base, t)
                for j in range(4):
                    f[j] = f[j] + plane(w_ref, base + j, t) + plane(kx_ref, k0 + j, t) * cl[j] + plane(kx_ref, k1 + j, t) * cr[j]
                set_plane(out, 0, t, f[0] + before)
                set_plane(out, 1, t, f[1])
                set_plane(out, 2, t, f[2])
                tail.append(f[3])
            return tuple(tail)

        zero = jnp.zeros((SEGS, COLS), jnp.float32)
        tail = lax.fori_loop(0, STEPS, body, (zero, zero), unroll=4)
        for out, last in zip((behind_ref, ahead_ref), tail):
            out[0:SEGS, :] = out[0:SEGS, :] + pltpu.roll(last, 1, 0)

    @pl.when((flag[0, 0] == 0) & (flag[1, 0] == odd))
    def _():
        v_ref[...] = w_ref[...]
        general_receive(v_ref, left, right, recv_any, recv_s)

        def body(t, carry):
            x = [plane(v_ref, q, t) * plane(im_ref, q, t) for q in range(16)]
            if updates:
                x = [plane(u_in, q, t) - visc[...] * x[q] for q in range(16)]
            out = weak(x, lambda q: plane(mx_ref, q, t), lambda q: plane(my_ref, q, t))
            for q in range(16):
                set_plane(v_ref, q, t, out[q])
            return carry

        lax.fori_loop(0, STEPS, body, 0)
        general_sums(v_ref, g_ref, partner_any, partner_s)
        pltpu.sync_copy(g_ref, g_out)
        general_messages(g_ref, behind_ref, ahead_ref, send_any, send_s)


def inner_kernel(kind, flag, w_in, g_in, forward, backward, pair, mx_ref, my_ref, im_ref, u_in, visc, recv_any, u_ref, w_ref, s_ref, recv_s):
    ok = flag[0, 0] == 1
    rate = visc[...]

    @pl.when(ok)
    def _():
        scale = -rate if kind == 1 else None

        def complete(left, right, t, carry):
            cl = edge_values(left, im_ref, 0, t, scale)
            cr = edge_values(right, im_ref, 12, t, scale)
            lines = [along_edge(cl, my_ref, 0, t), along_edge(cr, my_ref, 12, t)]
            for j in range(4):
                g = edge_gradient(cl[j], cr[j])
                f = divergence([plane(mx_ref, 4 * i + j, t) * g[i] for i in range(4)])
                f[0] = f[0] + lines[0][j]
                f[3] = f[3] + lines[1][j]
                for i in range(4):
                    set_plane(s_ref, 4 * i + j, t, plane(w_in, 4 * i + j, t) + f[i])
            if kind == 1:
                for j in range(4):
                    set_plane(u_ref, j, t, plane(u_in, j, t) + cl[j])
                    set_plane(u_ref, 12 + j, t, plane(u_in, 12 + j, t) + cr[j])
                for q in range(4, 12):
                    set_plane(u_ref, q, t, plane(u_in, q, t))
            return carry

        for odd, left, right in ((0, forward, pair), (1, pair, backward)):
            @pl.when(flag[1, 0] == odd)
            def _():
                lax.fori_loop(0, STEPS, functools.partial(complete, left, right), 0, unroll=2)

        ring_sums(s_ref)

        def onward(t, carry):
            x = [plane(s_ref, q, t) * plane(im_ref, q, t) for q in range(16)]
            if kind != 1:
                x = [plane(u_in, q, t) - rate * x[q] for q in range(16)]
                for q in range(16):
                    set_plane(u_ref, q, t, x[q])
            if kind != 2:
                out = weak(x, lambda q: plane(mx_ref, q, t), lambda q: plane(my_ref, q, t))
                for q in range(16):
                    set_plane(w_ref, q, t, out[q])
            return carry

        lax.fori_loop(0, STEPS, onward, 0, unroll=2)

    @pl.when(jnp.logical_not(ok))
    def _():
        pltpu.sync_copy(g_in, w_ref)
        if kind == 1:
            s_ref[...] = w_in[...]
            for odd, left, right in ((0, forward, pair), (1, pair, backward)):
                @pl.when(flag[1, 0] == odd)
                def _():
                    general_receive(s_ref, left, right, recv_any, recv_s)

            u_ref[...] = u_in[...] - rate * (s_ref[...] * im_ref[...])
        else:
            u_ref[...] = u_in[...]


def last_kernel(flag, seen, order_s, w_in, forward, backward, pair, im_ref, u_in, visc, recv_any, out, raw, v_ref, recv_s, sem):
    ok = flag[0, 0] == 1
    rate = visc[...]

    def leave(t, x):
        elems = []
        for s in range(SEGS):
            y = STEPS * s + t
            elems.append(16 * jnp.where(ok, order_s[0, 3 * y + 1] >> 4, y))
        for half in range(2):
            rows = flipped(x[8 * half:8 * half + 8])
            for s in range(SEGS):
                raw[pl.ds(pl.multiple_of(elems[s] + 8 * half, 8), 8), :] = rows[s]

    @pl.when(ok)
    def _():
        def body(left, right, t, carry):
            x = [plane(u_in, q, t) for q in range(16)]
            for base, arrived in ((0, left), (12, right)):
                c = edge_values(arrived, im_ref, base, t, rate)
                for j in range(4):
                    x[base + j] = x[base + j] - c[j]
            leave(t, x)
            return carry

        for odd, left, right in ((0, forward, pair), (1, pair, backward)):
            @pl.when(flag[1, 0] == odd)
            def _():
                lax.fori_loop(0, STEPS, functools.partial(body, left, right), 0, unroll=2)

    @pl.when(jnp.logical_not(ok))
    def _():
        v_ref[...] = w_in[...]
        for odd, left, right in ((0, forward, pair), (1, pair, backward)):
            @pl.when(flag[1, 0] == odd)
            def _():
                general_receive(v_ref, left, right, recv_any, recv_s)

        v_ref[...] = u_in[...] - rate * (v_ref[...] * im_ref[...])

        def body(t, carry):
            leave(t, [plane(v_ref, q, t) for q in range(16)])
            return carry

        lax.fori_loop(0, STEPS, body, 0)

    store = pltpu.make_async_copy(raw, out, sem)
    store.start()
    store.wait()


VM = pl.BlockSpec(memory_space=pltpu.VMEM)
SM = pl.BlockSpec(memory_space=pltpu.SMEM)
HB = pl.BlockSpec(memory_space=pltpu.HBM)
FREE = pl.BlockSpec(memory_space=pl.ANY)
FIELD = jax.ShapeDtypeStruct((ROWS, COLS), jnp.float32)
HELD = pltpu.HBM((ROWS, COLS), jnp.float32)
WORD = jax.ShapeDtypeStruct((8, 128), jnp.int32)
MESSAGE = jax.ShapeDtypeStruct((EDGE, COLS), jnp.float32)
TABLE = jax.ShapeDtypeStruct((ELEMS, COLS), jnp.float32)
SCRATCH = pltpu.VMEM((ROWS, COLS), jnp.float32)
TABLE_V = pltpu.VMEM((ELEMS, COLS), jnp.float32)
PARTNER_S = pltpu.SMEM((3, ROWS), jnp.int32)
SEND_S = pltpu.SMEM((2, EDGE), jnp.int32)
RECV_S = pltpu.SMEM((4, EDGE), jnp.int32)
WORK = 24 * ROWS * COLS
SIZE = 4 * ROWS * COLS


def call(kernel, ins, specs, shapes, outs, scratch, flops, moved, name, aliases={}):
    ins = [pltpu.with_memory_space_constraint(a, pltpu.HBM) if spec is HB else a for a, spec in zip(ins, specs)]
    return pl.pallas_call(
        kernel,
        out_shape=shapes,
        in_specs=specs,
        out_specs=outs,
        scratch_shapes=scratch,
        input_output_aliases=aliases,
        compiler_params=pltpu.CompilerParams(vmem_limit_bytes=VMEM_LIMIT),
        cost_estimate=pl.CostEstimate(flops=1, bytes_accessed=1, transcendentals=0),
        name=name,
    )(*ins)


def moved(value, by):
    size = lax.axis_size("elem")
    return lax.ppermute(value, "elem", [(i, (i + by) % size) for i in range(size)])


def crossed(value):
    size = lax.axis_size("elem")
    return lax.ppermute(value, "elem", [(i, i + 1 - 2 * (i % 2)) for i in range(size)])


def seen_kernel(arrived, before, out):
    out[...] = jnp.zeros_like(out)


def shards(prognostic, metric, inv_mass, viscosity, partner, send_rows, recv_rows):
    visc = viscosity.reshape(1, COLS)
    u, s, mx, my, order, behind, ahead, pair, flag = call(
        first_kernel,
        (prognostic, metric, send_rows, recv_rows, partner),
        [HB] * 5,
        [FIELD, FIELD, FIELD, FIELD, TABLE, MESSAGE, MESSAGE, MESSAGE, WORD],
        [VM] * 9,
        [SCRATCH, SCRATCH, TABLE_V, pltpu.VMEM((2, ROWS), jnp.float32), pltpu.VMEM((2, EDGE), jnp.int32),
         pltpu.VMEM((4, EDGE), jnp.int32), pltpu.VMEM((3, ROWS), jnp.int32), SEND_S, PARTNER_S, pltpu.SemaphoreType.DMA((6,))],
        2 * WORK, 8 * SIZE, "first",
    )
    crossing = crossed(pair)
    forward = moved(ahead, 1)
    backward = moved(behind, -1)
    im, kx, w = call(
        prepare_kernel,
        (flag, s, mx, my, order, inv_mass.reshape(ROWS // 128, 128)),
        [VM] * 6,
        [FIELD, jax.ShapeDtypeStruct((12 * ELEMS, COLS), jnp.float32), FIELD],
        [VM] * 3, [TABLE_V], WORK, 6 * SIZE, "prepare",
    )
    for step in range(2 * SUBCYCLES - 1):
        updates = step % 2 == 1
        chained = ()
        came = (forward, backward, crossing)
        for odd in ((0, 1) if step % 2 == 0 else (1, 0)):
            seen = call(seen_kernel, (came[odd], chained[0] if chained else flag), [FREE, FREE], WORD, VM, [], 0, 0, "seen")
            pair, g, chain = call(
                functools.partial(edge_kernel, updates, odd),
                (flag, seen, w, came[odd], crossing, mx, my, im, kx, u, visc, partner, send_rows, recv_rows) + chained,
                [VM, FREE] + [VM] * 9 + [HB] * 3 + [FREE, HB][:len(chained)], [MESSAGE, HELD, MESSAGE], [VM, HB, VM],
                [SCRATCH, SCRATCH, PARTNER_S, SEND_S, RECV_S], WORK // 3, 2 * SIZE, "edges",
                {14: 0, 15: 1} if chained else {},
            )
            chained = (pair, g)
            if odd:
                forward = moved(chain, 1)
            else:
                backward = moved(chain, -1)
        crossing = crossed(pair)
        kind = 1 if updates else 2 if step == 2 * SUBCYCLES - 2 else 0
        u, w = call(
            functools.partial(inner_kernel, kind),
            (flag, w, g, *came, mx, my, im, u, visc, recv_rows),
            [VM, VM, HB] + [VM] * 8 + [HB], [FIELD, FIELD], [VM] * 2,
            [SCRATCH, RECV_S], WORK * 2, 8 * SIZE, "inner",
        )
    seen = call(seen_kernel, (backward, flag), [FREE, FREE], WORD, VM, [], 0, 0, "seen")
    return call(
        last_kernel,
        (flag, seen, send_rows, w, forward, backward, crossing, im, u, visc, recv_rows),
        [VM, FREE, SM] + [VM] * 7 + [HB], FIELD, HB,
        [SCRATCH, SCRATCH, RECV_S, pltpu.SemaphoreType.DMA], WORK // 8, 4 * SIZE, "last",
    )


def solution(mesh):
    placed = (
        P("elem", None),
        P(None, "elem"),
        P("elem"),
        P(),
        P(None, "elem"),
        P("elem", None),
        P("elem", None),
    )
    return jax.shard_map(
        shards, mesh=mesh, in_specs=placed, out_specs=P("elem", None), check_vma=False
    )
```

```python
import functools
import math

import jax
import jax.numpy as jnp
import numpy as np
from jax import lax
from jax.experimental import pallas as pl
from jax.experimental.pallas import tpu as pltpu
from jax.sharding import PartitionSpec as P

SUBCYCLES = 2
ELEMS = 256
ROWS = 16 * ELEMS
COLS = 128
EDGE = 3 * ELEMS
SEGS = 8
STEPS = ELEMS // SEGS
NONE = ROWS
VMEM_LIMIT = 12 * 2**20


def node_tables():
    root = 1.0 / math.sqrt(5.0)
    points = [-1.0, -root, root, 1.0]
    weights = np.array([1.0, 5.0, 5.0, 1.0]) / 6.0
    products = []
    for first in range(4):
        value = 1.0
        for other in range(4):
            if other != first:
                value = value * (points[first] - points[other])
        products.append(value)
    table = []
    for first in range(4):
        line = []
        for other in range(4):
            if other == first:
                total = 0.0
                for third in range(4):
                    if third != first:
                        total = total + 1.0 / (points[first] - points[third])
                line.append(total)
            else:
                line.append(products[first] / (products[other] * (points[first] - points[other])))
        table.append(line)
    return (np.array(table), weights)


D, WEIGHTS = node_tables()


def gradient(v):
    o0, o1 = v[0] - v[3], v[1] - v[2]
    h = (v[0] + v[3]) - (v[1] + v[2])
    q0 = float(0.5 * (D[0, 0] + D[0, 3])) * h
    q1 = float(0.5 * (D[1, 0] + D[1, 3])) * h
    s0 = float(0.5 * (D[0, 0] - D[0, 3])) * o0 + float(0.5 * (D[0, 1] - D[0, 2])) * o1
    s1 = float(0.5 * (D[1, 0] - D[1, 3])) * o0 + float(0.5 * (D[1, 1] - D[1, 2])) * o1
    return [s0 + q0, s1 + q1, s1 - q1, s0 - q0]


def divergence(f):
    g0, g1 = f[0] - f[3], f[1] - f[2]
    t0, t1 = f[0] + f[3], f[1] + f[2]
    z = float(0.5 * (D[0, 0] + D[0, 3])) * g0 + float(0.5 * (D[1, 0] + D[1, 3])) * g1
    r0 = float(0.5 * (D[0, 0] - D[0, 3])) * t0 + float(0.5 * (D[1, 0] - D[1, 3])) * t1
    r1 = float(0.5 * (D[0, 1] - D[0, 2])) * t0 + float(0.5 * (D[1, 1] - D[1, 2])) * t1
    return [z + r0, r1 - z, -z - r1, z - r0]


def weak(x, mx, my):
    out = [None] * 16
    for j in range(4):
        g = gradient([x[4 * i + j] for i in range(4)])
        f = divergence([mx(4 * i + j) * g[i] for i in range(4)])
        for i in range(4):
            out[4 * i + j] = f[i]
    for i in range(4):
        g = gradient([x[4 * i + j] for j in range(4)])
        f = divergence([my(4 * i + j) * g[j] for j in range(4)])
        for j in range(4):
            out[4 * i + j] = out[4 * i + j] + f[j]
    return out


def plane(ref, q, t):
    return ref[pl.ds(pl.multiple_of(q * ELEMS + t * SEGS, SEGS), SEGS), :]


def set_plane(ref, q, t, value):
    ref[pl.ds(pl.multiple_of(q * ELEMS + t * SEGS, SEGS), SEGS), :] = value


def following(ref, q, t):
    last = t == STEPS - 1
    value = plane(ref, q, jnp.where(last, 0, t + 1))
    return jnp.where(last, pltpu.roll(value, SEGS - 1, 0), value)


def place_of(y):
    return lax.rem(y, STEPS) * SEGS + lax.div(y, STEPS)


def state_row(r):
    return lax.rem(r, 16) * ELEMS + place_of(lax.div(r, 16))


def wire_row(m):
    return lax.rem(m, 3) * ELEMS + place_of(lax.div(m, 3))


def one(ref, row):
    return ref[pl.ds(row, 1), :]


def ring_sums(s_ref):
    for i in range(4):
        for t in range(STEPS):
            upper = plane(s_ref, 4 * i, (t + 1) % STEPS)
            if t == STEPS - 1:
                upper = first
                lower = plane(s_ref, 4 * i + 3, t)
                total = lower + pltpu.roll(upper, SEGS - 1, 0)
                set_plane(s_ref, 4 * i + 3, t, total)
                set_plane(s_ref, 4 * i, 0, pltpu.roll(total, 1, 0))
            else:
                if t == 0:
                    first = plane(s_ref, 4 * i, 0)
                total = plane(s_ref, 4 * i + 3, t) + upper
                set_plane(s_ref, 4 * i + 3, t, total)
                set_plane(s_ref, 4 * i, t + 1, total)


def edge_messages(s_ref, behind_ref, ahead_ref):
    behind_ref[...] = s_ref[0:EDGE, :]
    ahead_ref[...] = s_ref[12 * ELEMS:15 * ELEMS, :]


def general_sums(v_ref, s_ref, partner_any, partner_s):
    pltpu.sync_copy(partner_any, partner_s)

    def body(r, carry):
        total = one(v_ref, state_row(r))
        for k in range(3):
            other = partner_s[k, r]
            found = one(v_ref, state_row(jnp.minimum(other, ROWS - 1)))
            total = total + jnp.where(other < NONE, found, 0.0)
        s_ref[pl.ds(state_row(r), 1), :] = total
        return carry

    lax.fori_loop(0, ROWS, body, 0)


def general_messages(s_ref, behind_ref, ahead_ref, send_any, send_s):
    pltpu.sync_copy(send_any, send_s)

    def body(m, carry):
        ahead_ref[pl.ds(wire_row(m), 1), :] = one(s_ref, state_row(send_s[0, m]))
        behind_ref[pl.ds(wire_row(m), 1), :] = one(s_ref, state_row(send_s[1, m]))
        return carry

    lax.fori_loop(0, EDGE, body, 0)


def general_receive(total_ref, left_ref, right_ref, recv_any, recv_s):
    pltpu.sync_copy(recv_any, recv_s)

    def body(m, carry):
        for k, arrived in ((0, left_ref), (1, right_ref)):
            for c in range(2):
                target = recv_s[2 * k + c, m]

                @pl.when(target < NONE)
                def _():
                    row = pl.ds(state_row(target), 1)
                    total_ref[row, :] = total_ref[row, :] + one(arrived, wire_row(m))
        return carry

    lax.fori_loop(0, EDGE, body, 0)


def iota(shape, axis):
    return lax.broadcasted_iota(jnp.int32, shape, axis)


def flipped(v):
    sub = iota((SEGS, COLS), 0)
    for b in (1, 2, 4):
        low = (sub & b) == 0
        out = list(v)
        for i in range(8):
            if i & b == 0:
                out[i] = jnp.where(low, v[i], pltpu.roll(v[i + b], b, 0))
                out[i + b] = jnp.where(low, pltpu.roll(v[i], 8 - b, 0), v[i + b])
        v = out
    return v


def tile(ref, row):
    return ref[pl.ds(pl.multiple_of(row, 8), 8), :]


def lanes_total(bad):
    ones = jnp.where(bad, 1.0, 0.0)
    if ones.shape[0] > 1:
        ones = jnp.sum(ones, axis=0, keepdims=True)
    total = ones[:, 0:128]
    for c in range(1, ones.shape[1] // 128):
        total = total + ones[:, 128 * c:128 * c + 128]
    return total


def pieces(row):
    high = row.astype(jnp.bfloat16).astype(jnp.float32)
    rest = row - high
    middle = rest.astype(jnp.bfloat16).astype(jnp.float32)
    return [high, middle, rest - middle]


def element_table(groups):
    own = (iota((16, 256), 1) >> 4) == iota((16, 256), 0)
    lane = iota((256, 128), 1)
    point = iota((256, 128), 0) & 15
    table = None
    for g, chunks in enumerate(groups):
        rows = [jnp.where(own, jnp.broadcast_to(c, (16, 256)), 0.0) for c in chunks]
        spread = jnp.concatenate(rows, axis=0).astype(jnp.bfloat16)
        chosen = (lane == point + 16 * g).astype(jnp.float32).astype(jnp.bfloat16)
        part = jnp.dot(spread, chosen, preferred_element_type=jnp.float32)
        table = part if table is None else table + part
    return table


def in_order(order, table):
    hot = (iota((ELEMS, ELEMS), 1).astype(jnp.float32) == order).astype(jnp.float32).astype(jnp.bfloat16)
    return jnp.dot(hot, table.astype(jnp.bfloat16), preferred_element_type=jnp.float32)


def first_kernel(prog, metric_h, send_h, recv_h, partner_h,
                 u_ref, s_ref, mx_ref, my_ref, order_ref, behind_ref, ahead_ref, pair_ref, flag_ref,
                 raw, v_ref, table, metric, send_v, recv_v, partner_v, send_s, partner_s, sems):
    loads = [pltpu.make_async_copy(a, b, sems.at[k]) for k, (a, b) in enumerate(
        ((send_h, send_v), (metric_h, metric), (partner_h, partner_v), (recv_h, recv_v), (send_h, send_s), (prog, raw)))]
    for load in loads:
        load.start()
    loads[0].wait()

    send = send_v[...]
    order_row = send[0:1, :] >> 4
    place = iota((ELEMS, 1), 0)
    ring = (place & 7) * STEPS + (place >> 3)
    picked = iota((ELEMS, EDGE), 1) == 3 * ring + 1
    order = jnp.sum(jnp.where(picked, order_row.astype(jnp.float32), 0.0), axis=1, keepdims=True)
    hot = (iota((ELEMS, ELEMS), 1).astype(jnp.float32) == order).astype(jnp.float32)
    seen = jnp.sum(hot, axis=0, keepdims=True)
    bad = lanes_total(seen != 1.0)

    loads[1].wait()
    loads[2].wait()
    partner = partner_v[...]
    least = jnp.minimum(jnp.minimum(partner[0:1], partner[1:2]), partner[2:3])
    bad = bad + lanes_total(partner[0:1] + partner[1:2] + partner[2:3] - least != 2 * NONE)
    both = [pieces(metric[k:k + 1, :]) for k in range(2)]
    rows = [both[k][n] for n in range(3) for k in range(2)]
    rows += [(least >> 4).astype(jnp.float32), (least & 15).astype(jnp.float32)]
    raw_table = element_table([[row[:, 256 * c:256 * c + 256] for c in range(16)] for row in rows])
    ordered = in_order(order, raw_table)

    wide_order = jnp.broadcast_to(order, (ELEMS, 128))
    before = jnp.concatenate([pltpu.roll(wide_order[ELEMS - SEGS:, :], 1, 0), wide_order[:-SEGS, :]], axis=0)
    after = jnp.concatenate([wide_order[SEGS:, :], pltpu.roll(wide_order[:SEGS, :], SEGS - 1, 0)], axis=0)
    lane = iota((1, 128), 1)
    point_i = (lane >> 2) & 3
    point_j = lane & 3
    expect_a = jnp.where(point_j == 0, before, jnp.where(point_j == 3, after, float(ELEMS)))
    expect_b = jnp.where(point_j == 0, 4 * point_i + 3, jnp.where(point_j == 3, 4 * point_i, 0)).astype(jnp.float32)
    expect = jnp.where(lane < 112, expect_a, expect_b)
    bad = bad + lanes_total((lane >= 96) & (ordered != expect))

    loads[3].wait()
    m = iota((1, EDGE), 1)
    p = m - 3 * ((m * 43691) >> 17)
    wide = jnp.broadcast_to(order_row, (8, EDGE))
    up1 = pltpu.roll(wide, EDGE - 1, 1)[0:1]
    down1 = pltpu.roll(wide, 1, 1)[0:1]
    down2 = pltpu.roll(wide, 2, 1)[0:1]
    own = 16 * jnp.where(p == 0, up1, jnp.where(p == 1, order_row, down1)) + p
    other = jnp.where(p == 0, 16 * down2 + 3, NONE)
    recv = recv_v[...]
    for k, shift in ((0, 12), (1, 0)):
        named = send[k:k + 1, :] - shift
        bad = bad + lanes_total((named != own) & ((p != 0) | (named != other)))
        a, b = recv[2 * (1 - k):2 * (1 - k) + 1, :], recv[2 * (1 - k) + 1:2 * (1 - k) + 2, :]
        want = jnp.where(p == 0, other + shift, NONE)
        bad = bad + lanes_total((jnp.minimum(a, b) != jnp.minimum(own + shift, want))
                                | (jnp.maximum(a, b) != jnp.maximum(own + shift, want)))
    ok = jnp.sum(bad) == 0.0
    odd = lax.rem(lax.axis_index("elem"), 2)
    flag_ref[...] = jnp.where(iota((8, 128), 0) == 0, jnp.where(ok, 1, 0), odd)

    weights = jnp.where((point_i == 0) | (point_i == 3), -1.0, -5.0) * jnp.where((point_j == 0) | (point_j == 3), 1.0, 5.0)
    weights = weights * (1.0 / 36.0)

    def set_table(ordered):
        table[...] = weights * (ordered + pltpu.roll(ordered, 96, 1) + pltpu.roll(ordered, 64, 1))

    set_table(ordered)
    order_ref[...] = wide_order

    @pl.when(jnp.logical_not(ok))
    def _():
        order_ref[...] = jnp.broadcast_to(ring.astype(jnp.float32), (ELEMS, 128))
        set_table(in_order(ring.astype(jnp.float32), raw_table))

    loads[4].wait()
    loads[5].wait()

    def body(t, carry):
        elems = []
        for s in range(SEGS):
            y = STEPS * s + t
            elems.append(16 * jnp.where(ok, send_s[0, 3 * y + 1] >> 4, y))
        x = flipped([tile(raw, e) for e in elems]) + flipped([tile(raw, e + 8) for e in elems])
        row = tile(table, t * SEGS)
        mx, my = [], []
        for q in range(16):
            set_plane(u_ref, q, t, x[q])
            mx.append(jnp.broadcast_to(row[:, q:q + 1], (SEGS, COLS)))
            my.append(jnp.broadcast_to(row[:, 16 + q:17 + q], (SEGS, COLS)))
            set_plane(mx_ref, q, t, mx[q])
            set_plane(my_ref, q, t, my[q])
        out = weak(x, lambda q: mx[q], lambda q: my[q])
        for q in range(16):
            set_plane(s_ref, q, t, out[q])
        return carry

    lax.fori_loop(0, STEPS, body, 0, unroll=2)

    @pl.when(ok)
    def _():
        ring_sums(s_ref)
        edge_messages(s_ref, behind_ref, ahead_ref)

    @pl.when(jnp.logical_not(ok))
    def _():
        v_ref[...] = s_ref[...]
        general_sums(v_ref, s_ref, partner_h, partner_s)
        general_messages(s_ref, behind_ref, ahead_ref, send_h, send_s)

    @pl.when(odd == 1)
    def _():
        pair_ref[...] = behind_ref[...]

    @pl.when(odd == 0)
    def _():
        pair_ref[...] = ahead_ref[...]


def edge_values(arrived, im_ref, base, t, scale):
    values = [plane(arrived, j, t) for j in range(3)] + [following(arrived, 0, t)]
    values = [values[j] * plane(im_ref, base + j, t) for j in range(4)]
    return values if scale is None else [scale * v for v in values]


def edge_gradient(left, right):
    h, o = left + right, left - right
    q0, q1 = float(0.5 * (D[0, 0] + D[0, 3])) * h, float(0.5 * (D[1, 0] + D[1, 3])) * h
    s0, s1 = float(0.5 * (D[0, 0] - D[0, 3])) * o, float(0.5 * (D[1, 0] - D[1, 3])) * o
    return [s0 + q0, s1 + q1, s1 - q1, s0 - q0]


def along_edge(c, my_ref, base, t):
    g = gradient(c)
    return divergence([plane(my_ref, base + j, t) * g[j] for j in range(4)])


def prepare_kernel(flag, s_in, mx_ref, my_ref, order, inv_mass, im_ref, kx_ref, w_ref, table):
    mass = inv_mass[...]
    mass = [jnp.concatenate([mass[2 * c:2 * c + 1, :], mass[2 * c + 1:2 * c + 2, :]], axis=1) for c in range(16)]
    split = [pieces(c) for c in mass]
    ordered = in_order(order[:, 0:1], element_table([[c[n] for c in split] for n in range(3)]))
    table[...] = ordered + pltpu.roll(ordered, 112, 1) + pltpu.roll(ordered, 96, 1)
    ok = flag[0, 0] == 1

    def body(t, carry):
        row = tile(table, t * SEGS)
        x = []
        for q in range(16):
            im = jnp.broadcast_to(row[:, q:q + 1], (SEGS, COLS))
            set_plane(im_ref, q, t, im)
            x.append(im * plane(s_in, q, t))
        mx = [plane(mx_ref, q, t) for q in range(16)]
        for j in range(4):
            for n, (a, b) in enumerate(((0, 0), (0, 3), (3, 3))):
                total = None
                for k in range(4):
                    term = float(D[k, a] * D[k, b]) * mx[4 * k + j]
                    total = term if total is None else total + term
                set_plane(kx_ref, 4 * n + j, t, total)
        out = weak(x, lambda q: mx[q], lambda q: plane(my_ref, q, t))
        for q in range(16):
            set_plane(w_ref, q, t, out[q])
        return carry

    lax.fori_loop(0, STEPS, body, 0, unroll=2)

    @pl.when(jnp.logical_not(ok))
    def _():
        w_ref[...] = s_in[...]


def edge_kernel(updates, odd, flag, seen, w_ref, chain, pair, mx_ref, my_ref, im_ref, kx_ref, u_in, visc, partner_any, send_any, recv_any, *rest):
    pair_ref, g_out, chain_ref, v_ref, g_ref, partner_s, send_s, recv_s = rest[-8:]
    ok = (flag[0, 0] == 1) & (flag[1, 0] == odd)
    left, right = (pair, chain) if odd else (chain, pair)
    behind_ref, ahead_ref = (pair_ref, chain_ref) if odd else (chain_ref, pair_ref)

    @pl.when(ok)
    def _():
        scale = -visc[...] if updates else None

        def body(t, carry):
            cl = edge_values(left, im_ref, 0, t, scale)
            cr = edge_values(right, im_ref, 12, t, scale)
            tail = []
            for base, c, out, k0, k1, before in ((0, cl, behind_ref, 0, 4, carry[0]), (12, cr, ahead_ref, 4, 8, carry[1])):
                f = along_edge(c, my_ref, base, t)
                for j in range(4):
                    f[j] = f[j] + plane(w_ref, base + j, t) + plane(kx_ref, k0 + j, t) * cl[j] + plane(kx_ref, k1 + j, t) * cr[j]
                set_plane(out, 0, t, f[0] + before)
                set_plane(out, 1, t, f[1])
                set_plane(out, 2, t, f[2])
                tail.append(f[3])
            return tuple(tail)

        zero = jnp.zeros((SEGS, COLS), jnp.float32)
        tail = lax.fori_loop(0, STEPS, body, (zero, zero), unroll=4)
        for out, last in zip((behind_ref, ahead_ref), tail):
            out[0:SEGS, :] = out[0:SEGS, :] + pltpu.roll(last, 1, 0)

    @pl.when((flag[0, 0] == 0) & (flag[1, 0] == odd))
    def _():
        v_ref[...] = w_ref[...]
        general_receive(v_ref, left, right, recv_any, recv_s)

        def body(t, carry):
            x = [plane(v_ref, q, t) * plane(im_ref, q, t) for q in range(16)]
            if updates:
                x = [plane(u_in, q, t) - visc[...] * x[q] for q in range(16)]
            out = weak(x, lambda q: plane(mx_ref, q, t), lambda q: plane(my_ref, q, t))
            for q in range(16):
                set_plane(v_ref, q, t, out[q])
            return carry

        lax.fori_loop(0, STEPS, body, 0)
        general_sums(v_ref, g_ref, partner_any, partner_s)
        pltpu.sync_copy(g_ref, g_out)
        general_messages(g_ref, behind_ref, ahead_ref, send_any, send_s)


def inner_kernel(kind, flag, w_in, g_in, forward, backward, pair_even, pair_odd, mx_ref, my_ref, im_ref, u_in, visc, recv_any, u_ref, w_ref, s_ref, recv_s):
    ok = flag[0, 0] == 1
    rate = visc[...]

    @pl.when(ok)
    def _():
        scale = -rate if kind == 1 else None

        def complete(left, right, t, carry):
            cl = edge_values(left, im_ref, 0, t, scale)
            cr = edge_values(right, im_ref, 12, t, scale)
            lines = [along_edge(cl, my_ref, 0, t), along_edge(cr, my_ref, 12, t)]
            for j in range(4):
                g = edge_gradient(cl[j], cr[j])
                f = divergence([plane(mx_ref, 4 * i + j, t) * g[i] for i in range(4)])
                f[0] = f[0] + lines[0][j]
                f[3] = f[3] + lines[1][j]
                for i in range(4):
                    set_plane(s_ref, 4 * i + j, t, plane(w_in, 4 * i + j, t) + f[i])
            if kind == 1:
                for j in range(4):
                    set_plane(u_ref, j, t, plane(u_in, j, t) + cl[j])
                    set_plane(u_ref, 12 + j, t, plane(u_in, 12 + j, t) + cr[j])
                for q in range(4, 12):
                    set_plane(u_ref, q, t, plane(u_in, q, t))
            return carry

        for odd, left, right in ((0, forward, pair_even), (1, pair_odd, backward)):
            @pl.when(flag[1, 0] == odd)
            def _():
                lax.fori_loop(0, STEPS, functools.partial(complete, left, right), 0, unroll=2)

        ring_sums(s_ref)

        def onward(t, carry):
            x = [plane(s_ref, q, t) * plane(im_ref, q, t) for q in range(16)]
            if kind != 1:
                x = [plane(u_in, q, t) - rate * x[q] for q in range(16)]
                for q in range(16):
                    set_plane(u_ref, q, t, x[q])
            if kind != 2:
                out = weak(x, lambda q: plane(mx_ref, q, t), lambda q: plane(my_ref, q, t))
                for q in range(16):
                    set_plane(w_ref, q, t, out[q])
            return carry

        lax.fori_loop(0, STEPS, onward, 0, unroll=2)

    @pl.when(jnp.logical_not(ok))
    def _():
        pltpu.sync_copy(g_in, w_ref)
        if kind == 1:
            s_ref[...] = w_in[...]
            for odd, left, right in ((0, forward, pair_even), (1, pair_odd, backward)):
                @pl.when(flag[1, 0] == odd)
                def _():
                    general_receive(s_ref, left, right, recv_any, recv_s)

            u_ref[...] = u_in[...] - rate * (s_ref[...] * im_ref[...])
        else:
            u_ref[...] = u_in[...]


def last_kernel(flag, seen, order_s, w_in, forward, backward, pair_even, pair_odd, im_ref, u_in, visc, recv_any, out, raw, v_ref, recv_s, sem):
    ok = flag[0, 0] == 1
    rate = visc[...]

    def leave(t, x):
        elems = []
        for s in range(SEGS):
            y = STEPS * s + t
            elems.append(16 * jnp.where(ok, order_s[0, 3 * y + 1] >> 4, y))
        for half in range(2):
            rows = flipped(x[8 * half:8 * half + 8])
            for s in range(SEGS):
                raw[pl.ds(pl.multiple_of(elems[s] + 8 * half, 8), 8), :] = rows[s]

    @pl.when(ok)
    def _():
        def body(left, right, t, carry):
            x = [plane(u_in, q, t) for q in range(16)]
            for base, arrived in ((0, left), (12, right)):
                c = edge_values(arrived, im_ref, base, t, rate)
                for j in range(4):
                    x[base + j] = x[base + j] - c[j]
            leave(t, x)
            return carry

        for odd, left, right in ((0, forward, pair_even), (1, pair_odd, backward)):
            @pl.when(flag[1, 0] == odd)
            def _():
                lax.fori_loop(0, STEPS, functools.partial(body, left, right), 0, unroll=2)

    @pl.when(jnp.logical_not(ok))
    def _():
        v_ref[...] = w_in[...]
        for odd, left, right in ((0, forward, pair_even), (1, pair_odd, backward)):
            @pl.when(flag[1, 0] == odd)
            def _():
                general_receive(v_ref, left, right, recv_any, recv_s)

        v_ref[...] = u_in[...] - rate * (v_ref[...] * im_ref[...])

        def body(t, carry):
            leave(t, [plane(v_ref, q, t) for q in range(16)])
            return carry

        lax.fori_loop(0, STEPS, body, 0)

    store = pltpu.make_async_copy(raw, out, sem)
    store.start()
    store.wait()


VM = pl.BlockSpec(memory_space=pltpu.VMEM)
SM = pl.BlockSpec(memory_space=pltpu.SMEM)
HB = pl.BlockSpec(memory_space=pltpu.HBM)
FREE = pl.BlockSpec(memory_space=pl.ANY)
FIELD = jax.ShapeDtypeStruct((ROWS, COLS), jnp.float32)
HELD = pltpu.HBM((ROWS, COLS), jnp.float32)
WORD = jax.ShapeDtypeStruct((8, 128), jnp.int32)
MESSAGE = jax.ShapeDtypeStruct((EDGE, COLS), jnp.float32)
TABLE = jax.ShapeDtypeStruct((ELEMS, COLS), jnp.float32)
SCRATCH = pltpu.VMEM((ROWS, COLS), jnp.float32)
TABLE_V = pltpu.VMEM((ELEMS, COLS), jnp.float32)
PARTNER_S = pltpu.SMEM((3, ROWS), jnp.int32)
SEND_S = pltpu.SMEM((2, EDGE), jnp.int32)
RECV_S = pltpu.SMEM((4, EDGE), jnp.int32)
WORK = 24 * ROWS * COLS
SIZE = 4 * ROWS * COLS


def call(kernel, ins, specs, shapes, outs, scratch, flops, moved, name, aliases={}):
    ins = [pltpu.with_memory_space_constraint(a, pltpu.HBM) if spec is HB else a for a, spec in zip(ins, specs)]
    return pl.pallas_call(
        kernel,
        out_shape=shapes,
        in_specs=specs,
        out_specs=outs,
        scratch_shapes=scratch,
        input_output_aliases=aliases,
        compiler_params=pltpu.CompilerParams(vmem_limit_bytes=VMEM_LIMIT),
        cost_estimate=pl.CostEstimate(flops=1, bytes_accessed=1, transcendentals=0),
        name=name,
    )(*ins)


def moved(value, by):
    size = lax.axis_size("elem")
    return lax.ppermute(value, "elem", [(i, (i + by) % size) for i in range(size)])


def crossed(value):
    size = lax.axis_size("elem")
    return lax.ppermute(value, "elem", [(i, i + 1 - 2 * (i % 2)) for i in range(size)])


def seen_kernel(arrived, before, out):
    out[...] = jnp.zeros_like(out)


def shards(prognostic, metric, inv_mass, viscosity, partner, send_rows, recv_rows):
    visc = viscosity.reshape(1, COLS)
    u, s, mx, my, order, behind, ahead, pair, flag = call(
        first_kernel,
        (prognostic, metric, send_rows, recv_rows, partner),
        [HB] * 5,
        [FIELD, FIELD, FIELD, FIELD, TABLE, MESSAGE, MESSAGE, MESSAGE, WORD],
        [VM] * 9,
        [SCRATCH, SCRATCH, TABLE_V, pltpu.VMEM((2, ROWS), jnp.float32), pltpu.VMEM((2, EDGE), jnp.int32),
         pltpu.VMEM((4, EDGE), jnp.int32), pltpu.VMEM((3, ROWS), jnp.int32), SEND_S, PARTNER_S, pltpu.SemaphoreType.DMA((6,))],
        2 * WORK, 8 * SIZE, "first",
    )
    crossing = crossed(pair)
    forward = moved(ahead, 1)
    backward = moved(behind, -1)
    im, kx, w = call(
        prepare_kernel,
        (flag, s, mx, my, order, inv_mass.reshape(ROWS // 128, 128)),
        [VM] * 6,
        [FIELD, jax.ShapeDtypeStruct((12 * ELEMS, COLS), jnp.float32), FIELD],
        [VM] * 3, [TABLE_V], WORK, 6 * SIZE, "prepare",
    )
    came = [forward, backward]
    pairs = [crossing, crossing]
    for step in range(2 * SUBCYCLES - 1):
        updates = step % 2 == 1
        chained = ()
        before = flag
        arrived, crossings = list(came), list(pairs)
        for odd in ((0, 1) if step % 2 == 0 else (1, 0)):
            seen = call(seen_kernel, (arrived[odd], before), [FREE, FREE], WORD, VM, [], 0, 0, "seen")
            before, g, chain = call(
                functools.partial(edge_kernel, updates, odd),
                (flag, seen, w, arrived[odd], crossings[odd], mx, my, im, kx, u, visc, partner, send_rows, recv_rows) + chained,
                [VM, FREE] + [VM] * 9 + [HB] * 3 + [HB] * len(chained), [MESSAGE, HELD, MESSAGE], [VM, HB, VM],
                [SCRATCH, SCRATCH, PARTNER_S, SEND_S, RECV_S], WORK // 3, 2 * SIZE, "edges",
                {14: 1} if chained else {},
            )
            chained = (g,)
            came[1 - odd] = moved(chain, 1 if odd else -1)
            pairs[1 - odd] = crossed(before)
        kind = 1 if updates else 2 if step == 2 * SUBCYCLES - 2 else 0
        u, w = call(
            functools.partial(inner_kernel, kind),
            (flag, w, g, *arrived, *crossings, mx, my, im, u, visc, recv_rows),
            [VM, VM, HB] + [VM] * 9 + [HB], [FIELD, FIELD], [VM] * 2,
            [SCRATCH, RECV_S], WORK * 2, 8 * SIZE, "inner",
        )
    seen = call(seen_kernel, (came[1], flag), [FREE, FREE], WORD, VM, [], 0, 0, "seen")
    return call(
        last_kernel,
        (flag, seen, send_rows, w, *came, *pairs, im, u, visc, recv_rows),
        [VM, FREE, SM] + [VM] * 8 + [HB], FIELD, HB,
        [SCRATCH, SCRATCH, RECV_S, pltpu.SemaphoreType.DMA], WORK // 8, 4 * SIZE, "last",
    )


def solution(mesh):
    placed = (
        P("elem", None),
        P(None, "elem"),
        P("elem"),
        P(),
        P(None, "elem"),
        P("elem", None),
        P("elem", None),
    )
    return jax.shard_map(
        shards, mesh=mesh, in_specs=placed, out_specs=P("elem", None), check_vma=False
    )
```

```python
import functools
import math

import jax
import jax.numpy as jnp
import numpy as np
from jax import lax
from jax.experimental import pallas as pl
from jax.experimental.pallas import tpu as pltpu
from jax.sharding import PartitionSpec as P

SUBCYCLES = 2
ELEMS = 256
ROWS = 16 * ELEMS
COLS = 128
EDGE = 3 * ELEMS
SEGS = 8
STEPS = ELEMS // SEGS
NONE = ROWS
VMEM_LIMIT = 12 * 2**20


def node_tables():
    root = 1.0 / math.sqrt(5.0)
    points = [-1.0, -root, root, 1.0]
    weights = np.array([1.0, 5.0, 5.0, 1.0]) / 6.0
    products = []
    for first in range(4):
        value = 1.0
        for other in range(4):
            if other != first:
                value = value * (points[first] - points[other])
        products.append(value)
    table = []
    for first in range(4):
        line = []
        for other in range(4):
            if other == first:
                total = 0.0
                for third in range(4):
                    if third != first:
                        total = total + 1.0 / (points[first] - points[third])
                line.append(total)
            else:
                line.append(products[first] / (products[other] * (points[first] - points[other])))
        table.append(line)
    return (np.array(table), weights)


D, WEIGHTS = node_tables()


def gradient(v):
    o0, o1 = v[0] - v[3], v[1] - v[2]
    h = (v[0] + v[3]) - (v[1] + v[2])
    q0 = float(0.5 * (D[0, 0] + D[0, 3])) * h
    q1 = float(0.5 * (D[1, 0] + D[1, 3])) * h
    s0 = float(0.5 * (D[0, 0] - D[0, 3])) * o0 + float(0.5 * (D[0, 1] - D[0, 2])) * o1
    s1 = float(0.5 * (D[1, 0] - D[1, 3])) * o0 + float(0.5 * (D[1, 1] - D[1, 2])) * o1
    return [s0 + q0, s1 + q1, s1 - q1, s0 - q0]


def divergence(f):
    g0, g1 = f[0] - f[3], f[1] - f[2]
    t0, t1 = f[0] + f[3], f[1] + f[2]
    z = float(0.5 * (D[0, 0] + D[0, 3])) * g0 + float(0.5 * (D[1, 0] + D[1, 3])) * g1
    r0 = float(0.5 * (D[0, 0] - D[0, 3])) * t0 + float(0.5 * (D[1, 0] - D[1, 3])) * t1
    r1 = float(0.5 * (D[0, 1] - D[0, 2])) * t0 + float(0.5 * (D[1, 1] - D[1, 2])) * t1
    return [z + r0, r1 - z, -z - r1, z - r0]


def weak(x, mx, my):
    out = [None] * 16
    for j in range(4):
        g = gradient([x[4 * i + j] for i in range(4)])
        f = divergence([mx(4 * i + j) * g[i] for i in range(4)])
        for i in range(4):
            out[4 * i + j] = f[i]
    for i in range(4):
        g = gradient([x[4 * i + j] for j in range(4)])
        f = divergence([my(4 * i + j) * g[j] for j in range(4)])
        for j in range(4):
            out[4 * i + j] = out[4 * i + j] + f[j]
    return out


def plane(ref, q, t):
    return ref[pl.ds(pl.multiple_of(q * ELEMS + t * SEGS, SEGS), SEGS), :]


def set_plane(ref, q, t, value):
    ref[pl.ds(pl.multiple_of(q * ELEMS + t * SEGS, SEGS), SEGS), :] = value


def following(ref, q, t):
    last = t == STEPS - 1
    value = plane(ref, q, jnp.where(last, 0, t + 1))
    return jnp.where(last, pltpu.roll(value, SEGS - 1, 0), value)


def preceding(ref, q, t):
    first = t == 0
    value = plane(ref, q, jnp.where(first, STEPS - 1, t - 1))
    return jnp.where(first, pltpu.roll(value, 1, 0), value)


def place_of(y):
    return lax.rem(y, STEPS) * SEGS + lax.div(y, STEPS)


def state_row(r):
    return lax.rem(r, 16) * ELEMS + place_of(lax.div(r, 16))


def wire_row(m):
    return lax.rem(m, 3) * ELEMS + place_of(lax.div(m, 3))


def one(ref, row):
    return ref[pl.ds(row, 1), :]


def ring_sums(s_ref):
    for i in range(4):
        for t in range(STEPS):
            upper = plane(s_ref, 4 * i, (t + 1) % STEPS)
            if t == STEPS - 1:
                upper = first
                lower = plane(s_ref, 4 * i + 3, t)
                total = lower + pltpu.roll(upper, SEGS - 1, 0)
                set_plane(s_ref, 4 * i + 3, t, total)
                set_plane(s_ref, 4 * i, 0, pltpu.roll(total, 1, 0))
            else:
                if t == 0:
                    first = plane(s_ref, 4 * i, 0)
                total = plane(s_ref, 4 * i + 3, t) + upper
                set_plane(s_ref, 4 * i + 3, t, total)
                set_plane(s_ref, 4 * i, t + 1, total)


def general_sums(v_ref, s_ref, partner_any, partner_s):
    pltpu.sync_copy(partner_any, partner_s)

    def body(r, carry):
        total = one(v_ref, state_row(r))
        for k in range(3):
            other = partner_s[k, r]
            found = one(v_ref, state_row(jnp.minimum(other, ROWS - 1)))
            total = total + jnp.where(other < NONE, found, 0.0)
        s_ref[pl.ds(state_row(r), 1), :] = total
        return carry

    lax.fori_loop(0, ROWS, body, 0)


def general_messages(s_ref, behind_ref, ahead_ref, send_any, send_s):
    pltpu.sync_copy(send_any, send_s)

    def body(m, carry):
        ahead_ref[pl.ds(wire_row(m), 1), :] = one(s_ref, state_row(send_s[0, m]))
        behind_ref[pl.ds(wire_row(m), 1), :] = one(s_ref, state_row(send_s[1, m]))
        return carry

    lax.fori_loop(0, EDGE, body, 0)


def general_receive(total_ref, left_ref, right_ref, recv_any, recv_s):
    pltpu.sync_copy(recv_any, recv_s)

    def body(m, carry):
        for k, arrived in ((0, left_ref), (1, right_ref)):
            for c in range(2):
                target = recv_s[2 * k + c, m]

                @pl.when(target < NONE)
                def _():
                    row = pl.ds(state_row(target), 1)
                    total_ref[row, :] = total_ref[row, :] + one(arrived, wire_row(m))
        return carry

    lax.fori_loop(0, EDGE, body, 0)


def iota(shape, axis):
    return lax.broadcasted_iota(jnp.int32, shape, axis)


def flipped(v):
    sub = iota((SEGS, COLS), 0)
    for b in (1, 2, 4):
        low = (sub & b) == 0
        out = list(v)
        for i in range(8):
            if i & b == 0:
                out[i] = jnp.where(low, v[i], pltpu.roll(v[i + b], b, 0))
                out[i + b] = jnp.where(low, pltpu.roll(v[i], 8 - b, 0), v[i + b])
        v = out
    return v


def tile(ref, row):
    return ref[pl.ds(pl.multiple_of(row, 8), 8), :]


def lanes_total(bad):
    ones = jnp.where(bad, 1.0, 0.0)
    if ones.shape[0] > 1:
        ones = jnp.sum(ones, axis=0, keepdims=True)
    total = ones[:, 0:128]
    for c in range(1, ones.shape[1] // 128):
        total = total + ones[:, 128 * c:128 * c + 128]
    return total


def pieces(row):
    high = row.astype(jnp.bfloat16).astype(jnp.float32)
    rest = row - high
    middle = rest.astype(jnp.bfloat16).astype(jnp.float32)
    return [high, middle, rest - middle]


def element_table(groups):
    own = (iota((16, 256), 1) >> 4) == iota((16, 256), 0)
    lane = iota((256, 128), 1)
    point = iota((256, 128), 0) & 15
    table = None
    for g, chunks in enumerate(groups):
        rows = [jnp.where(own, jnp.broadcast_to(c, (16, 256)), 0.0) for c in chunks]
        spread = jnp.concatenate(rows, axis=0).astype(jnp.bfloat16)
        chosen = (lane == point + 16 * g).astype(jnp.float32).astype(jnp.bfloat16)
        part = jnp.dot(spread, chosen, preferred_element_type=jnp.float32)
        table = part if table is None else table + part
    return table


def in_order(order, table):
    hot = (iota((ELEMS, ELEMS), 1).astype(jnp.float32) == order).astype(jnp.float32).astype(jnp.bfloat16)
    return jnp.dot(hot, table.astype(jnp.bfloat16), preferred_element_type=jnp.float32)


def first_kernel(prog, metric_h, send_h, recv_h, partner_h,
                 u_ref, s_ref, mx_ref, my_ref, order_ref, behind_ref, ahead_ref, pair_ref, flag_ref,
                 raw, v_ref, table, metric, send_v, recv_v, partner_v, send_s, partner_s, sems):
    loads = [pltpu.make_async_copy(a, b, sems.at[k]) for k, (a, b) in enumerate(
        ((send_h, send_v), (metric_h, metric), (partner_h, partner_v), (recv_h, recv_v), (send_h, send_s), (prog, raw)))]
    for load in loads:
        load.start()
    loads[0].wait()

    send = send_v[...]
    order_row = send[0:1, :] >> 4
    place = iota((ELEMS, 1), 0)
    ring = (place & 7) * STEPS + (place >> 3)
    picked = iota((ELEMS, EDGE), 1) == 3 * ring + 1
    order = jnp.sum(jnp.where(picked, order_row.astype(jnp.float32), 0.0), axis=1, keepdims=True)
    hot = (iota((ELEMS, ELEMS), 1).astype(jnp.float32) == order).astype(jnp.float32)
    seen = jnp.sum(hot, axis=0, keepdims=True)
    bad = lanes_total(seen != 1.0)

    loads[1].wait()
    loads[2].wait()
    partner = partner_v[...]
    least = jnp.minimum(jnp.minimum(partner[0:1], partner[1:2]), partner[2:3])
    bad = bad + lanes_total(partner[0:1] + partner[1:2] + partner[2:3] - least != 2 * NONE)
    both = [pieces(metric[k:k + 1, :]) for k in range(2)]
    rows = [both[k][n] for n in range(3) for k in range(2)]
    rows += [(least >> 4).astype(jnp.float32), (least & 15).astype(jnp.float32)]
    raw_table = element_table([[row[:, 256 * c:256 * c + 256] for c in range(16)] for row in rows])
    ordered = in_order(order, raw_table)

    wide_order = jnp.broadcast_to(order, (ELEMS, 128))
    before = jnp.concatenate([pltpu.roll(wide_order[ELEMS - SEGS:, :], 1, 0), wide_order[:-SEGS, :]], axis=0)
    after = jnp.concatenate([wide_order[SEGS:, :], pltpu.roll(wide_order[:SEGS, :], SEGS - 1, 0)], axis=0)
    lane = iota((1, 128), 1)
    point_i = (lane >> 2) & 3
    point_j = lane & 3
    expect_a = jnp.where(point_j == 0, before, jnp.where(point_j == 3, after, float(ELEMS)))
    expect_b = jnp.where(point_j == 0, 4 * point_i + 3, jnp.where(point_j == 3, 4 * point_i, 0)).astype(jnp.float32)
    expect = jnp.where(lane < 112, expect_a, expect_b)
    bad = bad + lanes_total((lane >= 96) & (ordered != expect))

    loads[3].wait()
    m = iota((1, EDGE), 1)
    p = m - 3 * ((m * 43691) >> 17)
    wide = jnp.broadcast_to(order_row, (8, EDGE))
    up1 = pltpu.roll(wide, EDGE - 1, 1)[0:1]
    down1 = pltpu.roll(wide, 1, 1)[0:1]
    down2 = pltpu.roll(wide, 2, 1)[0:1]
    own = 16 * jnp.where(p == 0, up1, jnp.where(p == 1, order_row, down1)) + p
    other = jnp.where(p == 0, 16 * down2 + 3, NONE)
    recv = recv_v[...]
    for k, shift in ((0, 12), (1, 0)):
        named = send[k:k + 1, :] - shift
        bad = bad + lanes_total((named != own) & ((p != 0) | (named != other)))
        a, b = recv[2 * (1 - k):2 * (1 - k) + 1, :], recv[2 * (1 - k) + 1:2 * (1 - k) + 2, :]
        want = jnp.where(p == 0, other + shift, NONE)
        bad = bad + lanes_total((jnp.minimum(a, b) != jnp.minimum(own + shift, want))
                                | (jnp.maximum(a, b) != jnp.maximum(own + shift, want)))
    ok = jnp.sum(bad) == 0.0
    odd = lax.rem(lax.axis_index("elem"), 2)
    flag_ref[...] = jnp.where(iota((8, 128), 0) == 0, jnp.where(ok, 1, 0), odd)

    weights = jnp.where((point_i == 0) | (point_i == 3), -1.0, -5.0) * jnp.where((point_j == 0) | (point_j == 3), 1.0, 5.0)
    weights = weights * (1.0 / 36.0)

    def set_table(ordered):
        table[...] = weights * (ordered + pltpu.roll(ordered, 96, 1) + pltpu.roll(ordered, 64, 1))

    set_table(ordered)
    order_ref[...] = wide_order

    @pl.when(jnp.logical_not(ok))
    def _():
        order_ref[...] = jnp.broadcast_to(ring.astype(jnp.float32), (ELEMS, 128))
        set_table(in_order(ring.astype(jnp.float32), raw_table))

    loads[4].wait()
    loads[5].wait()

    def body(t, carry):
        elems = []
        for s in range(SEGS):
            y = STEPS * s + t
            elems.append(16 * jnp.where(ok, send_s[0, 3 * y + 1] >> 4, y))
        x = flipped([tile(raw, e) for e in elems]) + flipped([tile(raw, e + 8) for e in elems])
        row = tile(table, t * SEGS)
        mx, my = [], []
        for q in range(16):
            set_plane(u_ref, q, t, x[q])
            mx.append(jnp.broadcast_to(row[:, q:q + 1], (SEGS, COLS)))
            my.append(jnp.broadcast_to(row[:, 16 + q:17 + q], (SEGS, COLS)))
            set_plane(mx_ref, q, t, mx[q])
            set_plane(my_ref, q, t, my[q])
        out = weak(x, lambda q: mx[q], lambda q: my[q])
        for q in range(16):
            set_plane(s_ref, q, t, out[q])
        behind = [out[0] + carry[0], out[1], out[2]]
        ahead = [out[12] + carry[1], out[13], out[14]]
        for j in range(3):
            set_plane(behind_ref, j, t, behind[j])
            set_plane(ahead_ref, j, t, ahead[j])
            set_plane(pair_ref, j, t, jnp.where(odd == 1, behind[j], ahead[j]))
        return (out[3], out[15])

    zero = jnp.zeros((SEGS, COLS), jnp.float32)
    tail = [pltpu.roll(v, 1, 0) for v in lax.fori_loop(0, STEPS, body, (zero, zero), unroll=4)]
    for message, value in ((behind_ref, tail[0]), (ahead_ref, tail[1]), (pair_ref, jnp.where(odd == 1, tail[0], tail[1]))):
        message[0:SEGS, :] = message[0:SEGS, :] + value

    @pl.when(jnp.logical_not(ok))
    def _():
        v_ref[...] = s_ref[...]
        general_sums(v_ref, s_ref, partner_h, partner_s)
        general_messages(s_ref, behind_ref, ahead_ref, send_h, send_s)

        @pl.when(odd == 1)
        def _():
            pair_ref[...] = behind_ref[...]

        @pl.when(odd == 0)
        def _():
            pair_ref[...] = ahead_ref[...]


def edge_values(arrived, im_ref, base, t, scale):
    values = [plane(arrived, j, t) for j in range(3)] + [following(arrived, 0, t)]
    values = [values[j] * plane(im_ref, base + j, t) for j in range(4)]
    return values if scale is None else [scale * v for v in values]


def edge_gradient(left, right):
    h, o = left + right, left - right
    q0, q1 = float(0.5 * (D[0, 0] + D[0, 3])) * h, float(0.5 * (D[1, 0] + D[1, 3])) * h
    s0, s1 = float(0.5 * (D[0, 0] - D[0, 3])) * o, float(0.5 * (D[1, 0] - D[1, 3])) * o
    return [s0 + q0, s1 + q1, s1 - q1, s0 - q0]


def along_edge(c, my_ref, base, t):
    g = gradient(c)
    return divergence([plane(my_ref, base + j, t) * g[j] for j in range(4)])


def prepare_kernel(flag, s_in, mx_ref, my_ref, order, inv_mass, im_ref, kx_ref, w_ref, table):
    mass = inv_mass[...]
    mass = [jnp.concatenate([mass[2 * c:2 * c + 1, :], mass[2 * c + 1:2 * c + 2, :]], axis=1) for c in range(16)]
    split = [pieces(c) for c in mass]
    ordered = in_order(order[:, 0:1], element_table([[c[n] for c in split] for n in range(3)]))
    table[...] = ordered + pltpu.roll(ordered, 112, 1) + pltpu.roll(ordered, 96, 1)
    ok = flag[0, 0] == 1

    def body(t, carry):
        row = tile(table, t * SEGS)
        x = []
        for q in range(16):
            im = jnp.broadcast_to(row[:, q:q + 1], (SEGS, COLS))
            set_plane(im_ref, q, t, im)
            value = plane(s_in, q, t)
            if q % 4 == 0:
                value = value + preceding(s_in, q + 3, t)
            if q % 4 == 3:
                value = value + following(s_in, q - 3, t)
            x.append(im * value)
        mx = [plane(mx_ref, q, t) for q in range(16)]
        for j in range(4):
            for n, (a, b) in enumerate(((0, 0), (0, 3), (3, 3))):
                total = None
                for k in range(4):
                    term = float(D[k, a] * D[k, b]) * mx[4 * k + j]
                    total = term if total is None else total + term
                set_plane(kx_ref, 4 * n + j, t, total)
        out = weak(x, lambda q: mx[q], lambda q: plane(my_ref, q, t))
        for q in range(16):
            set_plane(w_ref, q, t, out[q])
        return carry

    lax.fori_loop(0, STEPS, body, 0, unroll=2)

    @pl.when(jnp.logical_not(ok))
    def _():
        w_ref[...] = s_in[...]


def edge_kernel(updates, odd, flag, seen, w_ref, chain, pair, mx_ref, my_ref, im_ref, kx_ref, u_in, visc, partner_any, send_any, recv_any, *rest):
    pair_ref, g_out, chain_ref, v_ref, g_ref, partner_s, send_s, recv_s = rest[-8:]
    ok = (flag[0, 0] == 1) & (flag[1, 0] == odd)
    left, right = (pair, chain) if odd else (chain, pair)
    behind_ref, ahead_ref = (pair_ref, chain_ref) if odd else (chain_ref, pair_ref)

    @pl.when(ok)
    def _():
        scale = -visc[...] if updates else None

        def body(t, carry):
            cl = edge_values(left, im_ref, 0, t, scale)
            cr = edge_values(right, im_ref, 12, t, scale)
            tail = []
            for base, c, out, k0, k1, before in ((0, cl, behind_ref, 0, 4, carry[0]), (12, cr, ahead_ref, 4, 8, carry[1])):
                f = along_edge(c, my_ref, base, t)
                for j in range(4):
                    f[j] = f[j] + plane(w_ref, base + j, t) + plane(kx_ref, k0 + j, t) * cl[j] + plane(kx_ref, k1 + j, t) * cr[j]
                set_plane(out, 0, t, f[0] + before)
                set_plane(out, 1, t, f[1])
                set_plane(out, 2, t, f[2])
                tail.append(f[3])
            return tuple(tail)

        zero = jnp.zeros((SEGS, COLS), jnp.float32)
        tail = lax.fori_loop(0, STEPS, body, (zero, zero), unroll=8)
        for out, last in zip((behind_ref, ahead_ref), tail):
            out[0:SEGS, :] = out[0:SEGS, :] + pltpu.roll(last, 1, 0)

    @pl.when((flag[0, 0] == 0) & (flag[1, 0] == odd))
    def _():
        v_ref[...] = w_ref[...]
        general_receive(v_ref, left, right, recv_any, recv_s)

        def body(t, carry):
            x = [plane(v_ref, q, t) * plane(im_ref, q, t) for q in range(16)]
            if updates:
                x = [plane(u_in, q, t) - visc[...] * x[q] for q in range(16)]
            out = weak(x, lambda q: plane(mx_ref, q, t), lambda q: plane(my_ref, q, t))
            for q in range(16):
                set_plane(v_ref, q, t, out[q])
            return carry

        lax.fori_loop(0, STEPS, body, 0)
        general_sums(v_ref, g_ref, partner_any, partner_s)
        pltpu.sync_copy(g_ref, g_out)
        general_messages(g_ref, behind_ref, ahead_ref, send_any, send_s)


def leave(order_s, ok, raw, t, x):
    elems = []
    for s in range(SEGS):
        y = STEPS * s + t
        elems.append(16 * jnp.where(ok, order_s[0, 3 * y + 1] >> 4, y))
    for half in range(2):
        rows = flipped(x[8 * half:8 * half + 8])
        for s in range(SEGS):
            raw[pl.ds(pl.multiple_of(elems[s] + 8 * half, 8), 8), :] = rows[s]


def inner_kernel(kind, flag, w_in, g_in, forward, backward, pair_even, pair_odd, mx_ref, my_ref, im_ref, u_in, visc, send_any, recv_any, u_ref, w_ref, s_ref, recv_s, order_s, sem):
    if kind == 2:
        load = pltpu.make_async_copy(send_any, order_s, sem)
        load.start()
    ok = flag[0, 0] == 1
    rate = visc[...]
    if kind == 2:
        load.wait()

    @pl.when(ok)
    def _():
        scale = -rate if kind == 1 else None

        def complete(left, right, t, carry):
            cl = edge_values(left, im_ref, 0, t, scale)
            cr = edge_values(right, im_ref, 12, t, scale)
            lines = [along_edge(cl, my_ref, 0, t), along_edge(cr, my_ref, 12, t)]
            for j in range(4):
                g = edge_gradient(cl[j], cr[j])
                f = divergence([plane(mx_ref, 4 * i + j, t) * g[i] for i in range(4)])
                f[0] = f[0] + lines[0][j]
                f[3] = f[3] + lines[1][j]
                for i in range(4):
                    set_plane(s_ref, 4 * i + j, t, plane(w_in, 4 * i + j, t) + f[i])
            if kind == 1:
                for j in range(4):
                    set_plane(u_ref, j, t, plane(u_in, j, t) + cl[j])
                    set_plane(u_ref, 12 + j, t, plane(u_in, 12 + j, t) + cr[j])
                for q in range(4, 12):
                    set_plane(u_ref, q, t, plane(u_in, q, t))
            return carry

        for odd, left, right in ((0, forward, pair_even), (1, pair_odd, backward)):
            @pl.when(flag[1, 0] == odd)
            def _():
                lax.fori_loop(0, STEPS, functools.partial(complete, left, right), 0, unroll=2)

        ring_sums(s_ref)

        def onward(t, carry):
            x = [plane(s_ref, q, t) * plane(im_ref, q, t) for q in range(16)]
            if kind != 1:
                x = [plane(u_in, q, t) - rate * x[q] for q in range(16)]
            if kind == 0:
                for q in range(16):
                    set_plane(u_ref, q, t, x[q])
            if kind == 2:
                leave(order_s, ok, u_ref, t, x)
            if kind != 2:
                out = weak(x, lambda q: plane(mx_ref, q, t), lambda q: plane(my_ref, q, t))
                for q in range(16):
                    set_plane(w_ref, q, t, out[q])
            return carry

        lax.fori_loop(0, STEPS, onward, 0, unroll=2)

    @pl.when(jnp.logical_not(ok))
    def _():
        pltpu.sync_copy(g_in, w_ref)
        if kind == 1:
            s_ref[...] = w_in[...]
            for odd, left, right in ((0, forward, pair_even), (1, pair_odd, backward)):
                @pl.when(flag[1, 0] == odd)
                def _():
                    general_receive(s_ref, left, right, recv_any, recv_s)

            u_ref[...] = u_in[...] - rate * (s_ref[...] * im_ref[...])
        else:
            u_ref[...] = u_in[...]


def last_kernel(flag, seen, send_any, w_in, forward, backward, pair_even, pair_odd, im_ref, u_in, visc, recv_any, out,
                raw, v_ref, order_s, recv_s, sems):
    load = pltpu.make_async_copy(send_any, order_s, sems.at[0])
    load.start()
    ok = flag[0, 0] == 1
    rate = visc[...]

    @pl.when(ok)
    def _():
        def edges(left, right, t, carry):
            rows = flipped(edge_values(left, im_ref, 0, t, rate) + edge_values(right, im_ref, 12, t, rate))
            for s in range(SEGS):
                v_ref[pl.ds(pl.multiple_of((t * SEGS + s) * 8, 8), 8), :] = rows[s]
            return carry

        for odd, left, right in ((0, forward, pair_even), (1, pair_odd, backward)):
            @pl.when(flag[1, 0] == odd)
            def _():
                lax.fori_loop(0, STEPS, functools.partial(edges, left, right), 0, unroll=4)

    load.wait()

    @pl.when(ok)
    def _():
        low = iota((8, COLS), 0) < 4

        def body(t, carry):
            for s in range(SEGS):
                e = 16 * (order_s[0, 3 * (STEPS * s + t) + 1] >> 4)
                change = tile(v_ref, (t * SEGS + s) * 8)
                for half, mine in ((0, low), (8, jnp.logical_not(low))):
                    raw[pl.ds(pl.multiple_of(e + half, 8), 8), :] = tile(u_in, e + half) - jnp.where(mine, change, 0.0)
            return carry

        lax.fori_loop(0, STEPS, body, 0, unroll=4)

    @pl.when(jnp.logical_not(ok))
    def _():
        v_ref[...] = w_in[...]
        for odd, left, right in ((0, forward, pair_even), (1, pair_odd, backward)):
            @pl.when(flag[1, 0] == odd)
            def _():
                general_receive(v_ref, left, right, recv_any, recv_s)

        v_ref[...] = u_in[...] - rate * (v_ref[...] * im_ref[...])

        def body(t, carry):
            leave(order_s, ok, raw, t, [plane(v_ref, q, t) for q in range(16)])
            return carry

        lax.fori_loop(0, STEPS, body, 0)

    store = pltpu.make_async_copy(raw, out, sems.at[1])
    store.start()
    store.wait()


VM = pl.BlockSpec(memory_space=pltpu.VMEM)
SM = pl.BlockSpec(memory_space=pltpu.SMEM)
HB = pl.BlockSpec(memory_space=pltpu.HBM)
FREE = pl.BlockSpec(memory_space=pl.ANY)
FIELD = jax.ShapeDtypeStruct((ROWS, COLS), jnp.float32)
HELD = pltpu.HBM((ROWS, COLS), jnp.float32)
WORD = jax.ShapeDtypeStruct((8, 128), jnp.int32)
MESSAGE = jax.ShapeDtypeStruct((EDGE, COLS), jnp.float32)
TABLE = jax.ShapeDtypeStruct((ELEMS, COLS), jnp.float32)
SCRATCH = pltpu.VMEM((ROWS, COLS), jnp.float32)
TABLE_V = pltpu.VMEM((ELEMS, COLS), jnp.float32)
PARTNER_S = pltpu.SMEM((3, ROWS), jnp.int32)
SEND_S = pltpu.SMEM((2, EDGE), jnp.int32)
RECV_S = pltpu.SMEM((4, EDGE), jnp.int32)
WORK = 24 * ROWS * COLS
SIZE = 4 * ROWS * COLS


def call(kernel, ins, specs, shapes, outs, scratch, flops, moved, name, aliases={}):
    ins = [pltpu.with_memory_space_constraint(a, pltpu.HBM) if spec is HB else a for a, spec in zip(ins, specs)]
    return pl.pallas_call(
        kernel,
        out_shape=shapes,
        in_specs=specs,
        out_specs=outs,
        scratch_shapes=scratch,
        input_output_aliases=aliases,
        compiler_params=pltpu.CompilerParams(vmem_limit_bytes=VMEM_LIMIT),
        cost_estimate=pl.CostEstimate(flops=1, bytes_accessed=1, transcendentals=0),
        name=name,
    )(*ins)


def moved(value, by):
    size = lax.axis_size("elem")
    return lax.ppermute(value, "elem", [(i, (i + by) % size) for i in range(size)])


def crossed(value):
    size = lax.axis_size("elem")
    return lax.ppermute(value, "elem", [(i, i + 1 - 2 * (i % 2)) for i in range(size)])


def seen_kernel(arrived, before, out):
    out[...] = jnp.zeros_like(out)


def shards(prognostic, metric, inv_mass, viscosity, partner, send_rows, recv_rows):
    visc = viscosity.reshape(1, COLS)
    u, s, mx, my, order, behind, ahead, pair, flag = call(
        first_kernel,
        (prognostic, metric, send_rows, recv_rows, partner),
        [HB] * 5,
        [FIELD, FIELD, FIELD, FIELD, TABLE, MESSAGE, MESSAGE, MESSAGE, WORD],
        [VM] * 9,
        [SCRATCH, SCRATCH, TABLE_V, pltpu.VMEM((2, ROWS), jnp.float32), pltpu.VMEM((2, EDGE), jnp.int32),
         pltpu.VMEM((4, EDGE), jnp.int32), pltpu.VMEM((3, ROWS), jnp.int32), SEND_S, PARTNER_S, pltpu.SemaphoreType.DMA((6,))],
        2 * WORK, 8 * SIZE, "first",
    )
    crossing = crossed(pair)
    forward = moved(ahead, 1)
    backward = moved(behind, -1)
    im, kx, w = call(
        prepare_kernel,
        (flag, s, mx, my, order, inv_mass.reshape(ROWS // 128, 128)),
        [VM] * 6,
        [FIELD, jax.ShapeDtypeStruct((12 * ELEMS, COLS), jnp.float32), FIELD],
        [VM] * 3, [TABLE_V], WORK, 6 * SIZE, "prepare",
    )
    came = [forward, backward]
    pairs = [crossing, crossing]
    for step in range(2 * SUBCYCLES - 1):
        updates = step % 2 == 1
        chained = ()
        before = flag
        arrived, crossings = list(came), list(pairs)
        for odd in ((0, 1) if step % 2 == 0 else (1, 0)):
            seen = call(seen_kernel, (arrived[odd], before), [FREE, FREE], WORD, VM, [], 0, 0, "seen")
            before, g, chain = call(
                functools.partial(edge_kernel, updates, odd),
                (flag, seen, w, arrived[odd], crossings[odd], mx, my, im, kx, u, visc, partner, send_rows, recv_rows) + chained,
                [VM, FREE] + [VM] * 9 + [HB] * 3 + [HB] * len(chained), [MESSAGE, HELD, MESSAGE], [VM, HB, VM],
                [SCRATCH, SCRATCH, PARTNER_S, SEND_S, RECV_S], WORK // 3, 2 * SIZE, "edges",
                {14: 1} if chained else {},
            )
            chained = (g,)
            came[1 - odd] = moved(chain, 1 if odd else -1)
            pairs[1 - odd] = crossed(before)
        kind = 1 if updates else 2 if step == 2 * SUBCYCLES - 2 else 0
        u, w = call(
            functools.partial(inner_kernel, kind),
            (flag, w, g, *arrived, *crossings, mx, my, im, u, visc, send_rows, recv_rows),
            [VM, VM, HB] + [VM] * 9 + [HB] * 2, [FIELD, FIELD], [VM] * 2,
            [SCRATCH, RECV_S, SEND_S, pltpu.SemaphoreType.DMA], WORK * 2, 8 * SIZE, "inner",
        )
    seen = call(seen_kernel, (came[1], flag), [FREE, FREE], WORD, VM, [], 0, 0, "seen")
    return call(
        last_kernel,
        (flag, seen, send_rows, w, *came, *pairs, im, u, visc, recv_rows),
        [VM, FREE, HB] + [VM] * 8 + [HB], FIELD, HB,
        [SCRATCH, SCRATCH, SEND_S, RECV_S, pltpu.SemaphoreType.DMA((2,))], WORK // 8, 4 * SIZE, "last",
    )


def solution(mesh):
    placed = (
        P("elem", None),
        P(None, "elem"),
        P("elem"),
        P(),
        P(None, "elem"),
        P("elem", None),
        P("elem", None),
    )
    return jax.shard_map(
        shards, mesh=mesh, in_specs=placed, out_specs=P("elem", None), check_vma=False
    )
```

```python
import functools
import math

import jax
import jax.numpy as jnp
import numpy as np
from jax import lax
from jax.experimental import pallas as pl
from jax.experimental.pallas import tpu as pltpu
from jax.sharding import PartitionSpec as P

SUBCYCLES = 2
ELEMS = 256
ROWS = 16 * ELEMS
COLS = 128
EDGE = 3 * ELEMS
SEGS = 8
STEPS = ELEMS // SEGS
NONE = ROWS
VMEM_LIMIT = 12 * 2**20


def node_tables():
    root = 1.0 / math.sqrt(5.0)
    points = [-1.0, -root, root, 1.0]
    weights = np.array([1.0, 5.0, 5.0, 1.0]) / 6.0
    products = []
    for first in range(4):
        value = 1.0
        for other in range(4):
            if other != first:
                value = value * (points[first] - points[other])
        products.append(value)
    table = []
    for first in range(4):
        line = []
        for other in range(4):
            if other == first:
                total = 0.0
                for third in range(4):
                    if third != first:
                        total = total + 1.0 / (points[first] - points[third])
                line.append(total)
            else:
                line.append(products[first] / (products[other] * (points[first] - points[other])))
        table.append(line)
    return (np.array(table), weights)


D, WEIGHTS = node_tables()


def gradient(v):
    o0, o1 = v[0] - v[3], v[1] - v[2]
    h = (v[0] + v[3]) - (v[1] + v[2])
    q0 = float(0.5 * (D[0, 0] + D[0, 3])) * h
    q1 = float(0.5 * (D[1, 0] + D[1, 3])) * h
    s0 = float(0.5 * (D[0, 0] - D[0, 3])) * o0 + float(0.5 * (D[0, 1] - D[0, 2])) * o1
    s1 = float(0.5 * (D[1, 0] - D[1, 3])) * o0 + float(0.5 * (D[1, 1] - D[1, 2])) * o1
    return [s0 + q0, s1 + q1, s1 - q1, s0 - q0]


def divergence(f):
    g0, g1 = f[0] - f[3], f[1] - f[2]
    t0, t1 = f[0] + f[3], f[1] + f[2]
    z = float(0.5 * (D[0, 0] + D[0, 3])) * g0 + float(0.5 * (D[1, 0] + D[1, 3])) * g1
    r0 = float(0.5 * (D[0, 0] - D[0, 3])) * t0 + float(0.5 * (D[1, 0] - D[1, 3])) * t1
    r1 = float(0.5 * (D[0, 1] - D[0, 2])) * t0 + float(0.5 * (D[1, 1] - D[1, 2])) * t1
    return [z + r0, r1 - z, -z - r1, z - r0]


def weak(x, mx, my):
    out = [None] * 16
    for j in range(4):
        g = gradient([x[4 * i + j] for i in range(4)])
        f = divergence([mx(4 * i + j) * g[i] for i in range(4)])
        for i in range(4):
            out[4 * i + j] = f[i]
    for i in range(4):
        g = gradient([x[4 * i + j] for j in range(4)])
        f = divergence([my(4 * i + j) * g[j] for j in range(4)])
        for j in range(4):
            out[4 * i + j] = out[4 * i + j] + f[j]
    return out


def plane(ref, q, t):
    return ref[pl.ds(pl.multiple_of(q * ELEMS + t * SEGS, SEGS), SEGS), :]


def set_plane(ref, q, t, value):
    ref[pl.ds(pl.multiple_of(q * ELEMS + t * SEGS, SEGS), SEGS), :] = value


def following(ref, q, t):
    last = t == STEPS - 1
    value = plane(ref, q, jnp.where(last, 0, t + 1))
    return jnp.where(last, pltpu.roll(value, SEGS - 1, 0), value)


def preceding(ref, q, t):
    first = t == 0
    value = plane(ref, q, jnp.where(first, STEPS - 1, t - 1))
    return jnp.where(first, pltpu.roll(value, 1, 0), value)


def place_of(y):
    return lax.rem(y, STEPS) * SEGS + lax.div(y, STEPS)


def state_row(r):
    return lax.rem(r, 16) * ELEMS + place_of(lax.div(r, 16))


def wire_row(m):
    return lax.rem(m, 3) * ELEMS + place_of(lax.div(m, 3))


def one(ref, row):
    return ref[pl.ds(row, 1), :]


def ring_sums(s_ref):
    for i in range(4):
        for t in range(STEPS):
            upper = plane(s_ref, 4 * i, (t + 1) % STEPS)
            if t == STEPS - 1:
                upper = first
                lower = plane(s_ref, 4 * i + 3, t)
                total = lower + pltpu.roll(upper, SEGS - 1, 0)
                set_plane(s_ref, 4 * i + 3, t, total)
                set_plane(s_ref, 4 * i, 0, pltpu.roll(total, 1, 0))
            else:
                if t == 0:
                    first = plane(s_ref, 4 * i, 0)
                total = plane(s_ref, 4 * i + 3, t) + upper
                set_plane(s_ref, 4 * i + 3, t, total)
                set_plane(s_ref, 4 * i, t + 1, total)


def general_sums(v_ref, s_ref, partner_any, partner_s):
    pltpu.sync_copy(partner_any, partner_s)

    def body(r, carry):
        total = one(v_ref, state_row(r))
        for k in range(3):
            other = partner_s[k, r]
            found = one(v_ref, state_row(jnp.minimum(other, ROWS - 1)))
            total = total + jnp.where(other < NONE, found, 0.0)
        s_ref[pl.ds(state_row(r), 1), :] = total
        return carry

    lax.fori_loop(0, ROWS, body, 0)


def general_messages(s_ref, behind_ref, ahead_ref, send_any, send_s):
    pltpu.sync_copy(send_any, send_s)

    def body(m, carry):
        ahead_ref[pl.ds(wire_row(m), 1), :] = one(s_ref, state_row(send_s[0, m]))
        behind_ref[pl.ds(wire_row(m), 1), :] = one(s_ref, state_row(send_s[1, m]))
        return carry

    lax.fori_loop(0, EDGE, body, 0)


def general_receive(total_ref, left_ref, right_ref, recv_any, recv_s):
    pltpu.sync_copy(recv_any, recv_s)

    def body(m, carry):
        for k, arrived in ((0, left_ref), (1, right_ref)):
            for c in range(2):
                target = recv_s[2 * k + c, m]

                @pl.when(target < NONE)
                def _():
                    row = pl.ds(state_row(target), 1)
                    total_ref[row, :] = total_ref[row, :] + one(arrived, wire_row(m))
        return carry

    lax.fori_loop(0, EDGE, body, 0)


def iota(shape, axis):
    return lax.broadcasted_iota(jnp.int32, shape, axis)


def flipped(v):
    sub = iota((SEGS, COLS), 0)
    for b in (1, 2, 4):
        low = (sub & b) == 0
        out = list(v)
        for i in range(8):
            if i & b == 0:
                out[i] = jnp.where(low, v[i], pltpu.roll(v[i + b], b, 0))
                out[i + b] = jnp.where(low, pltpu.roll(v[i], 8 - b, 0), v[i + b])
        v = out
    return v


def tile(ref, row):
    return ref[pl.ds(pl.multiple_of(row, 8), 8), :]


def lanes_total(bad):
    ones = jnp.where(bad, 1.0, 0.0)
    if ones.shape[0] > 1:
        ones = jnp.sum(ones, axis=0, keepdims=True)
    total = ones[:, 0:128]
    for c in range(1, ones.shape[1] // 128):
        total = total + ones[:, 128 * c:128 * c + 128]
    return total


def pieces(row):
    high = row.astype(jnp.bfloat16).astype(jnp.float32)
    rest = row - high
    middle = rest.astype(jnp.bfloat16).astype(jnp.float32)
    return [high, middle, rest - middle]


def element_table(groups):
    own = (iota((16, 256), 1) >> 4) == iota((16, 256), 0)
    lane = iota((256, 128), 1)
    point = iota((256, 128), 0) & 15
    table = None
    for g, chunks in enumerate(groups):
        rows = [jnp.where(own, jnp.broadcast_to(c, (16, 256)), 0.0) for c in chunks]
        spread = jnp.concatenate(rows, axis=0).astype(jnp.bfloat16)
        chosen = (lane == point + 16 * g).astype(jnp.float32).astype(jnp.bfloat16)
        part = jnp.dot(spread, chosen, preferred_element_type=jnp.float32)
        table = part if table is None else table + part
    return table


def in_order(order, table):
    hot = (iota((ELEMS, ELEMS), 1).astype(jnp.float32) == order).astype(jnp.float32).astype(jnp.bfloat16)
    return jnp.dot(hot, table.astype(jnp.bfloat16), preferred_element_type=jnp.float32)


def first_kernel(prog, metric_h, send_h, recv_h, partner_h,
                 u_ref, s_ref, mx_ref, my_ref, order_ref, behind_ref, ahead_ref, pair_ref, flag_ref,
                 raw, v_ref, table, metric, send_v, recv_v, partner_v, send_s, partner_s, sems):
    loads = [pltpu.make_async_copy(a, b, sems.at[k]) for k, (a, b) in enumerate(
        ((send_h, send_v), (metric_h, metric), (partner_h, partner_v), (recv_h, recv_v), (send_h, send_s), (prog, raw)))]
    for load in loads:
        load.start()
    loads[0].wait()

    send = send_v[...]
    order_row = send[0:1, :] >> 4
    place = iota((ELEMS, 1), 0)
    ring = (place & 7) * STEPS + (place >> 3)
    picked = iota((ELEMS, EDGE), 1) == 3 * ring + 1
    order = jnp.sum(jnp.where(picked, order_row.astype(jnp.float32), 0.0), axis=1, keepdims=True)
    hot = (iota((ELEMS, ELEMS), 1).astype(jnp.float32) == order).astype(jnp.float32)
    seen = jnp.sum(hot, axis=0, keepdims=True)
    bad = lanes_total(seen != 1.0)

    loads[1].wait()
    loads[2].wait()
    partner = partner_v[...]
    least = jnp.minimum(jnp.minimum(partner[0:1], partner[1:2]), partner[2:3])
    bad = bad + lanes_total(partner[0:1] + partner[1:2] + partner[2:3] - least != 2 * NONE)
    both = [pieces(metric[k:k + 1, :]) for k in range(2)]
    rows = [both[k][n] for n in range(3) for k in range(2)]
    rows += [(least >> 4).astype(jnp.float32), (least & 15).astype(jnp.float32)]
    raw_table = element_table([[row[:, 256 * c:256 * c + 256] for c in range(16)] for row in rows])
    ordered = in_order(order, raw_table)

    wide_order = jnp.broadcast_to(order, (ELEMS, 128))
    before = jnp.concatenate([pltpu.roll(wide_order[ELEMS - SEGS:, :], 1, 0), wide_order[:-SEGS, :]], axis=0)
    after = jnp.concatenate([wide_order[SEGS:, :], pltpu.roll(wide_order[:SEGS, :], SEGS - 1, 0)], axis=0)
    lane = iota((1, 128), 1)
    point_i = (lane >> 2) & 3
    point_j = lane & 3
    expect_a = jnp.where(point_j == 0, before, jnp.where(point_j == 3, after, float(ELEMS)))
    expect_b = jnp.where(point_j == 0, 4 * point_i + 3, jnp.where(point_j == 3, 4 * point_i, 0)).astype(jnp.float32)
    expect = jnp.where(lane < 112, expect_a, expect_b)
    bad = bad + lanes_total((lane >= 96) & (ordered != expect))

    loads[3].wait()
    m = iota((1, EDGE), 1)
    p = m - 3 * ((m * 43691) >> 17)
    wide = jnp.broadcast_to(order_row, (8, EDGE))
    up1 = pltpu.roll(wide, EDGE - 1, 1)[0:1]
    down1 = pltpu.roll(wide, 1, 1)[0:1]
    down2 = pltpu.roll(wide, 2, 1)[0:1]
    own = 16 * jnp.where(p == 0, up1, jnp.where(p == 1, order_row, down1)) + p
    other = jnp.where(p == 0, 16 * down2 + 3, NONE)
    recv = recv_v[...]
    for k, shift in ((0, 12), (1, 0)):
        named = send[k:k + 1, :] - shift
        bad = bad + lanes_total((named != own) & ((p != 0) | (named != other)))
        a, b = recv[2 * (1 - k):2 * (1 - k) + 1, :], recv[2 * (1 - k) + 1:2 * (1 - k) + 2, :]
        want = jnp.where(p == 0, other + shift, NONE)
        bad = bad + lanes_total((jnp.minimum(a, b) != jnp.minimum(own + shift, want))
                                | (jnp.maximum(a, b) != jnp.maximum(own + shift, want)))
    ok = jnp.sum(bad) == 0.0
    odd = lax.rem(lax.axis_index("elem"), 2)
    flag_ref[...] = jnp.where(iota((8, 128), 0) == 0, jnp.where(ok, 1, 0), odd)

    weights = jnp.where((point_i == 0) | (point_i == 3), -1.0, -5.0) * jnp.where((point_j == 0) | (point_j == 3), 1.0, 5.0)
    weights = weights * (1.0 / 36.0)

    def set_table(ordered):
        table[...] = weights * (ordered + pltpu.roll(ordered, 96, 1) + pltpu.roll(ordered, 64, 1))

    set_table(ordered)
    order_ref[...] = wide_order

    @pl.when(jnp.logical_not(ok))
    def _():
        order_ref[...] = jnp.broadcast_to(ring.astype(jnp.float32), (ELEMS, 128))
        set_table(in_order(ring.astype(jnp.float32), raw_table))

    loads[4].wait()
    loads[5].wait()

    def body(t, carry):
        elems = []
        for s in range(SEGS):
            y = STEPS * s + t
            elems.append(16 * jnp.where(ok, send_s[0, 3 * y + 1] >> 4, y))
        x = flipped([tile(raw, e) for e in elems]) + flipped([tile(raw, e + 8) for e in elems])
        row = tile(table, t * SEGS)
        mx, my = [], []
        for q in range(16):
            set_plane(u_ref, q, t, x[q])
            mx.append(jnp.broadcast_to(row[:, q:q + 1], (SEGS, COLS)))
            my.append(jnp.broadcast_to(row[:, 16 + q:17 + q], (SEGS, COLS)))
            set_plane(mx_ref, q, t, mx[q])
            set_plane(my_ref, q, t, my[q])
        out = weak(x, lambda q: mx[q], lambda q: my[q])
        for q in range(16):
            set_plane(s_ref, q, t, out[q])
        behind = [out[0] + carry[0], out[1], out[2]]
        ahead = [out[12] + carry[1], out[13], out[14]]
        for j in range(3):
            set_plane(behind_ref, j, t, behind[j])
            set_plane(ahead_ref, j, t, ahead[j])
            set_plane(pair_ref, j, t, jnp.where(odd == 1, behind[j], ahead[j]))
        return (out[3], out[15])

    zero = jnp.zeros((SEGS, COLS), jnp.float32)
    tail = [pltpu.roll(v, 1, 0) for v in lax.fori_loop(0, STEPS, body, (zero, zero), unroll=8)]
    for message, value in ((behind_ref, tail[0]), (ahead_ref, tail[1]), (pair_ref, jnp.where(odd == 1, tail[0], tail[1]))):
        message[0:SEGS, :] = message[0:SEGS, :] + value

    @pl.when(jnp.logical_not(ok))
    def _():
        v_ref[...] = s_ref[...]
        general_sums(v_ref, s_ref, partner_h, partner_s)
        general_messages(s_ref, behind_ref, ahead_ref, send_h, send_s)

        @pl.when(odd == 1)
        def _():
            pair_ref[...] = behind_ref[...]

        @pl.when(odd == 0)
        def _():
            pair_ref[...] = ahead_ref[...]


def edge_values(arrived, im_ref, base, t, scale):
    values = [plane(arrived, j, t) for j in range(3)] + [following(arrived, 0, t)]
    values = [values[j] * plane(im_ref, base + j, t) for j in range(4)]
    return values if scale is None else [scale * v for v in values]


def edge_gradient(left, right):
    h, o = left + right, left - right
    q0, q1 = float(0.5 * (D[0, 0] + D[0, 3])) * h, float(0.5 * (D[1, 0] + D[1, 3])) * h
    s0, s1 = float(0.5 * (D[0, 0] - D[0, 3])) * o, float(0.5 * (D[1, 0] - D[1, 3])) * o
    return [s0 + q0, s1 + q1, s1 - q1, s0 - q0]


def along_edge(c, my_ref, base, t):
    g = gradient(c)
    return divergence([plane(my_ref, base + j, t) * g[j] for j in range(4)])


def prepare_kernel(flag, s_in, mx_ref, my_ref, order, inv_mass, im_ref, kx_ref, w_ref, table):
    mass = inv_mass[...]
    mass = [jnp.concatenate([mass[2 * c:2 * c + 1, :], mass[2 * c + 1:2 * c + 2, :]], axis=1) for c in range(16)]
    split = [pieces(c) for c in mass]
    ordered = in_order(order[:, 0:1], element_table([[c[n] for c in split] for n in range(3)]))
    table[...] = ordered + pltpu.roll(ordered, 112, 1) + pltpu.roll(ordered, 96, 1)
    ok = flag[0, 0] == 1

    def body(t, carry):
        row = tile(table, t * SEGS)
        x = []
        for q in range(16):
            im = jnp.broadcast_to(row[:, q:q + 1], (SEGS, COLS))
            set_plane(im_ref, q, t, im)
            value = plane(s_in, q, t)
            if q % 4 == 0:
                value = value + preceding(s_in, q + 3, t)
            if q % 4 == 3:
                value = value + following(s_in, q - 3, t)
            x.append(im * value)
        mx = [plane(mx_ref, q, t) for q in range(16)]
        for j in range(4):
            for n, (a, b) in enumerate(((0, 0), (0, 3), (3, 3))):
                total = None
                for k in range(4):
                    term = float(D[k, a] * D[k, b]) * mx[4 * k + j]
                    total = term if total is None else total + term
                set_plane(kx_ref, 4 * n + j, t, total)
        out = weak(x, lambda q: mx[q], lambda q: plane(my_ref, q, t))
        for q in range(16):
            set_plane(w_ref, q, t, out[q])
        return carry

    lax.fori_loop(0, STEPS, body, 0, unroll=2)

    @pl.when(jnp.logical_not(ok))
    def _():
        w_ref[...] = s_in[...]


def edge_kernel(updates, odd, flag, seen, w_ref, chain, pair, mx_ref, my_ref, im_ref, kx_ref, u_in, visc, partner_any, send_any, recv_any, *rest):
    pair_ref, g_out, chain_ref, v_ref, g_ref, partner_s, send_s, recv_s = rest[-8:]
    ok = (flag[0, 0] == 1) & (flag[1, 0] == odd)
    left, right = (pair, chain) if odd else (chain, pair)
    behind_ref, ahead_ref = (pair_ref, chain_ref) if odd else (chain_ref, pair_ref)

    @pl.when(ok)
    def _():
        scale = -visc[...] if updates else None

        def body(t, carry):
            cl = edge_values(left, im_ref, 0, t, scale)
            cr = edge_values(right, im_ref, 12, t, scale)
            tail = []
            for base, c, out, k0, k1, before in ((0, cl, behind_ref, 0, 4, carry[0]), (12, cr, ahead_ref, 4, 8, carry[1])):
                f = along_edge(c, my_ref, base, t)
                for j in range(4):
                    f[j] = f[j] + plane(w_ref, base + j, t) + plane(kx_ref, k0 + j, t) * cl[j] + plane(kx_ref, k1 + j, t) * cr[j]
                set_plane(out, 0, t, f[0] + before)
                set_plane(out, 1, t, f[1])
                set_plane(out, 2, t, f[2])
                tail.append(f[3])
            return tuple(tail)

        zero = jnp.zeros((SEGS, COLS), jnp.float32)
        tail = lax.fori_loop(0, STEPS, body, (zero, zero), unroll=8)
        for out, last in zip((behind_ref, ahead_ref), tail):
            out[0:SEGS, :] = out[0:SEGS, :] + pltpu.roll(last, 1, 0)

    @pl.when((flag[0, 0] == 0) & (flag[1, 0] == odd))
    def _():
        v_ref[...] = w_ref[...]
        general_receive(v_ref, left, right, recv_any, recv_s)

        def body(t, carry):
            x = [plane(v_ref, q, t) * plane(im_ref, q, t) for q in range(16)]
            if updates:
                x = [plane(u_in, q, t) - visc[...] * x[q] for q in range(16)]
            out = weak(x, lambda q: plane(mx_ref, q, t), lambda q: plane(my_ref, q, t))
            for q in range(16):
                set_plane(v_ref, q, t, out[q])
            return carry

        lax.fori_loop(0, STEPS, body, 0)
        general_sums(v_ref, g_ref, partner_any, partner_s)
        pltpu.sync_copy(g_ref, g_out)
        general_messages(g_ref, behind_ref, ahead_ref, send_any, send_s)


def leave(order_s, ok, raw, t, x):
    elems = []
    for s in range(SEGS):
        y = STEPS * s + t
        elems.append(16 * jnp.where(ok, order_s[0, 3 * y + 1] >> 4, y))
    for half in range(2):
        rows = flipped(x[8 * half:8 * half + 8])
        for s in range(SEGS):
            raw[pl.ds(pl.multiple_of(elems[s] + 8 * half, 8), 8), :] = rows[s]


def inner_kernel(kind, flag, w_in, g_in, forward, backward, pair_even, pair_odd, mx_ref, my_ref, im_ref, u_in, visc, send_any, recv_any, u_ref, w_ref, s_ref, recv_s, order_s, sem):
    if kind == 2:
        load = pltpu.make_async_copy(send_any, order_s, sem)
        load.start()
    ok = flag[0, 0] == 1
    rate = visc[...]
    if kind == 2:
        load.wait()

    @pl.when(ok)
    def _():
        scale = -rate if kind == 1 else None

        def complete(left, right, t, carry):
            cl = edge_values(left, im_ref, 0, t, scale)
            cr = edge_values(right, im_ref, 12, t, scale)
            lines = [along_edge(cl, my_ref, 0, t), along_edge(cr, my_ref, 12, t)]
            for j in range(4):
                g = edge_gradient(cl[j], cr[j])
                f = divergence([plane(mx_ref, 4 * i + j, t) * g[i] for i in range(4)])
                f[0] = f[0] + lines[0][j]
                f[3] = f[3] + lines[1][j]
                for i in range(4):
                    set_plane(s_ref, 4 * i + j, t, plane(w_in, 4 * i + j, t) + f[i])
            if kind == 1:
                for j in range(4):
                    set_plane(u_ref, j, t, plane(u_in, j, t) + cl[j])
                    set_plane(u_ref, 12 + j, t, plane(u_in, 12 + j, t) + cr[j])
                for q in range(4, 12):
                    set_plane(u_ref, q, t, plane(u_in, q, t))
            return carry

        for odd, left, right in ((0, forward, pair_even), (1, pair_odd, backward)):
            @pl.when(flag[1, 0] == odd)
            def _():
                lax.fori_loop(0, STEPS, functools.partial(complete, left, right), 0, unroll=2)

        ring_sums(s_ref)

        def onward(t, carry):
            x = [plane(s_ref, q, t) * plane(im_ref, q, t) for q in range(16)]
            if kind != 1:
                x = [plane(u_in, q, t) - rate * x[q] for q in range(16)]
            if kind == 0:
                for q in range(16):
                    set_plane(u_ref, q, t, x[q])
            if kind == 2:
                leave(order_s, ok, u_ref, t, x)
            if kind != 2:
                out = weak(x, lambda q: plane(mx_ref, q, t), lambda q: plane(my_ref, q, t))
                for q in range(16):
                    set_plane(w_ref, q, t, out[q])
            return carry

        lax.fori_loop(0, STEPS, onward, 0, unroll=2)

    @pl.when(jnp.logical_not(ok))
    def _():
        pltpu.sync_copy(g_in, w_ref)
        if kind == 1:
            s_ref[...] = w_in[...]
            for odd, left, right in ((0, forward, pair_even), (1, pair_odd, backward)):
                @pl.when(flag[1, 0] == odd)
                def _():
                    general_receive(s_ref, left, right, recv_any, recv_s)

            u_ref[...] = u_in[...] - rate * (s_ref[...] * im_ref[...])
        else:
            u_ref[...] = u_in[...]


def last_kernel(flag, seen, send_any, w_in, forward, backward, pair_even, pair_odd, im_ref, u_in, visc, recv_any, out,
                raw, v_ref, order_s, recv_s, sems):
    load = pltpu.make_async_copy(send_any, order_s, sems.at[0])
    load.start()
    ok = flag[0, 0] == 1
    rate = visc[...]

    @pl.when(ok)
    def _():
        def edges(left, right, t, carry):
            rows = flipped(edge_values(left, im_ref, 0, t, rate) + edge_values(right, im_ref, 12, t, rate))
            for s in range(SEGS):
                v_ref[pl.ds(pl.multiple_of((t * SEGS + s) * 8, 8), 8), :] = rows[s]
            return carry

        for odd, left, right in ((0, forward, pair_even), (1, pair_odd, backward)):
            @pl.when(flag[1, 0] == odd)
            def _():
                lax.fori_loop(0, STEPS, functools.partial(edges, left, right), 0, unroll=4)

    load.wait()

    @pl.when(ok)
    def _():
        low = iota((8, COLS), 0) < 4

        def body(t, carry):
            for s in range(SEGS):
                e = 16 * (order_s[0, 3 * (STEPS * s + t) + 1] >> 4)
                change = tile(v_ref, (t * SEGS + s) * 8)
                for half, mine in ((0, low), (8, jnp.logical_not(low))):
                    raw[pl.ds(pl.multiple_of(e + half, 8), 8), :] = tile(u_in, e + half) - jnp.where(mine, change, 0.0)
            return carry

        lax.fori_loop(0, STEPS, body, 0, unroll=4)

    @pl.when(jnp.logical_not(ok))
    def _():
        v_ref[...] = w_in[...]
        for odd, left, right in ((0, forward, pair_even), (1, pair_odd, backward)):
            @pl.when(flag[1, 0] == odd)
            def _():
                general_receive(v_ref, left, right, recv_any, recv_s)

        v_ref[...] = u_in[...] - rate * (v_ref[...] * im_ref[...])

        def body(t, carry):
            leave(order_s, ok, raw, t, [plane(v_ref, q, t) for q in range(16)])
            return carry

        lax.fori_loop(0, STEPS, body, 0)

    store = pltpu.make_async_copy(raw, out, sems.at[1])
    store.start()
    store.wait()


VM = pl.BlockSpec(memory_space=pltpu.VMEM)
SM = pl.BlockSpec(memory_space=pltpu.SMEM)
HB = pl.BlockSpec(memory_space=pltpu.HBM)
FREE = pl.BlockSpec(memory_space=pl.ANY)
FIELD = jax.ShapeDtypeStruct((ROWS, COLS), jnp.float32)
HELD = pltpu.HBM((ROWS, COLS), jnp.float32)
WORD = jax.ShapeDtypeStruct((8, 128), jnp.int32)
MESSAGE = jax.ShapeDtypeStruct((EDGE, COLS), jnp.float32)
TABLE = jax.ShapeDtypeStruct((ELEMS, COLS), jnp.float32)
SCRATCH = pltpu.VMEM((ROWS, COLS), jnp.float32)
TABLE_V = pltpu.VMEM((ELEMS, COLS), jnp.float32)
PARTNER_S = pltpu.SMEM((3, ROWS), jnp.int32)
SEND_S = pltpu.SMEM((2, EDGE), jnp.int32)
RECV_S = pltpu.SMEM((4, EDGE), jnp.int32)
WORK = 24 * ROWS * COLS
SIZE = 4 * ROWS * COLS


def call(kernel, ins, specs, shapes, outs, scratch, flops, moved, name, aliases={}):
    ins = [pltpu.with_memory_space_constraint(a, pltpu.HBM) if spec is HB else a for a, spec in zip(ins, specs)]
    return pl.pallas_call(
        kernel,
        out_shape=shapes,
        in_specs=specs,
        out_specs=outs,
        scratch_shapes=scratch,
        input_output_aliases=aliases,
        compiler_params=pltpu.CompilerParams(vmem_limit_bytes=VMEM_LIMIT),
        cost_estimate=pl.CostEstimate(flops=1, bytes_accessed=1, transcendentals=0),
        name=name,
    )(*ins)


def moved(value, by):
    size = lax.axis_size("elem")
    return lax.ppermute(value, "elem", [(i, (i + by) % size) for i in range(size)])


def crossed(value):
    size = lax.axis_size("elem")
    return lax.ppermute(value, "elem", [(i, i + 1 - 2 * (i % 2)) for i in range(size)])


def seen_kernel(arrived, before, out):
    out[...] = jnp.zeros_like(out)


def shards(prognostic, metric, inv_mass, viscosity, partner, send_rows, recv_rows):
    visc = viscosity.reshape(1, COLS)
    u, s, mx, my, order, behind, ahead, pair, flag = call(
        first_kernel,
        (prognostic, metric, send_rows, recv_rows, partner),
        [HB] * 5,
        [FIELD, FIELD, FIELD, FIELD, TABLE, MESSAGE, MESSAGE, MESSAGE, WORD],
        [VM] * 9,
        [SCRATCH, SCRATCH, TABLE_V, pltpu.VMEM((2, ROWS), jnp.float32), pltpu.VMEM((2, EDGE), jnp.int32),
         pltpu.VMEM((4, EDGE), jnp.int32), pltpu.VMEM((3, ROWS), jnp.int32), SEND_S, PARTNER_S, pltpu.SemaphoreType.DMA((6,))],
        2 * WORK, 8 * SIZE, "first",
    )
    crossing = crossed(pair)
    forward = moved(ahead, 1)
    backward = moved(behind, -1)
    im, kx, w = call(
        prepare_kernel,
        (flag, s, mx, my, order, inv_mass.reshape(ROWS // 128, 128)),
        [VM] * 6,
        [FIELD, jax.ShapeDtypeStruct((12 * ELEMS, COLS), jnp.float32), FIELD],
        [VM] * 3, [TABLE_V], WORK, 6 * SIZE, "prepare",
    )
    came = [forward, backward]
    pairs = [crossing, crossing]
    for step in range(2 * SUBCYCLES - 1):
        updates = step % 2 == 1
        chained = ()
        before = flag
        arrived, crossings = list(came), list(pairs)
        for odd in ((1, 0) if step % 2 == 0 else (0, 1)):
            seen = call(seen_kernel, (arrived[odd], before), [FREE, FREE], WORD, VM, [], 0, 0, "seen")
            before, g, chain = call(
                functools.partial(edge_kernel, updates, odd),
                (flag, seen, w, arrived[odd], crossings[odd], mx, my, im, kx, u, visc, partner, send_rows, recv_rows) + chained,
                [VM, FREE] + [VM] * 9 + [HB] * 3 + [HB] * len(chained), [MESSAGE, HELD, MESSAGE], [VM, HB, VM],
                [SCRATCH, SCRATCH, PARTNER_S, SEND_S, RECV_S], WORK // 3, 2 * SIZE, "edges",
                {14: 1} if chained else {},
            )
            chained = (g,)
            came[1 - odd] = moved(chain, 1 if odd else -1)
            pairs[1 - odd] = crossed(before)
        kind = 1 if updates else 2 if step == 2 * SUBCYCLES - 2 else 0
        u, w = call(
            functools.partial(inner_kernel, kind),
            (flag, w, g, *arrived, *crossings, mx, my, im, u, visc, send_rows, recv_rows),
            [VM, VM, HB] + [VM] * 9 + [HB] * 2, [FIELD, FIELD], [VM] * 2,
            [SCRATCH, RECV_S, SEND_S, pltpu.SemaphoreType.DMA], WORK * 2, 8 * SIZE, "inner",
        )
    seen = call(seen_kernel, (came[0], flag), [FREE, FREE], WORD, VM, [], 0, 0, "seen")
    return call(
        last_kernel,
        (flag, seen, send_rows, w, *came, *pairs, im, u, visc, recv_rows),
        [VM, FREE, HB] + [VM] * 8 + [HB], FIELD, HB,
        [SCRATCH, SCRATCH, SEND_S, RECV_S, pltpu.SemaphoreType.DMA((2,))], WORK // 8, 4 * SIZE, "last",
    )


def solution(mesh):
    placed = (
        P("elem", None),
        P(None, "elem"),
        P("elem"),
        P(),
        P(None, "elem"),
        P("elem", None),
        P("elem", None),
    )
    return jax.shard_map(
        shards, mesh=mesh, in_specs=placed, out_specs=P("elem", None), check_vma=False
    )
```

```python
import functools
import math

import jax
import jax.numpy as jnp
import numpy as np
from jax import lax
from jax.experimental import pallas as pl
from jax.experimental.pallas import tpu as pltpu
from jax.sharding import PartitionSpec as P

SUBCYCLES = 2
ELEMS = 256
ROWS = 16 * ELEMS
COLS = 128
EDGE = 3 * ELEMS
SEGS = 8
STEPS = ELEMS // SEGS
NONE = ROWS
VMEM_LIMIT = 12 * 2**20


def node_tables():
    root = 1.0 / math.sqrt(5.0)
    points = [-1.0, -root, root, 1.0]
    weights = np.array([1.0, 5.0, 5.0, 1.0]) / 6.0
    products = []
    for first in range(4):
        value = 1.0
        for other in range(4):
            if other != first:
                value = value * (points[first] - points[other])
        products.append(value)
    table = []
    for first in range(4):
        line = []
        for other in range(4):
            if other == first:
                total = 0.0
                for third in range(4):
                    if third != first:
                        total = total + 1.0 / (points[first] - points[third])
                line.append(total)
            else:
                line.append(products[first] / (products[other] * (points[first] - points[other])))
        table.append(line)
    return (np.array(table), weights)


D, WEIGHTS = node_tables()


def gradient(v):
    o0, o1 = v[0] - v[3], v[1] - v[2]
    h = (v[0] + v[3]) - (v[1] + v[2])
    q0 = float(0.5 * (D[0, 0] + D[0, 3])) * h
    q1 = float(0.5 * (D[1, 0] + D[1, 3])) * h
    s0 = float(0.5 * (D[0, 0] - D[0, 3])) * o0 + float(0.5 * (D[0, 1] - D[0, 2])) * o1
    s1 = float(0.5 * (D[1, 0] - D[1, 3])) * o0 + float(0.5 * (D[1, 1] - D[1, 2])) * o1
    return [s0 + q0, s1 + q1, s1 - q1, s0 - q0]


def divergence(f):
    g0, g1 = f[0] - f[3], f[1] - f[2]
    t0, t1 = f[0] + f[3], f[1] + f[2]
    z = float(0.5 * (D[0, 0] + D[0, 3])) * g0 + float(0.5 * (D[1, 0] + D[1, 3])) * g1
    r0 = float(0.5 * (D[0, 0] - D[0, 3])) * t0 + float(0.5 * (D[1, 0] - D[1, 3])) * t1
    r1 = float(0.5 * (D[0, 1] - D[0, 2])) * t0 + float(0.5 * (D[1, 1] - D[1, 2])) * t1
    return [z + r0, r1 - z, -z - r1, z - r0]


def weak(x, mx, my):
    out = [None] * 16
    for j in range(4):
        g = gradient([x[4 * i + j] for i in range(4)])
        f = divergence([mx(4 * i + j) * g[i] for i in range(4)])
        for i in range(4):
            out[4 * i + j] = f[i]
    for i in range(4):
        g = gradient([x[4 * i + j] for j in range(4)])
        f = divergence([my(4 * i + j) * g[j] for j in range(4)])
        for j in range(4):
            out[4 * i + j] = out[4 * i + j] + f[j]
    return out


def plane(ref, q, t):
    return ref[pl.ds(pl.multiple_of(q * ELEMS + t * SEGS, SEGS), SEGS), :]


def set_plane(ref, q, t, value):
    ref[pl.ds(pl.multiple_of(q * ELEMS + t * SEGS, SEGS), SEGS), :] = value


def following(ref, q, t):
    last = t == STEPS - 1
    value = plane(ref, q, jnp.where(last, 0, t + 1))
    return jnp.where(last, pltpu.roll(value, SEGS - 1, 0), value)


def preceding(ref, q, t):
    first = t == 0
    value = plane(ref, q, jnp.where(first, STEPS - 1, t - 1))
    return jnp.where(first, pltpu.roll(value, 1, 0), value)


def place_of(y):
    return lax.rem(y, STEPS) * SEGS + lax.div(y, STEPS)


def state_row(r):
    return lax.rem(r, 16) * ELEMS + place_of(lax.div(r, 16))


def wire_row(m):
    return lax.rem(m, 3) * ELEMS + place_of(lax.div(m, 3))


def one(ref, row):
    return ref[pl.ds(row, 1), :]


def ring_sums(s_ref):
    for i in range(4):
        for t in range(STEPS):
            upper = plane(s_ref, 4 * i, (t + 1) % STEPS)
            if t == STEPS - 1:
                upper = first
                lower = plane(s_ref, 4 * i + 3, t)
                total = lower + pltpu.roll(upper, SEGS - 1, 0)
                set_plane(s_ref, 4 * i + 3, t, total)
                set_plane(s_ref, 4 * i, 0, pltpu.roll(total, 1, 0))
            else:
                if t == 0:
                    first = plane(s_ref, 4 * i, 0)
                total = plane(s_ref, 4 * i + 3, t) + upper
                set_plane(s_ref, 4 * i + 3, t, total)
                set_plane(s_ref, 4 * i, t + 1, total)


def general_sums(v_ref, s_ref, partner_any, partner_s):
    pltpu.sync_copy(partner_any, partner_s)

    def body(r, carry):
        total = one(v_ref, state_row(r))
        for k in range(3):
            other = partner_s[k, r]
            found = one(v_ref, state_row(jnp.minimum(other, ROWS - 1)))
            total = total + jnp.where(other < NONE, found, 0.0)
        s_ref[pl.ds(state_row(r), 1), :] = total
        return carry

    lax.fori_loop(0, ROWS, body, 0)


def general_messages(s_ref, behind_ref, ahead_ref, send_any, send_s):
    pltpu.sync_copy(send_any, send_s)

    def body(m, carry):
        ahead_ref[pl.ds(wire_row(m), 1), :] = one(s_ref, state_row(send_s[0, m]))
        behind_ref[pl.ds(wire_row(m), 1), :] = one(s_ref, state_row(send_s[1, m]))
        return carry

    lax.fori_loop(0, EDGE, body, 0)


def general_receive(total_ref, left_ref, right_ref, recv_any, recv_s):
    pltpu.sync_copy(recv_any, recv_s)

    def body(m, carry):
        for k, arrived in ((0, left_ref), (1, right_ref)):
            for c in range(2):
                target = recv_s[2 * k + c, m]

                @pl.when(target < NONE)
                def _():
                    row = pl.ds(state_row(target), 1)
                    total_ref[row, :] = total_ref[row, :] + one(arrived, wire_row(m))
        return carry

    lax.fori_loop(0, EDGE, body, 0)


def iota(shape, axis):
    return lax.broadcasted_iota(jnp.int32, shape, axis)


def flipped(v):
    sub = iota((SEGS, COLS), 0)
    for b in (1, 2, 4):
        low = (sub & b) == 0
        out = list(v)
        for i in range(8):
            if i & b == 0:
                out[i] = jnp.where(low, v[i], pltpu.roll(v[i + b], b, 0))
                out[i + b] = jnp.where(low, pltpu.roll(v[i], 8 - b, 0), v[i + b])
        v = out
    return v


def tile(ref, row):
    return ref[pl.ds(pl.multiple_of(row, 8), 8), :]


def lanes_total(bad):
    ones = jnp.where(bad, 1.0, 0.0)
    if ones.shape[0] > 1:
        ones = jnp.sum(ones, axis=0, keepdims=True)
    total = ones[:, 0:128]
    for c in range(1, ones.shape[1] // 128):
        total = total + ones[:, 128 * c:128 * c + 128]
    return total


def pieces(row):
    high = row.astype(jnp.bfloat16).astype(jnp.float32)
    rest = row - high
    middle = rest.astype(jnp.bfloat16).astype(jnp.float32)
    return [high, middle, rest - middle]


def element_table(groups):
    own = (iota((16, 256), 1) >> 4) == iota((16, 256), 0)
    lane = iota((256, 128), 1)
    point = iota((256, 128), 0) & 15
    table = None
    for g, chunks in enumerate(groups):
        rows = [jnp.where(own, jnp.broadcast_to(c, (16, 256)), 0.0) for c in chunks]
        spread = jnp.concatenate(rows, axis=0).astype(jnp.bfloat16)
        chosen = (lane == point + 16 * g).astype(jnp.float32).astype(jnp.bfloat16)
        part = jnp.dot(spread, chosen, preferred_element_type=jnp.float32)
        table = part if table is None else table + part
    return table


def in_order(order, table):
    hot = (iota((ELEMS, ELEMS), 1).astype(jnp.float32) == order).astype(jnp.float32).astype(jnp.bfloat16)
    return jnp.dot(hot, table.astype(jnp.bfloat16), preferred_element_type=jnp.float32)


def first_kernel(prog, metric_h, send_h, recv_h, partner_h,
                 u_ref, s_ref, mx_ref, my_ref, order_ref, behind_ref, ahead_ref, pair_ref, flag_ref,
                 raw, v_ref, table, metric, send_v, recv_v, partner_v, send_s, partner_s, sems):
    loads = [pltpu.make_async_copy(a, b, sems.at[k]) for k, (a, b) in enumerate(
        ((send_h, send_v), (metric_h, metric), (partner_h, partner_v), (recv_h, recv_v), (send_h, send_s), (prog, raw)))]
    for load in loads:
        load.start()
    loads[0].wait()

    send = send_v[...]
    order_row = send[0:1, :] >> 4
    place = iota((ELEMS, 1), 0)
    ring = (place & 7) * STEPS + (place >> 3)
    picked = iota((ELEMS, EDGE), 1) == 3 * ring + 1
    order = jnp.sum(jnp.where(picked, order_row.astype(jnp.float32), 0.0), axis=1, keepdims=True)
    hot = (iota((ELEMS, ELEMS), 1).astype(jnp.float32) == order).astype(jnp.float32)
    seen = jnp.sum(hot, axis=0, keepdims=True)
    bad = lanes_total(seen != 1.0)

    loads[1].wait()
    loads[2].wait()
    partner = partner_v[...]
    least = jnp.minimum(jnp.minimum(partner[0:1], partner[1:2]), partner[2:3])
    bad = bad + lanes_total(partner[0:1] + partner[1:2] + partner[2:3] - least != 2 * NONE)
    both = [pieces(metric[k:k + 1, :]) for k in range(2)]
    rows = [both[k][n] for n in range(3) for k in range(2)]
    rows += [(least >> 4).astype(jnp.float32), (least & 15).astype(jnp.float32)]
    raw_table = element_table([[row[:, 256 * c:256 * c + 256] for c in range(16)] for row in rows])
    ordered = in_order(order, raw_table)

    wide_order = jnp.broadcast_to(order, (ELEMS, 128))
    before = jnp.concatenate([pltpu.roll(wide_order[ELEMS - SEGS:, :], 1, 0), wide_order[:-SEGS, :]], axis=0)
    after = jnp.concatenate([wide_order[SEGS:, :], pltpu.roll(wide_order[:SEGS, :], SEGS - 1, 0)], axis=0)
    lane = iota((1, 128), 1)
    point_i = (lane >> 2) & 3
    point_j = lane & 3
    expect_a = jnp.where(point_j == 0, before, jnp.where(point_j == 3, after, float(ELEMS)))
    expect_b = jnp.where(point_j == 0, 4 * point_i + 3, jnp.where(point_j == 3, 4 * point_i, 0)).astype(jnp.float32)
    expect = jnp.where(lane < 112, expect_a, expect_b)
    bad = bad + lanes_total((lane >= 96) & (ordered != expect))

    loads[3].wait()
    m = iota((1, EDGE), 1)
    p = m - 3 * ((m * 43691) >> 17)
    wide = jnp.broadcast_to(order_row, (8, EDGE))
    up1 = pltpu.roll(wide, EDGE - 1, 1)[0:1]
    down1 = pltpu.roll(wide, 1, 1)[0:1]
    down2 = pltpu.roll(wide, 2, 1)[0:1]
    own = 16 * jnp.where(p == 0, up1, jnp.where(p == 1, order_row, down1)) + p
    other = jnp.where(p == 0, 16 * down2 + 3, NONE)
    recv = recv_v[...]
    for k, shift in ((0, 12), (1, 0)):
        named = send[k:k + 1, :] - shift
        bad = bad + lanes_total((named != own) & ((p != 0) | (named != other)))
        a, b = recv[2 * (1 - k):2 * (1 - k) + 1, :], recv[2 * (1 - k) + 1:2 * (1 - k) + 2, :]
        want = jnp.where(p == 0, other + shift, NONE)
        bad = bad + lanes_total((jnp.minimum(a, b) != jnp.minimum(own + shift, want))
                                | (jnp.maximum(a, b) != jnp.maximum(own + shift, want)))
    ok = jnp.sum(bad) == 0.0
    odd = lax.rem(lax.axis_index("elem"), 2)
    flag_ref[...] = jnp.where(iota((8, 128), 0) == 0, jnp.where(ok, 1, 0), odd)

    weights = jnp.where((point_i == 0) | (point_i == 3), -1.0, -5.0) * jnp.where((point_j == 0) | (point_j == 3), 1.0, 5.0)
    weights = weights * (1.0 / 36.0)

    def set_table(ordered):
        table[...] = weights * (ordered + pltpu.roll(ordered, 96, 1) + pltpu.roll(ordered, 64, 1))

    set_table(ordered)
    order_ref[...] = wide_order

    @pl.when(jnp.logical_not(ok))
    def _():
        order_ref[...] = jnp.broadcast_to(ring.astype(jnp.float32), (ELEMS, 128))
        set_table(in_order(ring.astype(jnp.float32), raw_table))

    loads[4].wait()
    loads[5].wait()

    def body(t, carry):
        elems = []
        for s in range(SEGS):
            y = STEPS * s + t
            elems.append(16 * jnp.where(ok, send_s[0, 3 * y + 1] >> 4, y))
        x = flipped([tile(raw, e) for e in elems]) + flipped([tile(raw, e + 8) for e in elems])
        row = tile(table, t * SEGS)
        mx, my = [], []
        for q in range(16):
            set_plane(u_ref, q, t, x[q])
            mx.append(jnp.broadcast_to(row[:, q:q + 1], (SEGS, COLS)))
            my.append(jnp.broadcast_to(row[:, 16 + q:17 + q], (SEGS, COLS)))
            set_plane(mx_ref, q, t, mx[q])
            set_plane(my_ref, q, t, my[q])
        out = weak(x, lambda q: mx[q], lambda q: my[q])
        for q in range(16):
            set_plane(s_ref, q, t, out[q])
        behind = [out[0] + carry[0], out[1], out[2]]
        ahead = [out[12] + carry[1], out[13], out[14]]
        for j in range(3):
            set_plane(behind_ref, j, t, behind[j])
            set_plane(ahead_ref, j, t, ahead[j])
            set_plane(pair_ref, j, t, jnp.where(odd == 1, behind[j], ahead[j]))
        return (out[3], out[15])

    zero = jnp.zeros((SEGS, COLS), jnp.float32)
    tail = [pltpu.roll(v, 1, 0) for v in lax.fori_loop(0, STEPS, body, (zero, zero), unroll=8)]
    for message, value in ((behind_ref, tail[0]), (ahead_ref, tail[1]), (pair_ref, jnp.where(odd == 1, tail[0], tail[1]))):
        message[0:SEGS, :] = message[0:SEGS, :] + value

    @pl.when(jnp.logical_not(ok))
    def _():
        v_ref[...] = s_ref[...]
        general_sums(v_ref, s_ref, partner_h, partner_s)
        general_messages(s_ref, behind_ref, ahead_ref, send_h, send_s)

        @pl.when(odd == 1)
        def _():
            pair_ref[...] = behind_ref[...]

        @pl.when(odd == 0)
        def _():
            pair_ref[...] = ahead_ref[...]


def edge_values(arrived, im_ref, base, t, scale):
    values = [plane(arrived, j, t) for j in range(3)] + [following(arrived, 0, t)]
    values = [values[j] * plane(im_ref, base + j, t) for j in range(4)]
    return values if scale is None else [scale * v for v in values]


def edge_gradient(left, right):
    h, o = left + right, left - right
    q0, q1 = float(0.5 * (D[0, 0] + D[0, 3])) * h, float(0.5 * (D[1, 0] + D[1, 3])) * h
    s0, s1 = float(0.5 * (D[0, 0] - D[0, 3])) * o, float(0.5 * (D[1, 0] - D[1, 3])) * o
    return [s0 + q0, s1 + q1, s1 - q1, s0 - q0]


def along_edge(c, my_ref, base, t):
    g = gradient(c)
    return divergence([plane(my_ref, base + j, t) * g[j] for j in range(4)])


def prepare_kernel(flag, s_in, mx_ref, my_ref, order, inv_mass, im_ref, kx_ref, w_ref, table):
    mass = inv_mass[...]
    mass = [jnp.concatenate([mass[2 * c:2 * c + 1, :], mass[2 * c + 1:2 * c + 2, :]], axis=1) for c in range(16)]
    split = [pieces(c) for c in mass]
    ordered = in_order(order[:, 0:1], element_table([[c[n] for c in split] for n in range(3)]))
    table[...] = ordered + pltpu.roll(ordered, 112, 1) + pltpu.roll(ordered, 96, 1)
    ok = flag[0, 0] == 1

    def body(t, carry):
        row = tile(table, t * SEGS)
        x = []
        for q in range(16):
            im = jnp.broadcast_to(row[:, q:q + 1], (SEGS, COLS))
            set_plane(im_ref, q, t, im)
            value = plane(s_in, q, t)
            if q % 4 == 0:
                value = value + preceding(s_in, q + 3, t)
            if q % 4 == 3:
                value = value + following(s_in, q - 3, t)
            x.append(im * value)
        mx = [plane(mx_ref, q, t) for q in range(16)]
        for j in range(4):
            for n, (a, b) in enumerate(((0, 0), (0, 3), (3, 3))):
                total = None
                for k in range(4):
                    term = float(D[k, a] * D[k, b]) * mx[4 * k + j]
                    total = term if total is None else total + term
                set_plane(kx_ref, 4 * n + j, t, total)
        out = weak(x, lambda q: mx[q], lambda q: plane(my_ref, q, t))
        for q in range(16):
            set_plane(w_ref, q, t, out[q])
        return carry

    lax.fori_loop(0, STEPS, body, 0, unroll=2)

    @pl.when(jnp.logical_not(ok))
    def _():
        w_ref[...] = s_in[...]


def edge_kernel(updates, odd, flag, seen, w_ref, chain, pair, mx_ref, my_ref, im_ref, kx_ref, u_in, visc, partner_any, send_any, recv_any, *rest):
    pair_ref, g_out, chain_ref, v_ref, g_ref, partner_s, send_s, recv_s = rest[-8:]
    ok = (flag[0, 0] == 1) & (flag[1, 0] == odd)
    left, right = (pair, chain) if odd else (chain, pair)
    behind_ref, ahead_ref = (pair_ref, chain_ref) if odd else (chain_ref, pair_ref)

    @pl.when(ok)
    def _():
        scale = -visc[...] if updates else None

        def body(t, carry):
            cl = edge_values(left, im_ref, 0, t, scale)
            cr = edge_values(right, im_ref, 12, t, scale)
            tail = []
            for base, c, out, k0, k1, before in ((0, cl, behind_ref, 0, 4, carry[0]), (12, cr, ahead_ref, 4, 8, carry[1])):
                f = along_edge(c, my_ref, base, t)
                for j in range(4):
                    f[j] = f[j] + plane(w_ref, base + j, t) + plane(kx_ref, k0 + j, t) * cl[j] + plane(kx_ref, k1 + j, t) * cr[j]
                set_plane(out, 0, t, f[0] + before)
                set_plane(out, 1, t, f[1])
                set_plane(out, 2, t, f[2])
                tail.append(f[3])
            return tuple(tail)

        zero = jnp.zeros((SEGS, COLS), jnp.float32)
        tail = lax.fori_loop(0, STEPS, body, (zero, zero), unroll=16)
        for out, last in zip((behind_ref, ahead_ref), tail):
            out[0:SEGS, :] = out[0:SEGS, :] + pltpu.roll(last, 1, 0)

    @pl.when((flag[0, 0] == 0) & (flag[1, 0] == odd))
    def _():
        v_ref[...] = w_ref[...]
        general_receive(v_ref, left, right, recv_any, recv_s)

        def body(t, carry):
            x = [plane(v_ref, q, t) * plane(im_ref, q, t) for q in range(16)]
            if updates:
                x = [plane(u_in, q, t) - visc[...] * x[q] for q in range(16)]
            out = weak(x, lambda q: plane(mx_ref, q, t), lambda q: plane(my_ref, q, t))
            for q in range(16):
                set_plane(v_ref, q, t, out[q])
            return carry

        lax.fori_loop(0, STEPS, body, 0)
        general_sums(v_ref, g_ref, partner_any, partner_s)
        pltpu.sync_copy(g_ref, g_out)
        general_messages(g_ref, behind_ref, ahead_ref, send_any, send_s)


def leave(order_s, ok, raw, t, x):
    elems = []
    for s in range(SEGS):
        y = STEPS * s + t
        elems.append(16 * jnp.where(ok, order_s[0, 3 * y + 1] >> 4, y))
    for half in range(2):
        rows = flipped(x[8 * half:8 * half + 8])
        for s in range(SEGS):
            raw[pl.ds(pl.multiple_of(elems[s] + 8 * half, 8), 8), :] = rows[s]


def inner_kernel(kind, flag, w_in, g_in, forward, backward, pair_even, pair_odd, mx_ref, my_ref, im_ref, u_in, visc, send_any, recv_any, u_ref, w_ref, s_ref, recv_s, order_s, sem):
    if kind == 2:
        load = pltpu.make_async_copy(send_any, order_s, sem)
        load.start()
    ok = flag[0, 0] == 1
    rate = visc[...]
    if kind == 2:
        load.wait()

    @pl.when(ok)
    def _():
        scale = -rate if kind == 1 else None

        def complete(left, right, t, carry):
            cl = edge_values(left, im_ref, 0, t, scale)
            cr = edge_values(right, im_ref, 12, t, scale)
            lines = [along_edge(cl, my_ref, 0, t), along_edge(cr, my_ref, 12, t)]
            for j in range(4):
                g = edge_gradient(cl[j], cr[j])
                f = divergence([plane(mx_ref, 4 * i + j, t) * g[i] for i in range(4)])
                f[0] = f[0] + lines[0][j]
                f[3] = f[3] + lines[1][j]
                for i in range(4):
                    set_plane(s_ref, 4 * i + j, t, plane(w_in, 4 * i + j, t) + f[i])
            if kind == 1:
                for j in range(4):
                    set_plane(u_ref, j, t, plane(u_in, j, t) + cl[j])
                    set_plane(u_ref, 12 + j, t, plane(u_in, 12 + j, t) + cr[j])
                for q in range(4, 12):
                    set_plane(u_ref, q, t, plane(u_in, q, t))
            return carry

        for odd, left, right in ((0, forward, pair_even), (1, pair_odd, backward)):
            @pl.when(flag[1, 0] == odd)
            def _():
                lax.fori_loop(0, STEPS, functools.partial(complete, left, right), 0, unroll=2)

        ring_sums(s_ref)

        def onward(t, carry):
            x = [plane(s_ref, q, t) * plane(im_ref, q, t) for q in range(16)]
            if kind != 1:
                x = [plane(u_in, q, t) - rate * x[q] for q in range(16)]
            if kind == 0:
                for q in range(16):
                    set_plane(u_ref, q, t, x[q])
            if kind == 2:
                leave(order_s, ok, u_ref, t, x)
            if kind != 2:
                out = weak(x, lambda q: plane(mx_ref, q, t), lambda q: plane(my_ref, q, t))
                for q in range(16):
                    set_plane(w_ref, q, t, out[q])
            return carry

        lax.fori_loop(0, STEPS, onward, 0, unroll=2)

    @pl.when(jnp.logical_not(ok))
    def _():
        pltpu.sync_copy(g_in, w_ref)
        if kind == 1:
            s_ref[...] = w_in[...]
            for odd, left, right in ((0, forward, pair_even), (1, pair_odd, backward)):
                @pl.when(flag[1, 0] == odd)
                def _():
                    general_receive(s_ref, left, right, recv_any, recv_s)

            u_ref[...] = u_in[...] - rate * (s_ref[...] * im_ref[...])
        else:
            u_ref[...] = u_in[...]


def last_kernel(flag, seen, send_any, w_in, forward, backward, pair_even, pair_odd, im_ref, u_in, visc, recv_any, out,
                raw, v_ref, order_s, recv_s, sems):
    load = pltpu.make_async_copy(send_any, order_s, sems.at[0])
    load.start()
    ok = flag[0, 0] == 1
    rate = visc[...]

    @pl.when(ok)
    def _():
        def edges(left, right, t, carry):
            rows = flipped(edge_values(left, im_ref, 0, t, rate) + edge_values(right, im_ref, 12, t, rate))
            for s in range(SEGS):
                v_ref[pl.ds(pl.multiple_of((t * SEGS + s) * 8, 8), 8), :] = rows[s]
            return carry

        for odd, left, right in ((0, forward, pair_even), (1, pair_odd, backward)):
            @pl.when(flag[1, 0] == odd)
            def _():
                lax.fori_loop(0, STEPS, functools.partial(edges, left, right), 0, unroll=8)

    load.wait()

    @pl.when(ok)
    def _():
        low = iota((8, COLS), 0) < 4

        def body(t, carry):
            for s in range(SEGS):
                e = 16 * (order_s[0, 3 * (STEPS * s + t) + 1] >> 4)
                change = tile(v_ref, (t * SEGS + s) * 8)
                for half, mine in ((0, low), (8, jnp.logical_not(low))):
                    raw[pl.ds(pl.multiple_of(e + half, 8), 8), :] = tile(u_in, e + half) - jnp.where(mine, change, 0.0)
            return carry

        lax.fori_loop(0, STEPS, body, 0, unroll=8)

    @pl.when(jnp.logical_not(ok))
    def _():
        v_ref[...] = w_in[...]
        for odd, left, right in ((0, forward, pair_even), (1, pair_odd, backward)):
            @pl.when(flag[1, 0] == odd)
            def _():
                general_receive(v_ref, left, right, recv_any, recv_s)

        v_ref[...] = u_in[...] - rate * (v_ref[...] * im_ref[...])

        def body(t, carry):
            leave(order_s, ok, raw, t, [plane(v_ref, q, t) for q in range(16)])
            return carry

        lax.fori_loop(0, STEPS, body, 0)

    store = pltpu.make_async_copy(raw, out, sems.at[1])
    store.start()
    store.wait()


VM = pl.BlockSpec(memory_space=pltpu.VMEM)
SM = pl.BlockSpec(memory_space=pltpu.SMEM)
HB = pl.BlockSpec(memory_space=pltpu.HBM)
FREE = pl.BlockSpec(memory_space=pl.ANY)
FIELD = jax.ShapeDtypeStruct((ROWS, COLS), jnp.float32)
HELD = pltpu.HBM((ROWS, COLS), jnp.float32)
WORD = jax.ShapeDtypeStruct((8, 128), jnp.int32)
MESSAGE = jax.ShapeDtypeStruct((EDGE, COLS), jnp.float32)
TABLE = jax.ShapeDtypeStruct((ELEMS, COLS), jnp.float32)
SCRATCH = pltpu.VMEM((ROWS, COLS), jnp.float32)
TABLE_V = pltpu.VMEM((ELEMS, COLS), jnp.float32)
PARTNER_S = pltpu.SMEM((3, ROWS), jnp.int32)
SEND_S = pltpu.SMEM((2, EDGE), jnp.int32)
RECV_S = pltpu.SMEM((4, EDGE), jnp.int32)
WORK = 24 * ROWS * COLS
SIZE = 4 * ROWS * COLS


def call(kernel, ins, specs, shapes, outs, scratch, flops, moved, name, aliases={}):
    ins = [pltpu.with_memory_space_constraint(a, pltpu.HBM) if spec is HB else a for a, spec in zip(ins, specs)]
    return pl.pallas_call(
        kernel,
        out_shape=shapes,
        in_specs=specs,
        out_specs=outs,
        scratch_shapes=scratch,
        input_output_aliases=aliases,
        compiler_params=pltpu.CompilerParams(vmem_limit_bytes=VMEM_LIMIT),
        cost_estimate=pl.CostEstimate(flops=1, bytes_accessed=1, transcendentals=0),
        name=name,
    )(*ins)


def moved(value, by):
    size = lax.axis_size("elem")
    return lax.ppermute(value, "elem", [(i, (i + by) % size) for i in range(size)])


def crossed(value):
    size = lax.axis_size("elem")
    return lax.ppermute(value, "elem", [(i, i + 1 - 2 * (i % 2)) for i in range(size)])


def seen_kernel(arrived, before, out):
    out[...] = jnp.zeros_like(out)


def shards(prognostic, metric, inv_mass, viscosity, partner, send_rows, recv_rows):
    visc = viscosity.reshape(1, COLS)
    u, s, mx, my, order, behind, ahead, pair, flag = call(
        first_kernel,
        (prognostic, metric, send_rows, recv_rows, partner),
        [HB] * 5,
        [FIELD, FIELD, FIELD, FIELD, TABLE, MESSAGE, MESSAGE, MESSAGE, WORD],
        [VM] * 9,
        [SCRATCH, SCRATCH, TABLE_V, pltpu.VMEM((2, ROWS), jnp.float32), pltpu.VMEM((2, EDGE), jnp.int32),
         pltpu.VMEM((4, EDGE), jnp.int32), pltpu.VMEM((3, ROWS), jnp.int32), SEND_S, PARTNER_S, pltpu.SemaphoreType.DMA((6,))],
        2 * WORK, 8 * SIZE, "first",
    )
    crossing = crossed(pair)
    forward = moved(ahead, 1)
    backward = moved(behind, -1)
    im, kx, w = call(
        prepare_kernel,
        (flag, s, mx, my, order, inv_mass.reshape(ROWS // 128, 128)),
        [VM] * 6,
        [FIELD, jax.ShapeDtypeStruct((12 * ELEMS, COLS), jnp.float32), FIELD],
        [VM] * 3, [TABLE_V], WORK, 6 * SIZE, "prepare",
    )
    came = [forward, backward]
    pairs = [crossing, crossing]
    for step in range(2 * SUBCYCLES - 1):
        updates = step % 2 == 1
        chained = ()
        before = flag
        arrived, crossings = list(came), list(pairs)
        for odd in ((1, 0) if step % 2 == 0 else (0, 1)):
            seen = call(seen_kernel, (arrived[odd], before), [FREE, FREE], WORD, VM, [], 0, 0, "seen")
            before, g, chain = call(
                functools.partial(edge_kernel, updates, odd),
                (flag, seen, w, arrived[odd], crossings[odd], mx, my, im, kx, u, visc, partner, send_rows, recv_rows) + chained,
                [VM, FREE] + [VM] * 9 + [HB] * 3 + [HB] * len(chained), [MESSAGE, HELD, MESSAGE], [VM, HB, VM],
                [SCRATCH, SCRATCH, PARTNER_S, SEND_S, RECV_S], WORK // 3, 2 * SIZE, "edges",
                {14: 1} if chained else {},
            )
            chained = (g,)
            came[1 - odd] = moved(chain, 1 if odd else -1)
            pairs[1 - odd] = crossed(before)
        kind = 1 if updates else 2 if step == 2 * SUBCYCLES - 2 else 0
        u, w = call(
            functools.partial(inner_kernel, kind),
            (flag, w, g, *arrived, *crossings, mx, my, im, u, visc, send_rows, recv_rows),
            [VM, VM, HB] + [VM] * 9 + [HB] * 2, [FIELD, FIELD], [VM] * 2,
            [SCRATCH, RECV_S, SEND_S, pltpu.SemaphoreType.DMA], WORK * 2, 8 * SIZE, "inner",
        )
    seen = call(seen_kernel, (came[0], flag), [FREE, FREE], WORD, VM, [], 0, 0, "seen")
    return call(
        last_kernel,
        (flag, seen, send_rows, w, *came, *pairs, im, u, visc, recv_rows),
        [VM, FREE, HB] + [VM] * 8 + [HB], FIELD, HB,
        [SCRATCH, SCRATCH, SEND_S, RECV_S, pltpu.SemaphoreType.DMA((2,))], WORK // 8, 4 * SIZE, "last",
    )


def solution(mesh):
    placed = (
        P("elem", None),
        P(None, "elem"),
        P("elem"),
        P(),
        P(None, "elem"),
        P("elem", None),
        P("elem", None),
    )
    return jax.shard_map(
        shards, mesh=mesh, in_specs=placed, out_specs=P("elem", None), check_vma=False
    )
```
